32 devices in a mesh: dp: 8 (over z, y), fsdp: 4 (over x, core).
Axes of the slice: x: 2, y: 2, z: 4, core: 2. Of those that a mesh axis runs over, the one named last changes fastest.
Arguments:
- tokens: bfloat16 [4096, 1280], P(('dp', 'fsdp')), may hold values from -3 to 3
- qkv_weight: bfloat16 [3, 1280, 1280], P(None, 'dp', 'fsdp'), may hold values from -1 to 1
- out_weight: bfloat16 [1280, 1280], P('fsdp', 'dp'), may hold values from -0.15625 to 0.15625
- merge_weight: bfloat16 [5120, 1280], P(('dp', 'fsdp')), may hold values from -0.078125 to 0.078125
- ln_gains: float32 [2, 1280], replicated, may hold values from 0.25 to 1.75
- segments: int32 [8, 512], P('dp', 'fsdp'), may hold values from 0 to 2, never falling along the last dimension, each value on 1 to 256 neighbouring positions
- merge_rows: int32 [32, 128], P(('dp', 'fsdp')), may hold values from 0 to 127, each once within a row
- owners: int32 [1024, 1], P(('dp', 'fsdp')), may hold values from 0 to 7; in each aligned block of 32 rows (0 to 31, 32 to 63, ...) at most 8 rows name the same one
Outputs:
- owned: bfloat16 [2048, 1280], P(('dp', 'fsdp'))
The draws below stay inside these ranges and needn't reach their ends.
Inputs may be any that keep to these rules, and one draw needn't show every extreme that they name: `segments`: within each row segment numbers never fall, every number appears, each request has 1 to 256 tokens and one has exactly 256. `merge_rows`: each row is a permutation of the device's local rows. `owners`: among the 32 merged tokens of one device no owner appears more than 8 times, and in some devices one appears exactly 8 times.
All inputs are finite; a program needn't handle non-finite values.
Results may differ from the reference program's by a relative error of at most 0.02.
Values may be sent and summed in bfloat16 or wider, within the bound.
No kernel may reach another device: no remote copies, remote signals or barrier semaphores. Data moves between devices by JAX's collectives and lax.ppermute only.
A program may use at most 64 MiB of HBM per device.

```python
import math
import jax
import jax.numpy as jnp
import numpy as np
from jax import lax

D = 1280
HD = 80
MD = 1280
TOK_DEV = 128
SEGS = 3
QW = 1280
TOKENS = 4096
GROUP = 512
MERGED = 1024
CAP = 8
N_DP = 8
N_FSDP = 4


def draw_qkv_weight(key, part):
    base = jnp.clip(jax.random.normal(key, (3, D, QW), jnp.float32), -6.0, 6.0)
    chosen = jax.random.randint(jax.random.fold_in(key, 77), (2,), 0, N_DP)
    row_block = jnp.arange(D) // (D // N_DP)
    heavy = (row_block == chosen[0]) | (row_block == chosen[1])
    base = base * jnp.where(heavy, 4.0, 1.0)[None, :, None]
    return jnp.clip(base / math.sqrt(D), -1.0, 1.0).astype(jnp.bfloat16)


def block_levels(key, shape, cuts, least, largest):
    def one(dim, shards_of):
        heights = jax.random.uniform(jax.random.fold_in(jax.random.fold_in(key, 6), dim), (shards_of,), jnp.float32, least / len(cuts), largest / len(cuts))
        return jnp.repeat(jnp.exp(heights), shape[dim] // shards_of).reshape((-1,) + (1,) * (len(shape) - dim - 1))

    gain = one(*cuts[0])
    for cut in cuts[1:]:
        gain = gain * one(*cut)
    return gain


def profile(count, total, reach, skew):
    loads = [(1 << 20) // math.isqrt(rank ** skew) + 1 for rank in range(2, count + 1)]
    rest, given = total - reach - (count - 1), [1] * (count - 1)
    while rest > 0:
        free = [i for i in range(count - 1) if given[i] < reach]
        whole, left = sum([loads[i] for i in free]), rest
        for i in free:
            addition = min(reach - given[i], max(1, left * loads[i] // whole), rest)
            given[i] = given[i] + addition
            rest = rest - addition
    return np.array([reach] + given)


def uneven_parts(stream_key, amount, total, limit, skew):
    if amount == 2:
        one = jax.random.randint(stream_key, (), max(1, total - limit), min(limit, total - 1) + 1)
        return jnp.stack([one, total - one])
    tallies = jnp.asarray(profile(amount, total, limit, skew), jnp.int32)
    twos = (amount - 1) // 2
    donor, sink = tallies[1:1 + 2 * twos:2], tallies[2:2 + 2 * twos:2]
    slack = jnp.minimum(donor - 1, limit - sink)
    shifted = jax.random.randint(jax.random.fold_in(stream_key, 1), (twos,), 0, 1 << 20) % (slack + 1)
    tallies = tallies.at[1:1 + 2 * twos:2].set(donor - shifted).at[2:2 + 2 * twos:2].set(sink + shifted)
    return tallies[jax.random.permutation(jax.random.fold_in(stream_key, 2), amount)]


def routed_block(stream_key, own, number, rows, amount, top, most, skew):
    ranking = jax.random.permutation(stream_key, amount)
    crowded, common = portions_of(amount, rows * top, most, skew, True), portions_of(amount, rows * top, most, skew, False)
    places = jnp.arange(amount)

    def named(sizes, turn):
        used = int((sizes > 0).sum())
        fixed = max(1, used // 4)
        moved = fixed + (places - fixed + turn * (used - fixed)) % max(1, amount - fixed)
        return jnp.zeros((amount,), jnp.int32).at[ranking[jnp.where(places < fixed, places, moved)]].set(jnp.asarray(sizes, jnp.int32))

    sizes = jnp.where(number % 4 == 0, named(crowded, number // 4), named(common, number - number // 4 - 1))
    mixed = jax.random.permutation(jax.random.fold_in(own, 3), amount)
    giver, taker = mixed[0:amount // 2 * 2:2], mixed[1:amount // 2 * 2:2]
    room = jnp.minimum(sizes[giver] - 1, most - sizes[taker]) // 2
    room = jnp.where((giver == ranking[0]) | (taker == ranking[0]) | (sizes[taker] == 0), 0, jnp.maximum(room, 0))
    moved = jax.random.randint(jax.random.fold_in(own, 4), (amount // 2,), 0, 1 << 20) % (room + 1)
    sizes = sizes.at[giver].add(-moved).at[taker].add(moved)
    items = jnp.searchsorted(jnp.cumsum(sizes), jnp.arange(rows * top), side="right").astype(jnp.int32)
    table = items.reshape(top, rows).T
    table = table[jax.random.permutation(jax.random.fold_in(own, 1), rows)]
    turn = jax.random.randint(jax.random.fold_in(own, 2), (rows, 1), 0, top)
    return jnp.take_along_axis(table, (jnp.arange(top)[None, :] + turn) % top, axis=1)


def portions_of(number_of, total, bound, skew, full):
    loads = [(1 << 20) // math.isqrt(grade ** skew) + 1 for grade in range(1, number_of + 1)]
    largest = bound if full else min(bound, max(-(-total // number_of), total * loads[0] // sum(loads)))
    least = 1 if total - largest >= number_of - 1 else 0
    counts, spare = [largest] + [least] * (number_of - 1), total - largest - least * (number_of - 1)
    while spare > 0:
        movable = [i for i in range(1, number_of) if counts[i] < largest] or [i for i in range(1, number_of) if counts[i] < bound]
        pool, left = sum([loads[i] for i in movable]), spare
        for i in movable:
            addition = min(bound - counts[i], max(1, left * loads[i] // pool), spare)
            counts[i] = counts[i] + addition
            spare = spare - addition
    return np.array(counts)


def noise(own_key, dims, scale, most, cuts=(), kind=jnp.bfloat16):
    values = scale * jax.random.normal(own_key, dims, jnp.float32)
    if cuts:
        values = values * block_levels(own_key, dims, cuts, -0.22, 0.18)
    return jnp.clip(values, -most, most).astype(kind)


def setup_inputs(seed: int = 0) -> dict:
    arg_keys = jax.random.split(jax.random.key(seed), 9)
    tokens = noise(arg_keys[0], (TOKENS, D), 0.5, 3.0, ((0, 32),))
    qkv_weight = draw_qkv_weight(jax.random.fold_in(arg_keys[8], 71), 0)
    out_weight = noise(arg_keys[2], (QW, D), QW ** -0.5, 0.15625, ((0, 4), (1, 8)))
    merge_weight = noise(arg_keys[3], (4 * D, MD), (4 * D) ** -0.5, 0.078125, ((0, 32),))
    ln_gains = jnp.clip(1.0 + 0.15 * jax.random.normal(arg_keys[4], (2, D), jnp.float32), 0.25, 1.75)
    segments = jax.vmap(lambda own: jnp.searchsorted(jnp.cumsum(uneven_parts(own, SEGS, GROUP, 2 * TOK_DEV, 1)), jnp.arange(GROUP), side="right"))(jax.random.split(arg_keys[5], N_DP)).reshape((N_DP, GROUP)).astype(jnp.int32)
    merge_rows = jax.vmap(lambda own: jax.random.permutation(own, TOK_DEV))(jax.random.split(arg_keys[6], (N_DP * N_FSDP))).reshape((N_DP * N_FSDP, TOK_DEV)).astype(jnp.int32)
    owners_keys = jax.random.split(jax.random.fold_in(arg_keys[7], 1), MERGED // (TOK_DEV // 4))
    owners_turns = jax.random.permutation(jax.random.fold_in(arg_keys[7], 3), MERGED // (TOK_DEV // 4))
    owners = jax.vmap(lambda own, number: routed_block(jax.random.fold_in(arg_keys[7], 2), own, number, TOK_DEV // 4, N_DP, 1, CAP, 2))(owners_keys, owners_turns).reshape((MERGED, 1))
    return {"tokens": tokens, "qkv_weight": qkv_weight, "out_weight": out_weight, "merge_weight": merge_weight, "ln_gains": ln_gains, "segments": segments, "merge_rows": merge_rows, "owners": owners}


epsilon = 1e-06

def normalize(values_in, gain_row):
    widened = values_in.astype(jnp.float32)
    centered = widened - lax.optimization_barrier(jnp.mean(widened, axis=1, keepdims=True))
    variance = lax.optimization_barrier(jnp.mean(centered * centered, axis=1, keepdims=True))
    return (centered / jnp.sqrt(variance + epsilon) * gain_row).astype(jnp.bfloat16)

def attend(queries, keys_all, values_all, seg_rows, seg_cols):
    factor = 1.0 / math.sqrt(HD)
    allowed = seg_rows[:, None] == seg_cols[None, :]
    pieces = []
    for head_index in range(queries.shape[1] // HD):
        first_col = head_index * HD
        last_col = first_col + HD
        scores = jnp.dot(queries[:, first_col:last_col], keys_all[:, first_col:last_col].T, preferred_element_type=jnp.float32) * factor
        masked = jnp.where(allowed, scores, -jnp.inf)
        highest = lax.optimization_barrier(jnp.max(masked, axis=1, keepdims=True))
        weights = jnp.exp(masked - highest)
        totals = lax.optimization_barrier(jnp.sum(weights, axis=1, keepdims=True))
        head_out = jnp.dot(weights.astype(jnp.bfloat16), values_all[:, first_col:last_col], preferred_element_type=jnp.float32)
        pieces.append(head_out / totals)
    return jnp.concatenate(pieces, axis=1).astype(jnp.bfloat16)

def pack_lists(rows_block, targets):
    onehot = (targets[:, None] == jnp.arange(N_DP, dtype=jnp.int32)[None, :]).astype(jnp.int32)
    earlier = (jnp.cumsum(onehot, axis=0) - onehot).astype(jnp.int32)
    position = lax.optimization_barrier(jnp.sum(earlier * onehot, axis=1)).astype(jnp.int32)
    slot_index = targets * CAP + position
    placing = (jnp.arange(N_DP * CAP, dtype=jnp.int32)[:, None] == slot_index[None, :]).astype(jnp.bfloat16)
    return jnp.dot(placing, rows_block, preferred_element_type=jnp.float32).astype(jnp.bfloat16)

def reference(tokens, qkv_weight, out_weight, merge_weight, ln_gains, segments, merge_rows, owners):

    def one_group(operands):
        group_tokens, group_segs = operands
        normed = normalize(group_tokens, ln_gains[0])
        queries = jnp.dot(normed, qkv_weight[0], preferred_element_type=jnp.float32).astype(jnp.bfloat16)
        keys_all = jnp.dot(normed, qkv_weight[1], preferred_element_type=jnp.float32).astype(jnp.bfloat16)
        values_all = jnp.dot(normed, qkv_weight[2], preferred_element_type=jnp.float32).astype(jnp.bfloat16)
        attended = attend(queries, keys_all, values_all, group_segs, group_segs)
        update = jnp.dot(attended, out_weight, preferred_element_type=jnp.float32)
        layer_out = (group_tokens.astype(jnp.float32) + update).astype(jnp.bfloat16)
        return normalize(layer_out, ln_gains[1])
    merge_in = lax.map(one_group, (tokens.reshape(N_DP, N_FSDP * TOK_DEV, D), segments))
    merge_in = merge_in.reshape(N_DP * N_FSDP, TOK_DEV, D)
    stacked = jax.vmap(lambda rows_block, row_order: jnp.take(rows_block, row_order, axis=0))(merge_in, merge_rows)
    stacked = stacked.reshape(MERGED, 4 * D)
    merged = jnp.dot(stacked, merge_weight, preferred_element_type=jnp.float32).astype(jnp.bfloat16)
    packed = jax.vmap(pack_lists)(merged.reshape(N_DP * N_FSDP, TOK_DEV // 4, MD), owners.reshape(N_DP * N_FSDP, TOK_DEV // 4))
    packed = packed.reshape(N_DP, N_FSDP, N_DP, CAP, MD).transpose(2, 1, 0, 3, 4)
    return packed.reshape(N_DP * N_FSDP * N_DP * CAP, MD)
```

```python
import math

import jax
import jax.numpy as jnp
from jax import lax
from jax.sharding import PartitionSpec as P

HD = 80


epsilon = 1e-06


def normalize(values_in, gain_row):
    widened = values_in.astype(jnp.float32)
    centered = widened - jnp.mean(widened, axis=1, keepdims=True)
    variance = jnp.mean(centered * centered, axis=1, keepdims=True)
    return (centered * lax.rsqrt(variance + epsilon) * gain_row).astype(jnp.bfloat16)


def attend(queries, keys_all, values_all, seg_rows, seg_cols):
    factor = 1.0 / math.sqrt(HD)
    allowed = seg_rows[:, None] == seg_cols[None, :]
    pieces = []
    for head_index in range(queries.shape[1] // HD):
        first_col = head_index * HD
        last_col = first_col + HD
        scores = (
            lax.dot_general(
                queries[:, first_col:last_col],
                keys_all[:, first_col:last_col],
                (((1,), (1,)), ((), ())),
                preferred_element_type=jnp.float32,
            )
            * factor
        )
        masked = jnp.where(allowed, scores, -jnp.inf)
        highest = jnp.max(masked, axis=1, keepdims=True)
        weights = jnp.exp(masked - highest)
        totals = jnp.sum(weights, axis=1, keepdims=True)
        head_out = jnp.dot(
            weights.astype(jnp.bfloat16),
            values_all[:, first_col:last_col],
            preferred_element_type=jnp.float32,
        )
        pieces.append(head_out / totals)
    return jnp.concatenate(pieces, axis=1).astype(jnp.bfloat16)


def xor_pairs(n, k):
    return [(i, i ^ k) for i in range(n)]


def swap(value, axis, k):
    return lax.ppermute(value, axis, xor_pairs(lax.axis_size(axis), k))


def turn(value, k):
    n = lax.axis_size("dp")
    return lax.ppermute(value, "dp", [(i, (i + 2 * k) % n) for i in range(n)])


def after(value, other):
    return lax.optimization_barrier((value, other))[0]


def place(parts, dim, size):
    shape = list(parts[0][1].shape)
    step = shape[dim]
    shape[dim] = size * step
    whole = jnp.zeros(shape, parts[0][1].dtype)
    for index, block in parts:
        start = [0] * len(shape)
        start[dim] = index * step
        whole = lax.dynamic_update_slice(whole, block, start)
    return whole


def z_then_y(block, me):
    found = [(0, block)] + [(k, turn(block, k)) for k in (1, 3, 2)]
    mine, theirs = [], []
    for k, held in found:
        index = lax.rem(me + 8 - 2 * k, 8)
        mine.append((index, held))
        theirs.append((index ^ 1, swap(held, "dp", 1)))
    return mine, theirs


def y_then_z(block, me):
    other = swap(block, "dp", 1)
    low = jnp.where(me % 2 == 0, block, other)
    high = jnp.where(me % 2 == 0, other, block)
    pair = jnp.concatenate([low, high], axis=0)
    parts = [(me // 2, pair)]
    for k in (1, 3, 2):
        parts.append((lax.rem(me // 2 + 4 - k, 4), turn(pair, k)))
    return parts


def per_device(
    tokens, qkv_weight, out_weight, merge_weight, ln_gains, segments, merge_rows, owners
):
    n_dp = lax.axis_size("dp")
    n_fsdp = lax.axis_size("fsdp")
    me = lax.axis_index("dp")
    place_in_group = lax.axis_index("fsdp")
    normed = normalize(tokens, ln_gains[0])
    out_turned = out_weight.T
    if n_dp == 8:
        qkv_mine, qkv_theirs = z_then_y(qkv_weight, me)
        qkv_full = place(qkv_mine + qkv_theirs, 1, 8)
        out_parts = y_then_z(after(out_turned, qkv_mine[1][1]), me)
        out_rows = place(out_parts, 0, 4)
        merge_mine, merge_theirs = z_then_y(after(merge_weight, qkv_mine[2][1]), me)
        part_rows = place(merge_mine + merge_theirs, 0, 8)
    else:
        qkv_full = lax.all_gather(qkv_weight, "dp", axis=1, tiled=True)
        out_rows = lax.all_gather(out_turned, "dp", axis=0, tiled=True)
        part_rows = lax.all_gather(merge_weight, "dp", axis=0, tiled=True)

    others = range(1, n_fsdp)
    group_normed = place(
        [(place_in_group, normed)]
        + [(place_in_group ^ k, swap(normed, "fsdp", k)) for k in others],
        0,
        n_fsdp,
    )
    group_segs = place(
        [(place_in_group, segments)]
        + [(place_in_group ^ k, swap(segments, "fsdp", k)) for k in others],
        1,
        n_fsdp,
    )
    queries, keys_all, values_all = (
        jnp.dot(group_normed, qkv_full[n], preferred_element_type=jnp.float32).astype(jnp.bfloat16)
        for n in range(3)
    )
    attended_mine = attend(queries, keys_all, values_all, group_segs[0], group_segs[0])
    by_device = attended_mine.reshape(n_fsdp, tokens.shape[0], -1)

    update = tokens.astype(jnp.float32)
    for k in range(n_fsdp):
        heads = lax.dynamic_index_in_dim(by_device, place_in_group ^ k, 0, keepdims=False)
        rows = out_rows
        if k:
            heads, rows = swap(heads, "fsdp", k), swap(out_rows, "fsdp", k)
        update = update + lax.dot_general(
            heads, rows, (((1,), (1,)), ((), ())), preferred_element_type=jnp.float32
        )
    merge_in = normalize(update.astype(jnp.bfloat16), ln_gains[1])

    merge_count = tokens.shape[0] // 4
    slice_rows = merge_weight.shape[0]
    stacked = jnp.take(merge_in, merge_rows[0], axis=0).reshape(
        merge_count, n_dp, n_fsdp, slice_rows
    )
    by_slice = stacked.transpose(2, 0, 1, 3).reshape(n_fsdp, merge_count, n_dp * slice_rows)
    received = place(
        [
            (
                place_in_group ^ k,
                (lambda v, k=k: swap(v, "fsdp", k) if k else v)(
                    lax.dynamic_index_in_dim(by_slice, place_in_group ^ k, 0, keepdims=False)
                ),
            )
            for k in range(n_fsdp)
        ],
        0,
        n_fsdp,
    )
    partial = jnp.dot(received, part_rows, preferred_element_type=jnp.float32).astype(jnp.bfloat16)
    partial = partial.reshape(n_fsdp, merge_count, -1)
    total = 0.0
    for k in range(n_fsdp):
        share = lax.dynamic_index_in_dim(partial, place_in_group ^ k, 0, keepdims=False)
        if k:
            share = swap(share, "fsdp", k)
        total = total + share.astype(jnp.float32)
    merged = total.astype(jnp.bfloat16)

    capacity = max(2, (2 * merge_count + n_dp - 1) // n_dp)
    targets = owners[:, 0]
    onehot = (targets[:, None] == jnp.arange(n_dp, dtype=jnp.int32)[None, :]).astype(jnp.int32)
    earlier = jnp.cumsum(onehot, axis=0) - onehot
    position = jnp.sum(earlier * onehot, axis=1)
    slot_index = targets * capacity + position
    placing = (jnp.arange(n_dp * capacity, dtype=jnp.int32)[:, None] == slot_index[None, :]).astype(
        jnp.bfloat16
    )
    packed = jnp.dot(placing, merged, preferred_element_type=jnp.float32).astype(jnp.bfloat16)
    packed = packed.reshape(n_dp, capacity, merged.shape[1])
    arrived = lax.all_to_all(packed, "dp", split_axis=0, concat_axis=0, tiled=True)
    return arrived.reshape(n_dp * capacity, merged.shape[1])


def solution(mesh):
    return jax.shard_map(
        per_device,
        mesh=mesh,
        in_specs=(
            P(("dp", "fsdp"), None),
            P(None, "dp", "fsdp"),
            P("fsdp", "dp"),
            P(("dp", "fsdp"), None),
            P(),
            P("dp", "fsdp"),
            P(("dp", "fsdp"), None),
            P(("dp", "fsdp"), None),
        ),
        out_specs=P(("dp", "fsdp"), None),
        check_vma=False,
    )
```

```python
import functools
import math

import jax
import jax.numpy as jnp
from jax import lax
from jax.experimental import pallas as pl
from jax.experimental.pallas import tpu as pltpu
from jax.sharding import PartitionSpec as P

HD = 80


epsilon = 1e-06


def normalize(values_in, gain_row):
    widened = values_in.astype(jnp.float32)
    centered = widened - jnp.mean(widened, axis=1, keepdims=True)
    variance = jnp.mean(centered * centered, axis=1, keepdims=True)
    return (centered * lax.rsqrt(variance + epsilon) * gain_row).astype(jnp.bfloat16)


def attend(queries, keys_all, values_all, seg_rows, seg_cols):
    factor = 1.0 / math.sqrt(HD)
    allowed = seg_rows[:, None] == seg_cols[None, :]
    pieces = []
    for head_index in range(queries.shape[1] // HD):
        first_col = head_index * HD
        last_col = first_col + HD
        scores = (
            lax.dot_general(
                queries[:, first_col:last_col],
                keys_all[:, first_col:last_col],
                (((1,), (1,)), ((), ())),
                preferred_element_type=jnp.float32,
            )
            * factor
        )
        masked = jnp.where(allowed, scores, -jnp.inf)
        highest = jnp.max(masked, axis=1, keepdims=True)
        weights = jnp.exp(masked - highest)
        totals = jnp.sum(weights, axis=1, keepdims=True)
        head_out = jnp.dot(
            weights.astype(jnp.bfloat16),
            values_all[:, first_col:last_col],
            preferred_element_type=jnp.float32,
        )
        pieces.append(head_out / totals)
    return jnp.concatenate(pieces, axis=1).astype(jnp.bfloat16)


def slot_numbers(targets, capacity):
    n = targets.shape[0]
    same = targets[:, None] == targets[None, :]
    before = jnp.arange(n)[None, :] < jnp.arange(n)[:, None]
    return targets * capacity, jnp.sum((same & before).astype(jnp.int32), axis=1)


def by_gathers(
    tokens, qkv_weight, out_weight, merge_weight, ln_gains, segments, merge_rows, owners
):
    n_dp = lax.axis_size("dp")
    qkv_mine = lax.all_gather(qkv_weight, "dp", axis=1, tiled=True)
    out_mine = lax.all_gather(out_weight, "dp", axis=1, tiled=True)
    n_fsdp = lax.axis_size("fsdp")
    normed = normalize(tokens, ln_gains[0])
    group_normed = lax.all_gather(normed, "fsdp", axis=0, tiled=True)
    group_segs = lax.all_gather(segments, "fsdp", axis=1, tiled=True)
    queries, keys_all, values_all = (
        jnp.dot(group_normed, qkv_mine[n], preferred_element_type=jnp.float32).astype(jnp.bfloat16)
        for n in range(3)
    )
    attended_mine = attend(queries, keys_all, values_all, group_segs[0], group_segs[0])
    attended_local = lax.all_to_all(attended_mine, "fsdp", split_axis=0, concat_axis=1, tiled=True)
    out_full = lax.all_gather(out_mine, "fsdp", axis=0, tiled=True)
    update = jnp.dot(attended_local, out_full, preferred_element_type=jnp.float32)
    layer_out = (tokens.astype(jnp.float32) + update).astype(jnp.bfloat16)
    merge_in = normalize(layer_out, ln_gains[1])
    merge_count = tokens.shape[0] // 4
    stacked = jnp.take(merge_in, merge_rows[0], axis=0).reshape(merge_count, 4 * merge_in.shape[1])
    slice_rows = merge_weight.shape[0]
    part_rows = lax.all_gather(merge_weight, "dp", axis=0, tiled=True)
    blocks = stacked.reshape(merge_count, n_dp, n_fsdp * slice_rows)
    received = lax.all_to_all(blocks, "fsdp", split_axis=2, concat_axis=0, tiled=True)
    gathered_inputs = received.reshape(n_fsdp * merge_count, n_dp * slice_rows)
    merged = lax.psum_scatter(
        jnp.dot(gathered_inputs, part_rows, preferred_element_type=jnp.float32).astype(
            jnp.bfloat16
        ),
        "fsdp",
        scatter_dimension=0,
        tiled=True,
    )
    capacity = max(2, (2 * merge_count + n_dp - 1) // n_dp)
    first, rank = slot_numbers(owners[:, 0], capacity)
    placing = (
        jnp.arange(n_dp * capacity, dtype=jnp.int32)[:, None] == (first + rank)[None, :]
    ).astype(jnp.bfloat16)
    packed = jnp.dot(placing, merged, preferred_element_type=jnp.float32).astype(jnp.bfloat16)
    packed = packed.reshape(n_dp, capacity, merged.shape[1])
    arrived = lax.all_to_all(packed, "dp", split_axis=0, concat_axis=0, tiled=True)
    return arrived.reshape(n_dp * capacity, merged.shape[1])


def swap(value, axis, k):
    return lax.ppermute(value, axis, [(i, i ^ k) for i in range(lax.axis_size(axis))])


def turn(value, k):
    n = lax.axis_size("dp")
    return lax.ppermute(value, "dp", [(i, (i + 2 * k) % n) for i in range(n)])


def across(value, k):
    n_dp, n_fsdp = lax.axis_size("dp"), lax.axis_size("fsdp")
    pairs = [
        (i * n_fsdp + j, (i ^ 1) * n_fsdp + (j ^ k)) for i in range(n_dp) for j in range(n_fsdp)
    ]
    return lax.ppermute(value, ("dp", "fsdp"), pairs)


def after(value, other):
    return lax.optimization_barrier((value, other))[0]


ROUNDS = (1, 3, 2)
ORDER = (0, 1, 3, 2)


def dot(a, b):
    return jnp.dot(a, b, preferred_element_type=jnp.float32)


def dot_turned(a, b):
    return lax.dot_general(a, b, (((1,), (1,)), ((), ())), preferred_element_type=jnp.float32)


def call(kernel, outs, operands, scratch=(), flops=0, smem=0, exps=0):
    moved = sum(math.prod(x.shape) * x.dtype.itemsize for x in (*operands, *outs))
    specs = [pl.BlockSpec(memory_space=pltpu.SMEM)] * smem
    specs += [pl.BlockSpec(memory_space=pltpu.VMEM)] * (len(operands) - smem)
    return pl.pallas_call(
        kernel,
        out_shape=tuple(outs),
        in_specs=specs,
        out_specs=tuple(pl.BlockSpec(memory_space=pltpu.VMEM) for _ in outs),
        scratch_shapes=list(scratch),
        compiler_params=pltpu.CompilerParams(vmem_limit_bytes=40 * 1024 * 1024),
        cost_estimate=pl.CostEstimate(
            flops=flops, bytes_accessed=moved, transcendentals=exps
        ),
    )(*operands)


def norm_kernel(tokens_ref, gains_ref, segs_ref, out_ref):
    rows = tokens_ref.shape[0]
    out_ref[0:rows, :] = normalize(tokens_ref[...], gains_ref[0:1, :])
    out_ref[rows:, :] = jnp.zeros((out_ref.shape[0] - rows, out_ref.shape[1]), out_ref.dtype)
    out_ref[rows:, 0:rows] = jnp.broadcast_to(
        segs_ref[...].astype(jnp.float32), (out_ref.shape[0] - rows, rows)
    ).astype(out_ref.dtype)


def block_index(me, number, n_dp):
    mine = lax.rem(me + n_dp - 2 * ORDER[number % 4], n_dp)
    return mine if number < 4 else mine ^ 1


def lay_out(me, blocks, part, whole):
    step = blocks[0].shape[1]
    for number, block in enumerate(blocks):
        start = pl.multiple_of(block_index(me, number, len(blocks)) * step, 32)
        whole[pl.ds(start, step), :] = block[part]


def score_kernel(me_ref, *refs):
    tokens, blocks = refs[0:4], refs[4:12]
    rows_ref, weights_ref, totals_ref, q_whole, k_whole = refs[12:]
    rows = tokens[0].shape[0] - 16
    for n in range(4):
        rows_ref[n * rows : (n + 1) * rows, :] = tokens[n][0:rows, :]
    lay_out(me_ref[0], blocks, 0, q_whole)
    lay_out(me_ref[0], blocks, 1, k_whole)
    queries = dot(rows_ref[...], q_whole[...]).astype(jnp.bfloat16)
    keys = dot(rows_ref[...], k_whole[...]).astype(jnp.bfloat16)
    in_row = [t[rows : rows + 16, 0:rows].astype(jnp.float32)[0:1, :] for t in tokens]
    in_col = [jnp.broadcast_to(s, (rows, rows)).T[:, 0:1] for s in in_row]
    allowed = jnp.concatenate(in_col, axis=0) == jnp.concatenate(in_row, axis=1)
    factor = 1.0 / math.sqrt(HD)
    for head in range(queries.shape[1] // HD):
        cols = slice(head * HD, (head + 1) * HD)
        scores = dot_turned(queries[:, cols], keys[:, cols]) * factor
        masked = jnp.where(allowed, scores, -jnp.inf)
        weights = jnp.exp(masked - jnp.max(masked, axis=1, keepdims=True))
        weights_ref[head] = weights.astype(jnp.bfloat16)
        totals_ref[head] = jnp.sum(weights, axis=1, keepdims=True)


def value_kernel(me_ref, *refs):
    rows_ref, weights_ref, totals_ref = refs[0:3]
    blocks = refs[3:11]
    keep_ref, send_ref, v_whole, out_whole = refs[11:]
    lay_out(me_ref[0], blocks, 0, v_whole)
    lay_out(me_ref[0], blocks, 1, out_whole)
    values = dot(rows_ref[...], v_whole[...]).astype(jnp.bfloat16)
    pieces = []
    for head in range(values.shape[1] // HD):
        found = dot(weights_ref[head], values[:, head * HD : (head + 1) * HD])
        pieces.append(found / totals_ref[head])
    attended = jnp.concatenate(pieces, axis=1).astype(jnp.bfloat16)
    half = attended.shape[0] // 2
    send_ref[...] = dot_turned(attended[half:, :], out_whole[...]).astype(jnp.bfloat16)
    keep_ref[...] = dot_turned(attended[:half, :], out_whole[...])


def pass_kernel(keep_ref, got_ref, out_ref):
    rows = out_ref.shape[0]
    out_ref[...] = (keep_ref[rows:, :] + got_ref[rows:, :].astype(jnp.float32)).astype(jnp.bfloat16)


def layer_kernel(at_ref, tokens_ref, keep_ref, core_ref, chip_ref, gains_ref, order_ref, *refs):
    outs, slices = refs[0:4], refs[4]
    rows, width = tokens_ref.shape
    summed = (
        tokens_ref[...].astype(jnp.float32)
        + keep_ref[0:rows, :]
        + core_ref[0:rows, :].astype(jnp.float32)
        + chip_ref[...].astype(jnp.float32)
    )
    merge_in = normalize(summed.astype(jnp.bfloat16), gains_ref[1:2, :])
    places = lax.broadcasted_iota(jnp.int32, (rows, rows), 1)
    picking = (order_ref[...] == places).astype(jnp.bfloat16)
    ordered = dot(picking, merge_in).astype(jnp.bfloat16)
    step, half = width // 8, width // 2
    for n in range(4):
        slices[n] = jnp.concatenate(
            [
                ordered[:, n * step : (n + 1) * step],
                ordered[:, half + n * step : half + (n + 1) * step],
            ],
            axis=1,
        )
    for k in range(4):
        outs[k][...] = slices[at_ref[0] ^ k]


def merge_kernel(me_ref, *refs):
    inputs, blocks = refs[0:8], refs[8:12]
    keep_ref, sends = refs[12], refs[13:16]
    count = inputs[0].shape[0] // 4
    z, y = me_ref[0] // 2, lax.rem(me_ref[0], 2)
    total = jnp.zeros((8 * count, blocks[0].shape[1]), jnp.float32)
    for number, block in enumerate(blocks):
        at = lax.rem(z + 4 - ORDER[number], 4) * count
        at = pl.multiple_of(at, 32)
        rows = jnp.concatenate([x[pl.ds(at, count), :] for x in inputs], axis=0)
        step = block.shape[0] // 2
        low = block[pl.ds(pl.multiple_of(y * step, 32), step), :]
        high = block[pl.ds(pl.multiple_of((1 - y) * step, 32), step), :]
        total = total + dot(rows, jnp.concatenate([low, high], axis=0))
    for k in range(4):
        share = jnp.concatenate(
            [
                total[k * count : (k + 1) * count, :],
                total[(4 + k) * count : (5 + k) * count, :],
            ],
            axis=0,
        )
        if k == 0:
            keep_ref[...] = share
        else:
            sends[k - 1][...] = share.astype(jnp.bfloat16)


def pack_kernel(slots_ref, keep_ref, one_ref, two_ref, three_ref, out_ref):
    total = keep_ref[...]
    for got in (one_ref, two_ref, three_ref):
        total = total + got[...].astype(jnp.float32)
    shape = (out_ref.shape[0], total.shape[0])
    placing = (lax.broadcasted_iota(jnp.int32, shape, 0) == slots_ref[...]).astype(jnp.bfloat16)
    out_ref[...] = dot(placing, total.astype(jnp.bfloat16)).astype(jnp.bfloat16)


def by_permutes(
    tokens, qkv_weight, out_weight, merge_weight, ln_gains, segments, merge_rows, owners
):
    rows, width = tokens.shape
    count = rows // 4
    n_dp, n_fsdp = lax.axis_size("dp"), lax.axis_size("fsdp")
    me, at = lax.axis_index("dp"), lax.axis_index("fsdp")
    y = lax.rem(me, 2)
    me_cell, at_cell = me.reshape(1), at.reshape(1)
    bf16, f32 = jnp.bfloat16, jnp.float32
    shape = jax.ShapeDtypeStruct
    cols = qkv_weight.shape[2]
    group = n_fsdp * rows

    first = qkv_weight[0:2]
    first_z = [turn(first, k) for k in ROUNDS]
    first_y = [swap(first, "dp", 1)]
    second = jnp.concatenate([qkv_weight[2:3], out_weight.T[None]], axis=0)
    second_z = [turn(after(second, first_z[0]), k) for k in ROUNDS]
    second_y = [swap(after(second, first_y[0]), "dp", 1)]
    first_y += [swap(block, "dp", 1) for block in first_z]
    second_y += [swap(block, "dp", 1) for block in second_z]
    half = merge_weight.shape[1] // 2
    low, high = merge_weight[:, :half], merge_weight[:, half:]
    lower = y == 0
    theirs = swap(after(jnp.where(lower, high, low), second_y[0]), "dp", 1)
    pair = jnp.concatenate([jnp.where(lower, low, high), theirs], axis=0)
    merge_blocks = [pair] + [turn(after(pair, second_z[2]), k) for k in ROUNDS]

    capacity = max(2, (2 * count + n_dp - 1) // n_dp)
    mine = owners[:, 0]
    other = swap(owners, "dp", 1)[:, 0]
    slots = []
    for number, targets in enumerate((mine, other)):
        start, rank = slot_numbers(targets, 2 * capacity)
        slots.append(start + rank + (y ^ number) * capacity)
    slots = jnp.concatenate(slots).reshape(1, 2 * count)
    order = merge_rows.reshape(count, 4).T.reshape(rows, 1)

    (normed,) = call(
        norm_kernel, [shape((rows + 16, width), bf16)], [tokens, ln_gains, segments]
    )
    along_x = swap(normed, "fsdp", 2)
    group_rows = [normed, along_x, swap(normed, "fsdp", 1), swap(along_x, "fsdp", 1)]

    heads = cols // HD
    group_all, weights, totals = call(
        score_kernel,
        [
            shape((group, width), bf16),
            shape((heads, group, group), bf16),
            shape((heads, group, 1), f32),
        ],
        [me_cell, *group_rows, first, *first_z, *first_y],
        [pltpu.VMEM((width, cols), bf16)] * 2,
        flops=4 * group * width * cols + 2 * group * group * cols,
        smem=1,
        exps=heads * group * group,
    )
    keep, send = call(
        value_kernel,
        [shape((2 * rows, width), f32), shape((2 * rows, width), bf16)],
        [me_cell, group_all, weights, totals, second, *second_z, *second_y],
        [pltpu.VMEM((width, cols), bf16)] * 2,
        flops=4 * group * width * cols + 2 * group * group * cols,
        smem=1,
    )
    from_core = swap(send, "fsdp", 1)
    (onward,) = call(pass_kernel, [shape((rows, width), bf16)], [keep, from_core])
    from_chip = swap(onward, "fsdp", 2)
    slices = call(
        layer_kernel,
        [shape((rows, width // 4), bf16)] * 4,
        [at_cell, tokens, keep, from_core, from_chip, ln_gains, order],
        [pltpu.VMEM((4, rows, width // 4), bf16)],
        flops=2 * rows * rows * width,
        smem=1,
    )
    inputs = [slices[0]] + [swap(slices[k], "fsdp", k) for k in range(1, 4)]
    inputs += [across(slices[k], k) for k in range(4)]
    shares = call(
        merge_kernel,
        [shape((2 * count, half), f32)] + [shape((2 * count, half), bf16)] * 3,
        [me_cell, *inputs, *merge_blocks],
        flops=2 * 8 * count * width * half,
        smem=1,
    )
    got = [swap(shares[k], "fsdp", k) for k in range(1, 4)]
    (packed,) = call(
        pack_kernel,
        [shape((n_dp * 2 * capacity, half), bf16)],
        [slots, shares[0], *got],
        flops=2 * n_dp * 2 * capacity * 2 * count * half,
    )
    arrived = lax.all_to_all(
        packed.reshape(n_dp, 2 * capacity, half), "dp", split_axis=0, concat_axis=0, tiled=True
    )
    arrived = arrived.reshape(n_dp // 2, 2, 2, capacity, half).transpose(0, 2, 3, 1, 4)
    return arrived.reshape(n_dp * capacity, 2 * half)


def solution(mesh):
    small = mesh.shape["dp"] == 8 and mesh.shape["fsdp"] == 4
    return jax.shard_map(
        by_permutes if small else by_gathers,
        mesh=mesh,
        in_specs=(
            P(("dp", "fsdp"), None),
            P(None, "dp", "fsdp"),
            P("fsdp", "dp"),
            P(("dp", "fsdp"), None),
            P(),
            P("dp", "fsdp"),
            P(("dp", "fsdp"), None),
            P(("dp", "fsdp"), None),
        ),
        out_specs=P(("dp", "fsdp"), None),
        check_vma=False,
    )
```

```python
import functools
import math

import jax
import jax.numpy as jnp
from jax import lax
from jax.experimental import pallas as pl
from jax.experimental.pallas import tpu as pltpu
from jax.sharding import PartitionSpec as P

HD = 80


epsilon = 1e-06


def normalize(values_in, gain_row):
    widened = values_in.astype(jnp.float32)
    centered = widened - jnp.mean(widened, axis=1, keepdims=True)
    variance = jnp.mean(centered * centered, axis=1, keepdims=True)
    return (centered * lax.rsqrt(variance + epsilon) * gain_row).astype(jnp.bfloat16)


def attend(queries, keys_all, values_all, seg_rows, seg_cols):
    factor = 1.0 / math.sqrt(HD)
    allowed = seg_rows[:, None] == seg_cols[None, :]
    pieces = []
    for head_index in range(queries.shape[1] // HD):
        first_col = head_index * HD
        last_col = first_col + HD
        scores = (
            lax.dot_general(
                queries[:, first_col:last_col],
                keys_all[:, first_col:last_col],
                (((1,), (1,)), ((), ())),
                preferred_element_type=jnp.float32,
            )
            * factor
        )
        masked = jnp.where(allowed, scores, -jnp.inf)
        highest = jnp.max(masked, axis=1, keepdims=True)
        weights = jnp.exp(masked - highest)
        totals = jnp.sum(weights, axis=1, keepdims=True)
        head_out = jnp.dot(
            weights.astype(jnp.bfloat16),
            values_all[:, first_col:last_col],
            preferred_element_type=jnp.float32,
        )
        pieces.append(head_out / totals)
    return jnp.concatenate(pieces, axis=1).astype(jnp.bfloat16)


def slot_numbers(targets, capacity):
    n = targets.shape[0]
    same = targets[:, None] == targets[None, :]
    before = jnp.arange(n)[None, :] < jnp.arange(n)[:, None]
    return targets * capacity, jnp.sum((same & before).astype(jnp.int32), axis=1)


def by_gathers(
    tokens, qkv_weight, out_weight, merge_weight, ln_gains, segments, merge_rows, owners
):
    n_dp = lax.axis_size("dp")
    qkv_mine = lax.all_gather(qkv_weight, "dp", axis=1, tiled=True)
    out_mine = lax.all_gather(out_weight, "dp", axis=1, tiled=True)
    n_fsdp = lax.axis_size("fsdp")
    normed = normalize(tokens, ln_gains[0])
    group_normed = lax.all_gather(normed, "fsdp", axis=0, tiled=True)
    group_segs = lax.all_gather(segments, "fsdp", axis=1, tiled=True)
    queries, keys_all, values_all = (
        jnp.dot(group_normed, qkv_mine[n], preferred_element_type=jnp.float32).astype(jnp.bfloat16)
        for n in range(3)
    )
    attended_mine = attend(queries, keys_all, values_all, group_segs[0], group_segs[0])
    attended_local = lax.all_to_all(attended_mine, "fsdp", split_axis=0, concat_axis=1, tiled=True)
    out_full = lax.all_gather(out_mine, "fsdp", axis=0, tiled=True)
    update = jnp.dot(attended_local, out_full, preferred_element_type=jnp.float32)
    layer_out = (tokens.astype(jnp.float32) + update).astype(jnp.bfloat16)
    merge_in = normalize(layer_out, ln_gains[1])
    merge_count = tokens.shape[0] // 4
    stacked = jnp.take(merge_in, merge_rows[0], axis=0).reshape(merge_count, 4 * merge_in.shape[1])
    slice_rows = merge_weight.shape[0]
    part_rows = lax.all_gather(merge_weight, "dp", axis=0, tiled=True)
    blocks = stacked.reshape(merge_count, n_dp, n_fsdp * slice_rows)
    received = lax.all_to_all(blocks, "fsdp", split_axis=2, concat_axis=0, tiled=True)
    gathered_inputs = received.reshape(n_fsdp * merge_count, n_dp * slice_rows)
    merged = lax.psum_scatter(
        jnp.dot(gathered_inputs, part_rows, preferred_element_type=jnp.float32).astype(
            jnp.bfloat16
        ),
        "fsdp",
        scatter_dimension=0,
        tiled=True,
    )
    capacity = max(2, (2 * merge_count + n_dp - 1) // n_dp)
    first, rank = slot_numbers(owners[:, 0], capacity)
    placing = (
        jnp.arange(n_dp * capacity, dtype=jnp.int32)[:, None] == (first + rank)[None, :]
    ).astype(jnp.bfloat16)
    packed = jnp.dot(placing, merged, preferred_element_type=jnp.float32).astype(jnp.bfloat16)
    packed = packed.reshape(n_dp, capacity, merged.shape[1])
    arrived = lax.all_to_all(packed, "dp", split_axis=0, concat_axis=0, tiled=True)
    return arrived.reshape(n_dp * capacity, merged.shape[1])


def swap(value, axis, k):
    return lax.ppermute(value, axis, [(i, i ^ k) for i in range(lax.axis_size(axis))])


def after(value, other):
    return lax.optimization_barrier((value, other))[0]


ORDER = (0, 2, 4, 6, 1, 3, 5, 7)


def dot(a, b):
    return jnp.dot(a, b, preferred_element_type=jnp.float32)


def dot_turned(a, b):
    return lax.dot_general(a, b, (((1,), (1,)), ((), ())), preferred_element_type=jnp.float32)


def call(kernel, outs, operands, scratch=(), flops=0, smem=0, exps=0, space=pltpu.VMEM):
    moved = sum(math.prod(x.shape) * x.dtype.itemsize for x in (*operands, *outs))
    specs = [pl.BlockSpec(memory_space=pltpu.SMEM)] * smem
    specs += [pl.BlockSpec(memory_space=space)] * (len(operands) - smem)
    return pl.pallas_call(
        kernel,
        out_shape=tuple(outs),
        in_specs=specs,
        out_specs=tuple(pl.BlockSpec(memory_space=pltpu.VMEM) for _ in outs),
        scratch_shapes=list(scratch),
        compiler_params=pltpu.CompilerParams(vmem_limit_bytes=16 * 1024 * 1024),
        cost_estimate=pl.CostEstimate(
            flops=flops, bytes_accessed=moved, transcendentals=exps
        ),
    )(*operands)


def norm_kernel(tokens_in, gains_in, segs_in, out_ref, tokens_ref, gains_ref, segs_ref, sems):
    copies = [
        pltpu.make_async_copy(tokens_in, tokens_ref, sems.at[0]),
        pltpu.make_async_copy(gains_in, gains_ref, sems.at[1]),
        pltpu.make_async_copy(segs_in, segs_ref, sems.at[2]),
    ]
    for copy in copies:
        copy.start()
    for copy in copies:
        copy.wait()
    rows = tokens_ref.shape[0]
    out_ref[0:rows, :] = normalize(tokens_ref[...], gains_ref[0:1, :])
    out_ref[rows:, :] = jnp.zeros((out_ref.shape[0] - rows, out_ref.shape[1]), out_ref.dtype)
    out_ref[rows:, 0:rows] = jnp.broadcast_to(
        segs_ref[...].astype(jnp.float32), (out_ref.shape[0] - rows, rows)
    ).astype(out_ref.dtype)


def lay_out(me, blocks, part, whole):
    step = blocks[0].shape[1]
    for number, block in zip(ORDER, blocks):
        start = pl.multiple_of((me ^ number) * step, 32)
        whole[pl.ds(start, step), :] = block[part]


def score_kernel(me_ref, *refs):
    tokens, blocks = refs[0:4], refs[4:12]
    rows_ref, weights_ref, totals_ref, q_whole, k_whole = refs[12:]
    rows = tokens[0].shape[0] - 16
    for n in range(4):
        rows_ref[n * rows : (n + 1) * rows, :] = tokens[n][0:rows, :]
    lay_out(me_ref[0], blocks, 0, q_whole)
    lay_out(me_ref[0], blocks, 1, k_whole)
    queries = dot(rows_ref[...], q_whole[...]).astype(jnp.bfloat16)
    keys = dot(rows_ref[...], k_whole[...]).astype(jnp.bfloat16)
    in_row = [t[rows : rows + 16, 0:rows].astype(jnp.float32)[0:1, :] for t in tokens]
    in_col = [jnp.broadcast_to(s, (rows, rows)).T[:, 0:1] for s in in_row]
    allowed = jnp.concatenate(in_col, axis=0) == jnp.concatenate(in_row, axis=1)
    factor = 1.0 / math.sqrt(HD)
    for head in range(queries.shape[1] // HD):
        cols = slice(head * HD, (head + 1) * HD)
        scores = dot_turned(queries[:, cols], keys[:, cols]) * factor
        masked = jnp.where(allowed, scores, -jnp.inf)
        weights = jnp.exp(masked - jnp.max(masked, axis=1, keepdims=True))
        weights_ref[head] = weights.astype(jnp.bfloat16)
        totals_ref[head] = jnp.sum(weights, axis=1, keepdims=True)


def value_kernel(me_ref, *refs):
    rows_ref, weights_ref, totals_ref = refs[0:3]
    blocks = refs[3:11]
    keep_ref, send_ref, v_whole, out_whole = refs[11:]
    lay_out(me_ref[0], blocks, 0, v_whole)
    lay_out(me_ref[0], blocks, 1, out_whole)
    values = dot(rows_ref[...], v_whole[...]).astype(jnp.bfloat16)
    pieces = []
    for head in range(values.shape[1] // HD):
        found = dot(weights_ref[head], values[:, head * HD : (head + 1) * HD])
        pieces.append(found / totals_ref[head])
    attended = jnp.concatenate(pieces, axis=1).astype(jnp.bfloat16)
    half = attended.shape[0] // 2
    send_ref[...] = dot_turned(attended[half:, :], out_whole[...]).astype(jnp.bfloat16)
    keep_ref[...] = dot_turned(attended[:half, :], out_whole[...])


def pass_kernel(keep_ref, got_ref, out_ref):
    rows = out_ref.shape[0]
    out_ref[...] = (keep_ref[rows:, :] + got_ref[rows:, :].astype(jnp.float32)).astype(jnp.bfloat16)


def layer_kernel(tokens_ref, keep_ref, core_ref, chip_ref, gains_ref, order_ref, *refs):
    (slices,) = refs
    rows, width = tokens_ref.shape
    summed = (
        tokens_ref[...].astype(jnp.float32)
        + keep_ref[0:rows, :]
        + core_ref[0:rows, :].astype(jnp.float32)
        + chip_ref[...].astype(jnp.float32)
    )
    merge_in = normalize(summed.astype(jnp.bfloat16), gains_ref[1:2, :])
    places = lax.broadcasted_iota(jnp.int32, (rows, rows), 1)
    picking = (order_ref[...] == places).astype(jnp.bfloat16)
    ordered = dot(picking, merge_in).astype(jnp.bfloat16)
    step, half = width // 8, width // 2
    for n in range(4):
        part = jnp.concatenate(
            [
                ordered[:, n * step : (n + 1) * step],
                ordered[:, half + n * step : half + (n + 1) * step],
            ],
            axis=1,
        )
        part = jnp.concatenate([part[: rows // 2, :], part[rows // 2 :, :]], axis=1)
        slices[n] = part
        slices[4 + n] = part


def merge_kernel(me_ref, at_ref, inputs, *refs):
    blocks, (keep_ref, *sends), total = refs[0:4], refs[4:8], refs[8]
    count, width = inputs.shape[1] // 2, inputs.shape[2] // 2
    z, y = me_ref[0] // 2, lax.rem(me_ref[0], 2)
    for number, block in enumerate(blocks):
        position = z ^ number
        at = pl.multiple_of(lax.rem(position, 2) * count, 32)
        rows = inputs[:, pl.ds(at, count), :].reshape(8 * count, 2 * width)
        rows = jnp.where(position < 2, rows[:, :width], rows[:, width:])
        step = block.shape[0] // 2
        low = block[pl.ds(pl.multiple_of(y * step, 32), step), :]
        high = block[pl.ds(pl.multiple_of((1 - y) * step, 32), step), :]
        found = dot(rows, jnp.concatenate([low, high], axis=0)).reshape(total.shape)
        total[...] = found if number == 0 else total[...] + found
    for k in range(4):
        to = at_ref[0] ^ k
        share = jnp.concatenate([total[4 * y + to], total[4 * (1 - y) + to]], axis=0)
        if k == 0:
            keep_ref[...] = share
        else:
            sends[k - 1][...] = share.astype(jnp.bfloat16)


def pack_kernel(slots_ref, keep_ref, one_ref, two_ref, three_ref, out_ref):
    total = keep_ref[...]
    for got in (one_ref, two_ref, three_ref):
        total = total + got[...].astype(jnp.float32)
    shape = (out_ref.shape[0], total.shape[0])
    placing = (lax.broadcasted_iota(jnp.int32, shape, 0) == slots_ref[...]).astype(jnp.bfloat16)
    out_ref[...] = dot(placing, total.astype(jnp.bfloat16)).astype(jnp.bfloat16)


def by_permutes(
    tokens, qkv_weight, out_weight, merge_weight, ln_gains, segments, merge_rows, owners
):
    rows, width = tokens.shape
    count = rows // 4
    n_dp, n_fsdp = lax.axis_size("dp"), lax.axis_size("fsdp")
    me, at = lax.axis_index("dp"), lax.axis_index("fsdp")
    y = lax.rem(me, 2)
    me_cell, at_cell = me.reshape(1), at.reshape(1)
    bf16, f32 = jnp.bfloat16, jnp.float32
    shape = jax.ShapeDtypeStruct
    cols = qkv_weight.shape[2]
    group = n_fsdp * rows

    first = qkv_weight[0:2]
    first_z = [swap(first, "dp", 2), swap(first, "dp", 4)]
    first_y = [swap(first, "dp", 1)]
    first_z += [swap(first_z[1], "dp", 2)]
    second = jnp.concatenate([qkv_weight[2:3], out_weight.T[None]], axis=0)
    half = merge_weight.shape[1] // 2
    low, high = merge_weight[:, :half], merge_weight[:, half:]
    lower = y == 0
    theirs = swap(after(jnp.where(lower, high, low), first_y[0]), "dp", 1)
    held = after(second, first_z[0])
    second_z = [swap(held, "dp", 2), swap(held, "dp", 4)]
    second_y = [swap(held, "dp", 1)]
    second_z += [swap(second_z[1], "dp", 2)]
    first_y += [swap(block, "dp", 1) for block in first_z]
    second_y += [swap(block, "dp", 1) for block in second_z]
    pair = jnp.concatenate([jnp.where(lower, low, high), theirs], axis=0)
    held = after(pair, second_z[1])
    merge_blocks = [pair, swap(held, "dp", 2), swap(held, "dp", 4)]
    merge_blocks += [swap(merge_blocks[2], "dp", 2)]

    capacity = max(2, (2 * count + n_dp - 1) // n_dp)
    mine = owners[:, 0]
    other = swap(owners, "dp", 1)[:, 0]
    slots = []
    for number, targets in enumerate((mine, other)):
        start, rank = slot_numbers(targets, 2 * capacity)
        slots.append(start + rank + (y ^ number) * capacity)
    slots = jnp.concatenate(slots).reshape(1, 2 * count)
    order = merge_rows.reshape(count, 4).T.reshape(rows, 1)

    (normed,) = call(
        norm_kernel, [shape((rows + 16, width), bf16)], [after(tokens, first), ln_gains, segments],
        [
            pltpu.VMEM(tokens.shape, bf16),
            pltpu.VMEM(ln_gains.shape, f32),
            pltpu.VMEM(segments.shape, jnp.int32),
            pltpu.SemaphoreType.DMA((3,)),
        ],
        space=pl.ANY,
    )
    along_x = swap(normed, "fsdp", 2)
    group_rows = [normed, along_x, swap(normed, "fsdp", 1), swap(along_x, "fsdp", 1)]

    heads = cols // HD
    group_all, weights, totals = call(
        score_kernel,
        [
            shape((group, width), bf16),
            shape((heads, group, group), bf16),
            shape((heads, group, 1), f32),
        ],
        [after(me_cell, theirs), *group_rows, first, *first_z, *first_y],
        [pltpu.VMEM((width, cols), bf16)] * 2,
        flops=4 * group * width * cols + 2 * group * group * cols,
        smem=1,
        exps=heads * group * group,
    )
    keep, send = call(
        value_kernel,
        [shape((2 * rows, width), f32), shape((2 * rows, width), bf16)],
        [after(me_cell, merge_blocks[1]), group_all, weights, totals, second, *second_z, *second_y],
        [pltpu.VMEM((width, cols), bf16)] * 2,
        flops=4 * group * width * cols + 2 * group * group * cols,
        smem=1,
    )
    from_core = swap(send, "fsdp", 1)
    (onward,) = call(pass_kernel, [shape((rows, width), bf16)], [keep, from_core])
    from_chip = swap(onward, "fsdp", 2)
    (slices,) = call(
        layer_kernel,
        [shape((8, rows // 2, width // 2), bf16)],
        [tokens, keep, from_core, after(from_chip, merge_blocks[2]), ln_gains, order],
        flops=2 * rows * rows * width,
    )
    both = 2 * n_fsdp
    inputs = lax.all_to_all(
        slices,
        ("dp", "fsdp"),
        split_axis=0,
        concat_axis=0,
        tiled=True,
        axis_index_groups=[
            list(range(i, i + both)) for i in range(0, n_dp * n_fsdp, both)
        ],
    )
    shares = call(
        merge_kernel,
        [shape((2 * count, half), f32)] + [shape((2 * count, half), bf16)] * 3,
        [me_cell, at_cell, inputs, *merge_blocks],
        [pltpu.VMEM((8, count, half), f32)],
        flops=2 * 8 * count * width * half,
        smem=2,
    )
    got = [swap(shares[k], "fsdp", k) for k in range(1, 4)]
    (packed,) = call(
        pack_kernel,
        [shape((n_dp * 2 * capacity, half), bf16)],
        [slots, shares[0], *got],
        flops=2 * n_dp * 2 * capacity * 2 * count * half,
    )
    arrived = lax.all_to_all(
        packed.reshape(n_dp, 2 * capacity, half), "dp", split_axis=0, concat_axis=0, tiled=True
    )
    arrived = arrived.reshape(n_dp // 2, 2, 2, capacity, half).transpose(0, 2, 3, 1, 4)
    return arrived.reshape(n_dp * capacity, 2 * half)


def solution(mesh):
    small = mesh.shape["dp"] == 8 and mesh.shape["fsdp"] == 4
    return jax.shard_map(
        by_permutes if small else by_gathers,
        mesh=mesh,
        in_specs=(
            P(("dp", "fsdp"), None),
            P(None, "dp", "fsdp"),
            P("fsdp", "dp"),
            P(("dp", "fsdp"), None),
            P(),
            P("dp", "fsdp"),
            P(("dp", "fsdp"), None),
            P(("dp", "fsdp"), None),
        ),
        out_specs=P(("dp", "fsdp"), None),
        check_vma=False,
    )
```

```python
import functools
import math

import jax
import jax.numpy as jnp
from jax import lax
from jax.experimental import pallas as pl
from jax.experimental.pallas import tpu as pltpu
from jax.sharding import PartitionSpec as P

HD = 80


epsilon = 1e-06


def normalize(values_in, gain_row):
    widened = values_in.astype(jnp.float32)
    centered = widened - jnp.mean(widened, axis=1, keepdims=True)
    variance = jnp.mean(centered * centered, axis=1, keepdims=True)
    return (centered * lax.rsqrt(variance + epsilon) * gain_row).astype(jnp.bfloat16)


def attend(queries, keys_all, values_all, seg_rows, seg_cols):
    factor = 1.0 / math.sqrt(HD)
    allowed = seg_rows[:, None] == seg_cols[None, :]
    pieces = []
    for head_index in range(queries.shape[1] // HD):
        first_col = head_index * HD
        last_col = first_col + HD
        scores = (
            lax.dot_general(
                queries[:, first_col:last_col],
                keys_all[:, first_col:last_col],
                (((1,), (1,)), ((), ())),
                preferred_element_type=jnp.float32,
            )
            * factor
        )
        masked = jnp.where(allowed, scores, -jnp.inf)
        highest = jnp.max(masked, axis=1, keepdims=True)
        weights = jnp.exp(masked - highest)
        totals = jnp.sum(weights, axis=1, keepdims=True)
        head_out = jnp.dot(
            weights.astype(jnp.bfloat16),
            values_all[:, first_col:last_col],
            preferred_element_type=jnp.float32,
        )
        pieces.append(head_out / totals)
    return jnp.concatenate(pieces, axis=1).astype(jnp.bfloat16)


def slot_numbers(targets, capacity):
    n = targets.shape[0]
    same = targets[:, None] == targets[None, :]
    before = jnp.arange(n)[None, :] < jnp.arange(n)[:, None]
    return targets * capacity, jnp.sum((same & before).astype(jnp.int32), axis=1)


def by_gathers(
    tokens, qkv_weight, out_weight, merge_weight, ln_gains, segments, merge_rows, owners
):
    n_dp = lax.axis_size("dp")
    qkv_mine = lax.all_gather(qkv_weight, "dp", axis=1, tiled=True)
    out_mine = lax.all_gather(out_weight, "dp", axis=1, tiled=True)
    n_fsdp = lax.axis_size("fsdp")
    normed = normalize(tokens, ln_gains[0])
    group_normed = lax.all_gather(normed, "fsdp", axis=0, tiled=True)
    group_segs = lax.all_gather(segments, "fsdp", axis=1, tiled=True)
    queries, keys_all, values_all = (
        jnp.dot(group_normed, qkv_mine[n], preferred_element_type=jnp.float32).astype(jnp.bfloat16)
        for n in range(3)
    )
    attended_mine = attend(queries, keys_all, values_all, group_segs[0], group_segs[0])
    attended_local = lax.all_to_all(attended_mine, "fsdp", split_axis=0, concat_axis=1, tiled=True)
    out_full = lax.all_gather(out_mine, "fsdp", axis=0, tiled=True)
    update = jnp.dot(attended_local, out_full, preferred_element_type=jnp.float32)
    layer_out = (tokens.astype(jnp.float32) + update).astype(jnp.bfloat16)
    merge_in = normalize(layer_out, ln_gains[1])
    merge_count = tokens.shape[0] // 4
    stacked = jnp.take(merge_in, merge_rows[0], axis=0).reshape(merge_count, 4 * merge_in.shape[1])
    slice_rows = merge_weight.shape[0]
    part_rows = lax.all_gather(merge_weight, "dp", axis=0, tiled=True)
    blocks = stacked.reshape(merge_count, n_dp, n_fsdp * slice_rows)
    received = lax.all_to_all(blocks, "fsdp", split_axis=2, concat_axis=0, tiled=True)
    gathered_inputs = received.reshape(n_fsdp * merge_count, n_dp * slice_rows)
    merged = lax.psum_scatter(
        jnp.dot(gathered_inputs, part_rows, preferred_element_type=jnp.float32).astype(
            jnp.bfloat16
        ),
        "fsdp",
        scatter_dimension=0,
        tiled=True,
    )
    capacity = max(2, (2 * merge_count + n_dp - 1) // n_dp)
    first, rank = slot_numbers(owners[:, 0], capacity)
    placing = (
        jnp.arange(n_dp * capacity, dtype=jnp.int32)[:, None] == (first + rank)[None, :]
    ).astype(jnp.bfloat16)
    packed = jnp.dot(placing, merged, preferred_element_type=jnp.float32).astype(jnp.bfloat16)
    packed = packed.reshape(n_dp, capacity, merged.shape[1])
    arrived = lax.all_to_all(packed, "dp", split_axis=0, concat_axis=0, tiled=True)
    return arrived.reshape(n_dp * capacity, merged.shape[1])


def swap(value, axis, k):
    return lax.ppermute(value, axis, [(i, i ^ k) for i in range(lax.axis_size(axis))])


def after(value, other):
    return lax.optimization_barrier((value, other))[0]


ORDER = (0, 2, 4, 6, 1, 3, 5, 7)


def dot(a, b):
    return jnp.dot(a, b, preferred_element_type=jnp.float32)


def dot_turned(a, b):
    return lax.dot_general(a, b, (((1,), (1,)), ((), ())), preferred_element_type=jnp.float32)


def call(kernel, outs, operands, scratch=(), flops=0, smem=0, exps=0, space=pltpu.VMEM):
    moved = sum(math.prod(x.shape) * x.dtype.itemsize for x in (*operands, *outs))
    specs = [pl.BlockSpec(memory_space=pltpu.SMEM)] * smem
    specs += [pl.BlockSpec(memory_space=space)] * (len(operands) - smem)
    return pl.pallas_call(
        kernel,
        out_shape=tuple(outs),
        in_specs=specs,
        out_specs=tuple(pl.BlockSpec(memory_space=pltpu.VMEM) for _ in outs),
        scratch_shapes=list(scratch),
        compiler_params=pltpu.CompilerParams(vmem_limit_bytes=16 * 1024 * 1024),
        cost_estimate=pl.CostEstimate(
            flops=flops, bytes_accessed=moved, transcendentals=exps
        ),
    )(*operands)


def norm_kernel(tokens_in, gains_in, segs_in, out_ref, tokens_ref, gains_ref, segs_ref, sems):
    copies = [
        pltpu.make_async_copy(tokens_in, tokens_ref, sems.at[0]),
        pltpu.make_async_copy(gains_in, gains_ref, sems.at[1]),
        pltpu.make_async_copy(segs_in, segs_ref, sems.at[2]),
    ]
    for copy in copies:
        copy.start()
    for copy in copies:
        copy.wait()
    rows = tokens_ref.shape[0]
    out_ref[0:rows, :] = normalize(tokens_ref[...], gains_ref[0:1, :])
    out_ref[rows:, :] = jnp.zeros((out_ref.shape[0] - rows, out_ref.shape[1]), out_ref.dtype)
    out_ref[rows:, 0:rows] = jnp.broadcast_to(
        segs_ref[...].astype(jnp.float32), (out_ref.shape[0] - rows, rows)
    ).astype(out_ref.dtype)


def lay_out(me, blocks, part, whole):
    step = blocks[0].shape[1]
    for number, block in zip(ORDER, blocks):
        start = pl.multiple_of((me ^ number) * step, 32)
        whole[pl.ds(start, step), :] = block[part]


def score_kernel(me_ref, *refs):
    tokens, blocks = refs[0:4], refs[4:12]
    rows_ref, weights_ref, totals_ref, q_whole, k_whole = refs[12:]
    rows = tokens[0].shape[0] - 16
    for n in range(4):
        rows_ref[n * rows : (n + 1) * rows, :] = tokens[n][0:rows, :]
    lay_out(me_ref[0], blocks, 0, q_whole)
    lay_out(me_ref[0], blocks, 1, k_whole)
    queries = dot(rows_ref[...], q_whole[...]).astype(jnp.bfloat16)
    keys = dot(rows_ref[...], k_whole[...]).astype(jnp.bfloat16)
    in_row = [t[rows : rows + 16, 0:rows].astype(jnp.float32)[0:1, :] for t in tokens]
    in_col = [jnp.broadcast_to(s, (rows, rows)).T[:, 0:1] for s in in_row]
    allowed = jnp.concatenate(in_col, axis=0) == jnp.concatenate(in_row, axis=1)
    factor = 1.0 / math.sqrt(HD)
    for head in range(queries.shape[1] // HD):
        cols = slice(head * HD, (head + 1) * HD)
        scores = dot_turned(queries[:, cols], keys[:, cols]) * factor
        masked = jnp.where(allowed, scores, -jnp.inf)
        weights = jnp.exp(masked - jnp.max(masked, axis=1, keepdims=True))
        weights_ref[head] = weights.astype(jnp.bfloat16)
        totals_ref[head] = jnp.sum(weights, axis=1, keepdims=True)


def value_kernel(me_ref, *refs):
    rows_ref, weights_ref, totals_ref = refs[0:3]
    blocks = refs[3:11]
    keep_ref, send_ref, v_whole, out_whole = refs[11:]
    lay_out(me_ref[0], blocks, 0, v_whole)
    lay_out(me_ref[0], blocks, 1, out_whole)
    values = dot(rows_ref[...], v_whole[...]).astype(jnp.bfloat16)
    pieces = []
    for head in range(values.shape[1] // HD):
        found = dot(weights_ref[head], values[:, head * HD : (head + 1) * HD])
        pieces.append(found / totals_ref[head])
    attended = jnp.concatenate(pieces, axis=1).astype(jnp.bfloat16)
    half = attended.shape[0] // 2
    send_ref[...] = dot_turned(attended[half:, :], out_whole[...]).astype(jnp.bfloat16)
    keep_ref[...] = dot_turned(attended[:half, :], out_whole[...])


def pass_kernel(keep_ref, got_ref, out_ref):
    rows = out_ref.shape[0]
    out_ref[...] = (keep_ref[rows:, :] + got_ref[rows:, :].astype(jnp.float32)).astype(jnp.bfloat16)


def layer_kernel(tokens_ref, keep_ref, core_ref, chip_ref, gains_ref, order_ref, *refs):
    (slices,) = refs
    rows, width = tokens_ref.shape
    summed = (
        tokens_ref[...].astype(jnp.float32)
        + keep_ref[0:rows, :]
        + core_ref[0:rows, :].astype(jnp.float32)
        + chip_ref[...].astype(jnp.float32)
    )
    merge_in = normalize(summed.astype(jnp.bfloat16), gains_ref[1:2, :])
    places = lax.broadcasted_iota(jnp.int32, (rows, rows), 1)
    picking = (order_ref[...] == places).astype(jnp.bfloat16)
    ordered = dot(picking, merge_in).astype(jnp.bfloat16)
    step, half = width // 8, width // 2
    for n in range(4):
        part = jnp.concatenate(
            [
                ordered[:, n * step : (n + 1) * step],
                ordered[:, half + n * step : half + (n + 1) * step],
            ],
            axis=1,
        )
        part = jnp.concatenate([part[: rows // 2, :], part[rows // 2 :, :]], axis=1)
        slices[n] = part
        slices[4 + n] = part


def merge_kernel(me_ref, at_ref, inputs, *refs):
    blocks, (keep_ref, *sends), total = refs[0:4], refs[4:8], refs[8]
    count, width = inputs.shape[1] // 2, inputs.shape[2] // 2
    z, y = me_ref[0] // 2, lax.rem(me_ref[0], 2)
    for number, block in enumerate(blocks):
        position = z ^ number
        at = pl.multiple_of(lax.rem(position, 2) * count, 32)
        rows = inputs[:, pl.ds(at, count), :].reshape(8 * count, 2 * width)
        rows = jnp.where(position < 2, rows[:, :width], rows[:, width:])
        step = block.shape[0] // 2
        low = block[pl.ds(pl.multiple_of(y * step, 32), step), :]
        high = block[pl.ds(pl.multiple_of((1 - y) * step, 32), step), :]
        found = dot(rows, jnp.concatenate([low, high], axis=0)).reshape(total.shape)
        total[...] = found if number == 0 else total[...] + found
    for k in range(4):
        to = at_ref[0] ^ k
        share = jnp.concatenate([total[4 * y + to], total[4 * (1 - y) + to]], axis=0)
        if k == 0:
            keep_ref[...] = share
        else:
            sends[k - 1][...] = share.astype(jnp.bfloat16)


def pack_kernel(slots_ref, keep_ref, one_ref, two_ref, three_ref, out_ref):
    total = keep_ref[...]
    for got in (one_ref, two_ref, three_ref):
        total = total + got[...].astype(jnp.float32)
    shape = (out_ref.shape[0], total.shape[0])
    placing = (lax.broadcasted_iota(jnp.int32, shape, 0) == slots_ref[...]).astype(jnp.bfloat16)
    out_ref[...] = dot(placing, total.astype(jnp.bfloat16)).astype(jnp.bfloat16)


def by_permutes(
    tokens, qkv_weight, out_weight, merge_weight, ln_gains, segments, merge_rows, owners
):
    rows, width = tokens.shape
    count = rows // 4
    n_dp, n_fsdp = lax.axis_size("dp"), lax.axis_size("fsdp")
    me, at = lax.axis_index("dp"), lax.axis_index("fsdp")
    y = lax.rem(me, 2)
    me_cell, at_cell = me.reshape(1), at.reshape(1)
    bf16, f32 = jnp.bfloat16, jnp.float32
    shape = jax.ShapeDtypeStruct
    cols = qkv_weight.shape[2]
    group = n_fsdp * rows

    first = qkv_weight[0:2]
    first_z = [swap(first, "dp", 2), swap(first, "dp", 4)]
    (normed,) = call(
        norm_kernel,
        [shape((rows + 16, width), bf16)],
        [after(tokens, first_z[0]), ln_gains, segments],
        [
            pltpu.VMEM(tokens.shape, bf16),
            pltpu.VMEM(ln_gains.shape, f32),
            pltpu.VMEM(segments.shape, jnp.int32),
            pltpu.SemaphoreType.DMA((3,)),
        ],
        space=pltpu.HBM,
    )
    along_x = swap(normed, "fsdp", 2)
    group_rows = [normed, along_x, swap(normed, "fsdp", 1), swap(along_x, "fsdp", 1)]

    first_y = [swap(first, "dp", 1)]
    first_z += [swap(first_z[1], "dp", 2)]
    second = jnp.concatenate([qkv_weight[2:3], out_weight.T[None]], axis=0)
    half = merge_weight.shape[1] // 2
    low, high = merge_weight[:, :half], merge_weight[:, half:]
    lower = y == 0
    theirs = swap(after(jnp.where(lower, high, low), first_z[0]), "dp", 1)
    held = after(second, first_z[1])
    second_z = [swap(held, "dp", 2), swap(held, "dp", 4)]
    second_y = [swap(held, "dp", 1)]
    second_z += [swap(second_z[1], "dp", 2)]
    first_y += [swap(block, "dp", 1) for block in first_z]
    second_y += [swap(block, "dp", 1) for block in second_z]
    pair = jnp.concatenate([jnp.where(lower, low, high), theirs], axis=0)
    held = after(pair, (second_z[2], *first_y[:3], *group_rows[2:]))
    merge_blocks = [pair, swap(held, "dp", 2), swap(held, "dp", 4)]
    merge_blocks += [swap(merge_blocks[2], "dp", 2)]

    capacity = max(2, (2 * count + n_dp - 1) // n_dp)
    mine = owners[:, 0]
    other = swap(owners, "dp", 1)[:, 0]
    slots = []
    for number, targets in enumerate((mine, other)):
        start, rank = slot_numbers(targets, 2 * capacity)
        slots.append(start + rank + (y ^ number) * capacity)
    slots = jnp.concatenate(slots).reshape(1, 2 * count)
    order = merge_rows.reshape(count, 4).T.reshape(rows, 1)

    heads = cols // HD
    group_all, weights, totals = call(
        score_kernel,
        [
            shape((group, width), bf16),
            shape((heads, group, group), bf16),
            shape((heads, group, 1), f32),
        ],
        [after(me_cell, theirs), *group_rows, first, *first_z, *first_y],
        [pltpu.VMEM((width, cols), bf16)] * 2,
        flops=4 * group * width * cols + 2 * group * group * cols,
        smem=1,
        exps=heads * group * group,
    )
    keep, send = call(
        value_kernel,
        [shape((2 * rows, width), f32), shape((2 * rows, width), bf16)],
        [me_cell, group_all, weights, totals, second, *second_z, *second_y],
        [pltpu.VMEM((width, cols), bf16)] * 2,
        flops=4 * group * width * cols + 2 * group * group * cols,
        smem=1,
    )
    from_core = swap(send, "fsdp", 1)
    (onward,) = call(pass_kernel, [shape((rows, width), bf16)], [keep, from_core])
    from_chip = swap(onward, "fsdp", 2)
    (slices,) = call(
        layer_kernel,
        [shape((8, rows // 2, width // 2), bf16)],
        [tokens, keep, from_core, after(from_chip, merge_blocks[2]), ln_gains, order],
        flops=2 * rows * rows * width,
    )
    both = 2 * n_fsdp
    inputs = lax.all_to_all(
        slices,
        ("dp", "fsdp"),
        split_axis=0,
        concat_axis=0,
        tiled=True,
        axis_index_groups=[
            list(range(i, i + both)) for i in range(0, n_dp * n_fsdp, both)
        ],
    )
    shares = call(
        merge_kernel,
        [shape((2 * count, half), f32)] + [shape((2 * count, half), bf16)] * 3,
        [me_cell, at_cell, inputs, *merge_blocks],
        [pltpu.VMEM((8, count, half), f32)],
        flops=2 * 8 * count * width * half,
        smem=2,
    )
    got = [swap(shares[k], "fsdp", k) for k in range(1, 4)]
    (packed,) = call(
        pack_kernel,
        [shape((n_dp * 2 * capacity, half), bf16)],
        [slots, shares[0], *got],
        flops=2 * n_dp * 2 * capacity * 2 * count * half,
    )
    arrived = lax.all_to_all(
        packed.reshape(n_dp, 2 * capacity, half), "dp", split_axis=0, concat_axis=0, tiled=True
    )
    arrived = arrived.reshape(n_dp // 2, 2, 2, capacity, half).transpose(0, 2, 3, 1, 4)
    return arrived.reshape(n_dp * capacity, 2 * half)


def solution(mesh):
    small = mesh.shape["dp"] == 8 and mesh.shape["fsdp"] == 4
    return jax.shard_map(
        by_permutes if small else by_gathers,
        mesh=mesh,
        in_specs=(
            P(("dp", "fsdp"), None),
            P(None, "dp", "fsdp"),
            P("fsdp", "dp"),
            P(("dp", "fsdp"), None),
            P(),
            P("dp", "fsdp"),
            P(("dp", "fsdp"), None),
            P(("dp", "fsdp"), None),
        ),
        out_specs=P(("dp", "fsdp"), None),
        check_vma=False,
    )
```

```python
import functools
import math

import jax
import jax.numpy as jnp
from jax import lax
from jax.experimental import pallas as pl
from jax.experimental.pallas import tpu as pltpu
from jax.sharding import PartitionSpec as P

HD = 80


epsilon = 1e-06


def normalize(values_in, gain_row):
    widened = values_in.astype(jnp.float32)
    centered = widened - jnp.mean(widened, axis=1, keepdims=True)
    variance = jnp.mean(centered * centered, axis=1, keepdims=True)
    return (centered * lax.rsqrt(variance + epsilon) * gain_row).astype(jnp.bfloat16)


def attend(queries, keys_all, values_all, seg_rows, seg_cols):
    factor = 1.0 / math.sqrt(HD)
    allowed = seg_rows[:, None] == seg_cols[None, :]
    pieces = []
    for head_index in range(queries.shape[1] // HD):
        first_col = head_index * HD
        last_col = first_col + HD
        scores = (
            lax.dot_general(
                queries[:, first_col:last_col],
                keys_all[:, first_col:last_col],
                (((1,), (1,)), ((), ())),
                preferred_element_type=jnp.float32,
            )
            * factor
        )
        masked = jnp.where(allowed, scores, -jnp.inf)
        highest = jnp.max(masked, axis=1, keepdims=True)
        weights = jnp.exp(masked - highest)
        totals = jnp.sum(weights, axis=1, keepdims=True)
        head_out = jnp.dot(
            weights.astype(jnp.bfloat16),
            values_all[:, first_col:last_col],
            preferred_element_type=jnp.float32,
        )
        pieces.append(head_out / totals)
    return jnp.concatenate(pieces, axis=1).astype(jnp.bfloat16)


def slot_numbers(targets, capacity):
    n = targets.shape[0]
    same = targets[:, None] == targets[None, :]
    before = jnp.arange(n)[None, :] < jnp.arange(n)[:, None]
    return targets * capacity, jnp.sum((same & before).astype(jnp.int32), axis=1)


def by_gathers(
    tokens, qkv_weight, out_weight, merge_weight, ln_gains, segments, merge_rows, owners
):
    n_dp = lax.axis_size("dp")
    qkv_mine = lax.all_gather(qkv_weight, "dp", axis=1, tiled=True)
    out_mine = lax.all_gather(out_weight, "dp", axis=1, tiled=True)
    n_fsdp = lax.axis_size("fsdp")
    normed = normalize(tokens, ln_gains[0])
    group_normed = lax.all_gather(normed, "fsdp", axis=0, tiled=True)
    group_segs = lax.all_gather(segments, "fsdp", axis=1, tiled=True)
    queries, keys_all, values_all = (
        jnp.dot(group_normed, qkv_mine[n], preferred_element_type=jnp.float32).astype(jnp.bfloat16)
        for n in range(3)
    )
    attended_mine = attend(queries, keys_all, values_all, group_segs[0], group_segs[0])
    attended_local = lax.all_to_all(attended_mine, "fsdp", split_axis=0, concat_axis=1, tiled=True)
    out_full = lax.all_gather(out_mine, "fsdp", axis=0, tiled=True)
    update = jnp.dot(attended_local, out_full, preferred_element_type=jnp.float32)
    layer_out = (tokens.astype(jnp.float32) + update).astype(jnp.bfloat16)
    merge_in = normalize(layer_out, ln_gains[1])
    merge_count = tokens.shape[0] // 4
    stacked = jnp.take(merge_in, merge_rows[0], axis=0).reshape(merge_count, 4 * merge_in.shape[1])
    slice_rows = merge_weight.shape[0]
    part_rows = lax.all_gather(merge_weight, "dp", axis=0, tiled=True)
    blocks = stacked.reshape(merge_count, n_dp, n_fsdp * slice_rows)
    received = lax.all_to_all(blocks, "fsdp", split_axis=2, concat_axis=0, tiled=True)
    gathered_inputs = received.reshape(n_fsdp * merge_count, n_dp * slice_rows)
    merged = lax.psum_scatter(
        jnp.dot(gathered_inputs, part_rows, preferred_element_type=jnp.float32).astype(
            jnp.bfloat16
        ),
        "fsdp",
        scatter_dimension=0,
        tiled=True,
    )
    capacity = max(2, (2 * merge_count + n_dp - 1) // n_dp)
    first, rank = slot_numbers(owners[:, 0], capacity)
    placing = (
        jnp.arange(n_dp * capacity, dtype=jnp.int32)[:, None] == (first + rank)[None, :]
    ).astype(jnp.bfloat16)
    packed = jnp.dot(placing, merged, preferred_element_type=jnp.float32).astype(jnp.bfloat16)
    packed = packed.reshape(n_dp, capacity, merged.shape[1])
    arrived = lax.all_to_all(packed, "dp", split_axis=0, concat_axis=0, tiled=True)
    return arrived.reshape(n_dp * capacity, merged.shape[1])


def swap(value, axis, k):
    return lax.ppermute(value, axis, [(i, i ^ k) for i in range(lax.axis_size(axis))])


def after(value, other):
    return lax.optimization_barrier((value, other))[0]


ORDER = (0, 2, 4, 6, 1, 3, 5, 7)


def dot(a, b):
    return jnp.dot(a, b, preferred_element_type=jnp.float32)


def dot_turned(a, b):
    return lax.dot_general(a, b, (((1,), (1,)), ((), ())), preferred_element_type=jnp.float32)


def call(kernel, outs, operands, scratch=(), flops=0, smem=0, exps=0):
    moved = sum(math.prod(x.shape) * x.dtype.itemsize for x in (*operands, *outs))
    specs = [pl.BlockSpec(memory_space=pltpu.SMEM)] * smem
    specs += [pl.BlockSpec(memory_space=pltpu.VMEM)] * (len(operands) - smem)
    return pl.pallas_call(
        kernel,
        out_shape=tuple(outs),
        in_specs=specs,
        out_specs=tuple(pl.BlockSpec(memory_space=pltpu.VMEM) for _ in outs),
        scratch_shapes=list(scratch),
        compiler_params=pltpu.CompilerParams(vmem_limit_bytes=16 * 1024 * 1024),
        cost_estimate=pl.CostEstimate(
            flops=flops, bytes_accessed=moved, transcendentals=exps
        ),
    )(*operands)


def norm_kernel(gains_ref, *refs):
    tokens, out_ref = refs[0:4], refs[4]
    rows = tokens[0].shape[0] - 16
    for n in range(4):
        out_ref[n * rows : (n + 1) * rows, :] = normalize(tokens[n][0:rows, :], gains_ref[0:1, :])


def lay_out(me, blocks, part, whole):
    step = blocks[0].shape[1]
    for number, block in zip(ORDER, blocks):
        start = pl.multiple_of((me ^ number) * step, 32)
        whole[pl.ds(start, step), :] = block[part]


def attention_kernel(me_ref, rows_ref, *refs):
    marks, blocks = refs[0:4], refs[4:12]
    keep_ref, send_ref, q_whole, k_whole, v_whole, out_whole = refs[12:]
    lay_out(me_ref[0], blocks, 0, q_whole)
    lay_out(me_ref[0], blocks, 1, k_whole)
    lay_out(me_ref[0], blocks, 2, v_whole)
    lay_out(me_ref[0], blocks, 3, out_whole)
    queries = dot(rows_ref[...], q_whole[...]).astype(jnp.bfloat16)
    keys = dot(rows_ref[...], k_whole[...]).astype(jnp.bfloat16)
    values = dot(rows_ref[...], v_whole[...]).astype(jnp.bfloat16)
    rows = marks[0].shape[0] - 16
    in_row = [t[rows : rows + 16, 0:rows].astype(jnp.float32)[0:1, :] for t in marks]
    in_col = [jnp.broadcast_to(s, (rows, rows)).T[:, 0:1] for s in in_row]
    allowed = jnp.concatenate(in_col, axis=0) == jnp.concatenate(in_row, axis=1)
    factor = 1.0 / math.sqrt(HD)
    pieces = []
    for head in range(queries.shape[1] // HD):
        cols = slice(head * HD, (head + 1) * HD)
        scores = dot_turned(queries[:, cols], keys[:, cols]) * factor
        masked = jnp.where(allowed, scores, -jnp.inf)
        weights = jnp.exp(masked - jnp.max(masked, axis=1, keepdims=True))
        totals = jnp.sum(weights, axis=1, keepdims=True)
        pieces.append(dot(weights.astype(jnp.bfloat16), values[:, cols]) / totals)
    attended = jnp.concatenate(pieces, axis=1).astype(jnp.bfloat16)
    half = attended.shape[0] // 2
    send_ref[...] = dot_turned(attended[half:, :], out_whole[...]).astype(jnp.bfloat16)
    keep_ref[...] = dot_turned(attended[:half, :], out_whole[...])


def pass_kernel(keep_ref, got_ref, out_ref):
    rows = out_ref.shape[0]
    out_ref[...] = (keep_ref[rows:, :] + got_ref[rows:, :].astype(jnp.float32)).astype(jnp.bfloat16)


def layer_kernel(tokens_ref, keep_ref, core_ref, chip_ref, gains_ref, order_ref, *refs):
    (slices,) = refs
    rows, width = tokens_ref.shape
    summed = (
        tokens_ref[...].astype(jnp.float32)
        + keep_ref[0:rows, :]
        + core_ref[0:rows, :].astype(jnp.float32)
        + chip_ref[...].astype(jnp.float32)
    )
    merge_in = normalize(summed.astype(jnp.bfloat16), gains_ref[1:2, :])
    places = lax.broadcasted_iota(jnp.int32, (rows, rows), 1)
    picking = (order_ref[...] == places).astype(jnp.bfloat16)
    ordered = dot(picking, merge_in).astype(jnp.bfloat16)
    step, half = width // 8, width // 2
    for n in range(4):
        part = jnp.concatenate(
            [
                ordered[:, n * step : (n + 1) * step],
                ordered[:, half + n * step : half + (n + 1) * step],
            ],
            axis=1,
        )
        part = jnp.concatenate([part[: rows // 2, :], part[rows // 2 :, :]], axis=1)
        slices[n] = part
        slices[4 + n] = part


def merge_kernel(me_ref, at_ref, inputs, *refs):
    pieces, (keep_ref, *sends), total = refs[0:8], refs[8:12], refs[12]
    count, width = inputs.shape[1] // 2, inputs.shape[2] // 2
    z, y = me_ref[0] // 2, lax.rem(me_ref[0], 2)
    for number in range(4):
        position = z ^ number
        at = pl.multiple_of(lax.rem(position, 2) * count, 32)
        rows = inputs[:, pl.ds(at, count), :].reshape(8 * count, 2 * width)
        rows = jnp.where(position < 2, rows[:, :width], rows[:, width:])
        own, other = pieces[2 * number][...], pieces[2 * number + 1][...]
        block = jnp.concatenate(
            [jnp.where(y == 0, own, other), jnp.where(y == 0, other, own)], axis=0
        )
        found = dot(rows, block).reshape(total.shape)
        total[...] = found if number == 0 else total[...] + found
    for k in range(4):
        to = at_ref[0] ^ k
        share = jnp.concatenate([total[4 * y + to], total[4 * (1 - y) + to]], axis=0)
        if k == 0:
            keep_ref[...] = share
        else:
            sends[k - 1][...] = share.astype(jnp.bfloat16)


def pack_kernel(slots_ref, keep_ref, one_ref, two_ref, three_ref, out_ref):
    total = keep_ref[...]
    for got in (one_ref, two_ref, three_ref):
        total = total + got[...].astype(jnp.float32)
    shape = (out_ref.shape[0], total.shape[0])
    placing = (lax.broadcasted_iota(jnp.int32, shape, 0) == slots_ref[...]).astype(jnp.bfloat16)
    out_ref[...] = dot(placing, total.astype(jnp.bfloat16)).astype(jnp.bfloat16)


def by_permutes(
    tokens, qkv_weight, out_weight, merge_weight, ln_gains, segments, merge_rows, owners
):
    rows, width = tokens.shape
    count = rows // 4
    n_dp, n_fsdp = lax.axis_size("dp"), lax.axis_size("fsdp")
    me, at = lax.axis_index("dp"), lax.axis_index("fsdp")
    y = lax.rem(me, 2)
    me_cell, at_cell = me.reshape(1), at.reshape(1)
    bf16, f32 = jnp.bfloat16, jnp.float32
    shape = jax.ShapeDtypeStruct
    cols = qkv_weight.shape[2]
    group = n_fsdp * rows

    heads = jnp.concatenate([qkv_weight, out_weight.T[None]], axis=0)
    along_z = [swap(heads, "dp", 2), swap(heads, "dp", 4)]
    along_y = [swap(heads, "dp", 1)]
    along_z += [swap(along_z[1], "dp", 2)]
    along_y += [swap(block, "dp", 1) for block in along_z]

    marks = jnp.pad(segments.astype(bf16), ((0, 15), (0, width - rows)))
    marked = after(jnp.concatenate([tokens, marks], axis=0), along_z[0])
    along_x = swap(marked, "fsdp", 2)
    group_rows = [marked, along_x, swap(marked, "fsdp", 1), swap(along_x, "fsdp", 1)]
    (normed,) = call(norm_kernel, [shape((group, width), bf16)], [ln_gains, *group_rows])

    half = merge_weight.shape[1] // 2
    low, high = merge_weight[:, :half], merge_weight[:, half:]
    lower = y == 0
    mine = jnp.where(lower, low, high)
    theirs = swap(after(jnp.where(lower, high, low), along_z[0]), "dp", 1)
    held, held_other = after((mine, theirs), (along_z[2], *along_y[:3], *group_rows[2:]))
    merge_pieces = [mine, theirs, swap(held, "dp", 2), swap(held_other, "dp", 2)]
    merge_pieces += [swap(held, "dp", 4)]
    merge_pieces += [swap(after(held_other, merge_pieces[4]), "dp", 4)]
    merge_pieces += [swap(piece, "dp", 2) for piece in merge_pieces[4:6]]

    capacity = max(2, (2 * count + n_dp - 1) // n_dp)
    mine = owners[:, 0]
    other = swap(owners, "dp", 1)[:, 0]
    slots = []
    for number, targets in enumerate((mine, other)):
        start, rank = slot_numbers(targets, 2 * capacity)
        slots.append(start + rank + (y ^ number) * capacity)
    slots = jnp.concatenate(slots).reshape(1, 2 * count)
    order = merge_rows.reshape(count, 4).T.reshape(rows, 1)

    keep, send = call(
        attention_kernel,
        [shape((2 * rows, width), f32), shape((2 * rows, width), bf16)],
        [
            after(me_cell, merge_pieces[2:5]),
            normed,
            *group_rows,
            heads,
            *along_z,
            *along_y,
        ],
        [pltpu.VMEM((width, cols), bf16)] * 4,
        flops=8 * group * width * cols + 4 * group * group * cols,
        smem=1,
        exps=cols // HD * group * group,
    )
    from_core = swap(send, "fsdp", 1)
    (onward,) = call(pass_kernel, [shape((rows, width), bf16)], [keep, from_core])
    from_chip = swap(onward, "fsdp", 2)
    (slices,) = call(
        layer_kernel,
        [shape((8, rows // 2, width // 2), bf16)],
        [tokens, keep, from_core, after(from_chip, merge_pieces[5:7]), ln_gains, order],
        flops=2 * rows * rows * width,
    )
    both = 2 * n_fsdp
    inputs = lax.all_to_all(
        slices,
        ("dp", "fsdp"),
        split_axis=0,
        concat_axis=0,
        tiled=True,
        axis_index_groups=[
            list(range(i, i + both)) for i in range(0, n_dp * n_fsdp, both)
        ],
    )
    shares = call(
        merge_kernel,
        [shape((2 * count, half), f32)] + [shape((2 * count, half), bf16)] * 3,
        [me_cell, at_cell, inputs, *merge_pieces],
        [pltpu.VMEM((8, count, half), f32)],
        flops=2 * 8 * count * width * half,
        smem=2,
    )
    got = [swap(shares[k], "fsdp", k) for k in range(1, 4)]
    (packed,) = call(
        pack_kernel,
        [shape((n_dp * 2 * capacity, half), bf16)],
        [slots, shares[0], *got],
        flops=2 * n_dp * 2 * capacity * 2 * count * half,
    )
    arrived = lax.all_to_all(
        packed.reshape(n_dp, 2 * capacity, half), "dp", split_axis=0, concat_axis=0, tiled=True
    )
    arrived = arrived.reshape(n_dp // 2, 2, 2, capacity, half).transpose(0, 2, 3, 1, 4)
    return arrived.reshape(n_dp * capacity, 2 * half)


def solution(mesh):
    small = mesh.shape["dp"] == 8 and mesh.shape["fsdp"] == 4
    return jax.shard_map(
        by_permutes if small else by_gathers,
        mesh=mesh,
        in_specs=(
            P(("dp", "fsdp"), None),
            P(None, "dp", "fsdp"),
            P("fsdp", "dp"),
            P(("dp", "fsdp"), None),
            P(),
            P("dp", "fsdp"),
            P(("dp", "fsdp"), None),
            P(("dp", "fsdp"), None),
        ),
        out_specs=P(("dp", "fsdp"), None),
        check_vma=False,
    )
```

```python
import functools
import math

import jax
import jax.numpy as jnp
from jax import lax
from jax.experimental import pallas as pl
from jax.experimental.pallas import tpu as pltpu
from jax.sharding import PartitionSpec as P

HD = 80


epsilon = 1e-06


def normalize(values_in, gain_row):
    widened = values_in.astype(jnp.float32)
    centered = widened - jnp.mean(widened, axis=1, keepdims=True)
    variance = jnp.mean(centered * centered, axis=1, keepdims=True)
    return (centered * lax.rsqrt(variance + epsilon) * gain_row).astype(jnp.bfloat16)


def attend(queries, keys_all, values_all, seg_rows, seg_cols):
    factor = 1.0 / math.sqrt(HD)
    allowed = seg_rows[:, None] == seg_cols[None, :]
    pieces = []
    for head_index in range(queries.shape[1] // HD):
        first_col = head_index * HD
        last_col = first_col + HD
        scores = (
            lax.dot_general(
                queries[:, first_col:last_col],
                keys_all[:, first_col:last_col],
                (((1,), (1,)), ((), ())),
                preferred_element_type=jnp.float32,
            )
            * factor
        )
        masked = jnp.where(allowed, scores, -jnp.inf)
        highest = jnp.max(masked, axis=1, keepdims=True)
        weights = jnp.exp(masked - highest)
        totals = jnp.sum(weights, axis=1, keepdims=True)
        head_out = jnp.dot(
            weights.astype(jnp.bfloat16),
            values_all[:, first_col:last_col],
            preferred_element_type=jnp.float32,
        )
        pieces.append(head_out / totals)
    return jnp.concatenate(pieces, axis=1).astype(jnp.bfloat16)


def slot_numbers(targets, capacity):
    n = targets.shape[0]
    same = targets[:, None] == targets[None, :]
    before = jnp.arange(n)[None, :] < jnp.arange(n)[:, None]
    return targets * capacity, jnp.sum((same & before).astype(jnp.int32), axis=1)


def by_gathers(
    tokens, qkv_weight, out_weight, merge_weight, ln_gains, segments, merge_rows, owners
):
    n_dp = lax.axis_size("dp")
    qkv_mine = lax.all_gather(qkv_weight, "dp", axis=1, tiled=True)
    out_mine = lax.all_gather(out_weight, "dp", axis=1, tiled=True)
    n_fsdp = lax.axis_size("fsdp")
    normed = normalize(tokens, ln_gains[0])
    group_normed = lax.all_gather(normed, "fsdp", axis=0, tiled=True)
    group_segs = lax.all_gather(segments, "fsdp", axis=1, tiled=True)
    queries, keys_all, values_all = (
        jnp.dot(group_normed, qkv_mine[n], preferred_element_type=jnp.float32).astype(jnp.bfloat16)
        for n in range(3)
    )
    attended_mine = attend(queries, keys_all, values_all, group_segs[0], group_segs[0])
    attended_local = lax.all_to_all(attended_mine, "fsdp", split_axis=0, concat_axis=1, tiled=True)
    out_full = lax.all_gather(out_mine, "fsdp", axis=0, tiled=True)
    update = jnp.dot(attended_local, out_full, preferred_element_type=jnp.float32)
    layer_out = (tokens.astype(jnp.float32) + update).astype(jnp.bfloat16)
    merge_in = normalize(layer_out, ln_gains[1])
    merge_count = tokens.shape[0] // 4
    stacked = jnp.take(merge_in, merge_rows[0], axis=0).reshape(merge_count, 4 * merge_in.shape[1])
    slice_rows = merge_weight.shape[0]
    part_rows = lax.all_gather(merge_weight, "dp", axis=0, tiled=True)
    blocks = stacked.reshape(merge_count, n_dp, n_fsdp * slice_rows)
    received = lax.all_to_all(blocks, "fsdp", split_axis=2, concat_axis=0, tiled=True)
    gathered_inputs = received.reshape(n_fsdp * merge_count, n_dp * slice_rows)
    merged = lax.psum_scatter(
        jnp.dot(gathered_inputs, part_rows, preferred_element_type=jnp.float32).astype(
            jnp.bfloat16
        ),
        "fsdp",
        scatter_dimension=0,
        tiled=True,
    )
    capacity = max(2, (2 * merge_count + n_dp - 1) // n_dp)
    first, rank = slot_numbers(owners[:, 0], capacity)
    placing = (
        jnp.arange(n_dp * capacity, dtype=jnp.int32)[:, None] == (first + rank)[None, :]
    ).astype(jnp.bfloat16)
    packed = jnp.dot(placing, merged, preferred_element_type=jnp.float32).astype(jnp.bfloat16)
    packed = packed.reshape(n_dp, capacity, merged.shape[1])
    arrived = lax.all_to_all(packed, "dp", split_axis=0, concat_axis=0, tiled=True)
    return arrived.reshape(n_dp * capacity, merged.shape[1])


def swap(value, axis, k):
    return lax.ppermute(value, axis, [(i, i ^ k) for i in range(lax.axis_size(axis))])


def after(value, other):
    return lax.optimization_barrier((value, other))[0]


ORDER = (0, 2, 4, 6, 1, 3, 5, 7)


def dot(a, b):
    return jnp.dot(a, b, preferred_element_type=jnp.float32)


def dot_turned(a, b):
    return lax.dot_general(a, b, (((1,), (1,)), ((), ())), preferred_element_type=jnp.float32)


def call(kernel, outs, operands, scratch=(), flops=0, smem=0, exps=0):
    moved = sum(math.prod(x.shape) * x.dtype.itemsize for x in (*operands, *outs))
    specs = [pl.BlockSpec(memory_space=pltpu.SMEM)] * smem
    specs += [pl.BlockSpec(memory_space=pltpu.VMEM)] * (len(operands) - smem)
    return pl.pallas_call(
        kernel,
        out_shape=tuple(outs),
        in_specs=specs,
        out_specs=tuple(pl.BlockSpec(memory_space=pltpu.VMEM) for _ in outs),
        scratch_shapes=list(scratch),
        compiler_params=pltpu.CompilerParams(vmem_limit_bytes=16 * 1024 * 1024),
        cost_estimate=pl.CostEstimate(
            flops=flops, bytes_accessed=moved, transcendentals=exps
        ),
    )(*operands)


def norm_kernel(gains_ref, *refs):
    tokens, out_ref = refs[0:4], refs[4]
    rows = tokens[0].shape[0] - 16
    for n in range(4):
        out_ref[n * rows : (n + 1) * rows, :] = normalize(tokens[n][0:rows, :], gains_ref[0:1, :])


def lay_out(me, blocks, part, whole):
    step = blocks[0].shape[1]
    for number, block in zip(ORDER, blocks):
        start = pl.multiple_of((me ^ number) * step, 32)
        whole[pl.ds(start, step), :] = block[part]


def attention_kernel(me_ref, rows_ref, *refs):
    marks, blocks = refs[0:4], refs[4:12]
    keep_ref, send_ref, q_whole, k_whole, v_whole, out_whole = refs[12:]
    lay_out(me_ref[0], blocks, 0, q_whole)
    lay_out(me_ref[0], blocks, 1, k_whole)
    lay_out(me_ref[0], blocks, 2, v_whole)
    lay_out(me_ref[0], blocks, 3, out_whole)
    queries = dot(rows_ref[...], q_whole[...]).astype(jnp.bfloat16)
    keys = dot(rows_ref[...], k_whole[...]).astype(jnp.bfloat16)
    values = dot(rows_ref[...], v_whole[...]).astype(jnp.bfloat16)
    rows = marks[0].shape[0] - 16
    in_row = [t[rows : rows + 16, 0:rows].astype(jnp.float32)[0:1, :] for t in marks]
    in_col = [jnp.broadcast_to(s, (rows, rows)).T[:, 0:1] for s in in_row]
    allowed = jnp.concatenate(in_col, axis=0) == jnp.concatenate(in_row, axis=1)
    factor = 1.0 / math.sqrt(HD)
    pieces = []
    for head in range(queries.shape[1] // HD):
        cols = slice(head * HD, (head + 1) * HD)
        scores = dot_turned(queries[:, cols], keys[:, cols]) * factor
        masked = jnp.where(allowed, scores, -jnp.inf)
        weights = jnp.exp(masked - jnp.max(masked, axis=1, keepdims=True))
        totals = jnp.sum(weights, axis=1, keepdims=True)
        pieces.append(dot(weights.astype(jnp.bfloat16), values[:, cols]) / totals)
    attended = jnp.concatenate(pieces, axis=1).astype(jnp.bfloat16)
    half = attended.shape[0] // 2
    send_ref[...] = dot_turned(attended[half:, :], out_whole[...]).astype(jnp.bfloat16)
    keep_ref[...] = dot_turned(attended[:half, :], out_whole[...])


def pass_kernel(keep_ref, got_ref, out_ref):
    rows = out_ref.shape[0]
    out_ref[...] = (keep_ref[rows:, :] + got_ref[rows:, :].astype(jnp.float32)).astype(jnp.bfloat16)


def layer_kernel(tokens_ref, keep_ref, core_ref, chip_ref, gains_ref, order_ref, *refs):
    (slices,) = refs
    rows, width = tokens_ref.shape
    summed = (
        tokens_ref[...].astype(jnp.float32)
        + keep_ref[0:rows, :]
        + core_ref[0:rows, :].astype(jnp.float32)
        + chip_ref[...].astype(jnp.float32)
    )
    merge_in = normalize(summed.astype(jnp.bfloat16), gains_ref[1:2, :])
    places = lax.broadcasted_iota(jnp.int32, (rows, rows), 1)
    picking = (order_ref[...] == places).astype(jnp.bfloat16)
    ordered = dot(picking, merge_in).astype(jnp.bfloat16)
    step, half = width // 8, width // 2
    for n in range(4):
        part = jnp.concatenate(
            [
                ordered[:, n * step : (n + 1) * step],
                ordered[:, half + n * step : half + (n + 1) * step],
            ],
            axis=1,
        )
        part = jnp.concatenate([part[: rows // 2, :], part[rows // 2 :, :]], axis=1)
        slices[n] = part
        slices[4 + n] = part


def merge_kernel(me_ref, at_ref, inputs, *refs):
    pieces, (keep_ref, *sends), total = refs[0:8], refs[8:12], refs[12]
    count, width = inputs.shape[1] // 2, inputs.shape[2] // 2
    z, y = me_ref[0] // 2, lax.rem(me_ref[0], 2)
    for number in range(4):
        position = z ^ number
        at = pl.multiple_of(lax.rem(position, 2) * count, 32)
        rows = inputs[:, pl.ds(at, count), :].reshape(8 * count, 2 * width)
        rows = jnp.where(position < 2, rows[:, :width], rows[:, width:])
        own, other = pieces[2 * number][...], pieces[2 * number + 1][...]
        block = jnp.concatenate(
            [jnp.where(y == 0, own, other), jnp.where(y == 0, other, own)], axis=0
        )
        found = dot(rows, block).reshape(total.shape)
        total[...] = found if number == 0 else total[...] + found
    for k in range(4):
        to = at_ref[0] ^ k
        share = jnp.concatenate([total[4 * y + to], total[4 * (1 - y) + to]], axis=0)
        if k == 0:
            keep_ref[...] = share
        else:
            sends[k - 1][...] = share.astype(jnp.bfloat16)


def pack_kernel(slots_ref, keep_ref, one_ref, two_ref, three_ref, out_ref):
    total = keep_ref[...]
    for got in (one_ref, two_ref, three_ref):
        total = total + got[...].astype(jnp.float32)
    shape = (out_ref.shape[0], total.shape[0])
    placing = (lax.broadcasted_iota(jnp.int32, shape, 0) == slots_ref[...]).astype(jnp.bfloat16)
    out_ref[...] = dot(placing, total.astype(jnp.bfloat16)).astype(jnp.bfloat16)


def by_permutes(
    tokens, qkv_weight, out_weight, merge_weight, ln_gains, segments, merge_rows, owners
):
    rows, width = tokens.shape
    count = rows // 4
    n_dp, n_fsdp = lax.axis_size("dp"), lax.axis_size("fsdp")
    me, at = lax.axis_index("dp"), lax.axis_index("fsdp")
    y = lax.rem(me, 2)
    me_cell, at_cell = me.reshape(1), at.reshape(1)
    bf16, f32 = jnp.bfloat16, jnp.float32
    shape = jax.ShapeDtypeStruct
    cols = qkv_weight.shape[2]
    group = n_fsdp * rows

    heads = jnp.concatenate([qkv_weight, out_weight.T[None]], axis=0)
    along_z, along_y = [swap(heads, "dp", 2)], [swap(heads, "dp", 1)]
    along_z += [swap(after(heads, (along_z[0], along_y[0])), "dp", 4)]
    along_y += [swap(along_z[0], "dp", 1)]
    half = merge_weight.shape[1] // 2
    low, high = merge_weight[:, :half], merge_weight[:, half:]
    lower = y == 0
    mine = jnp.where(lower, low, high)
    theirs = swap(after(jnp.where(lower, high, low), along_z[0]), "dp", 1)
    along_z += [swap(after(along_z[1], (along_y[1], theirs)), "dp", 2)]
    along_y += [swap(block, "dp", 1) for block in along_z[1:]]

    marks = jnp.pad(segments.astype(bf16), ((0, 15), (0, width - rows)))
    marked = after(jnp.concatenate([tokens, marks], axis=0), along_z[0])
    along_x = swap(marked, "fsdp", 2)
    group_rows = [marked, along_x, swap(marked, "fsdp", 1), swap(along_x, "fsdp", 1)]
    (normed,) = call(norm_kernel, [shape((group, width), bf16)], [ln_gains, *group_rows])

    far = swap(after(mine, (along_z[2], *group_rows[2:])), "dp", 4)
    held, held_other = after((mine, theirs), far)
    merge_pieces = [mine, theirs, swap(held, "dp", 2), swap(held_other, "dp", 2)]
    merge_pieces += [far, swap(held_other, "dp", 4)]
    merge_pieces += [swap(piece, "dp", 2) for piece in merge_pieces[4:6]]

    capacity = max(2, (2 * count + n_dp - 1) // n_dp)
    mine = owners[:, 0]
    other = swap(owners, "dp", 1)[:, 0]
    slots = []
    for number, targets in enumerate((mine, other)):
        start, rank = slot_numbers(targets, 2 * capacity)
        slots.append(start + rank + (y ^ number) * capacity)
    slots = jnp.concatenate(slots).reshape(1, 2 * count)
    order = merge_rows.reshape(count, 4).T.reshape(rows, 1)

    keep, send = call(
        attention_kernel,
        [shape((2 * rows, width), f32), shape((2 * rows, width), bf16)],
        [
            after(me_cell, far),
            normed,
            *group_rows,
            heads,
            *along_z,
            *along_y,
        ],
        [pltpu.VMEM((width, cols), bf16)] * 4,
        flops=8 * group * width * cols + 4 * group * group * cols,
        smem=1,
        exps=cols // HD * group * group,
    )
    from_core = swap(send, "fsdp", 1)
    (onward,) = call(pass_kernel, [shape((rows, width), bf16)], [keep, from_core])
    from_chip = swap(onward, "fsdp", 2)
    (slices,) = call(
        layer_kernel,
        [shape((8, rows // 2, width // 2), bf16)],
        [tokens, keep, from_core, after(from_chip, merge_pieces[5:7]), ln_gains, order],
        flops=2 * rows * rows * width,
    )
    both = 2 * n_fsdp
    inputs = lax.all_to_all(
        slices,
        ("dp", "fsdp"),
        split_axis=0,
        concat_axis=0,
        tiled=True,
        axis_index_groups=[
            list(range(i, i + both)) for i in range(0, n_dp * n_fsdp, both)
        ],
    )
    shares = call(
        merge_kernel,
        [shape((2 * count, half), f32)] + [shape((2 * count, half), bf16)] * 3,
        [me_cell, at_cell, inputs, *merge_pieces],
        [pltpu.VMEM((8, count, half), f32)],
        flops=2 * 8 * count * width * half,
        smem=2,
    )
    got = [swap(shares[k], "fsdp", k) for k in range(1, 4)]
    (packed,) = call(
        pack_kernel,
        [shape((n_dp * 2 * capacity, half), bf16)],
        [slots, shares[0], *got],
        flops=2 * n_dp * 2 * capacity * 2 * count * half,
    )
    arrived = lax.all_to_all(
        packed.reshape(n_dp, 2 * capacity, half), "dp", split_axis=0, concat_axis=0, tiled=True
    )
    arrived = arrived.reshape(n_dp // 2, 2, 2, capacity, half).transpose(0, 2, 3, 1, 4)
    return arrived.reshape(n_dp * capacity, 2 * half)


def solution(mesh):
    small = mesh.shape["dp"] == 8 and mesh.shape["fsdp"] == 4
    return jax.shard_map(
        by_permutes if small else by_gathers,
        mesh=mesh,
        in_specs=(
            P(("dp", "fsdp"), None),
            P(None, "dp", "fsdp"),
            P("fsdp", "dp"),
            P(("dp", "fsdp"), None),
            P(),
            P("dp", "fsdp"),
            P(("dp", "fsdp"), None),
            P(("dp", "fsdp"), None),
        ),
        out_specs=P(("dp", "fsdp"), None),
        check_vma=False,
    )
```

```python
import functools
import math

import jax
import jax.numpy as jnp
from jax import lax
from jax.experimental import pallas as pl
from jax.experimental.pallas import tpu as pltpu
from jax.sharding import PartitionSpec as P

HD = 80


epsilon = 1e-06


def normalize(values_in, gain_row):
    widened = values_in.astype(jnp.float32)
    centered = widened - jnp.mean(widened, axis=1, keepdims=True)
    variance = jnp.mean(centered * centered, axis=1, keepdims=True)
    return (centered * lax.rsqrt(variance + epsilon) * gain_row).astype(jnp.bfloat16)


def attend(queries, keys_all, values_all, seg_rows, seg_cols):
    factor = 1.0 / math.sqrt(HD)
    allowed = seg_rows[:, None] == seg_cols[None, :]
    pieces = []
    for head_index in range(queries.shape[1] // HD):
        first_col = head_index * HD
        last_col = first_col + HD
        scores = (
            lax.dot_general(
                queries[:, first_col:last_col],
                keys_all[:, first_col:last_col],
                (((1,), (1,)), ((), ())),
                preferred_element_type=jnp.float32,
            )
            * factor
        )
        masked = jnp.where(allowed, scores, -jnp.inf)
        highest = jnp.max(masked, axis=1, keepdims=True)
        weights = jnp.exp(masked - highest)
        totals = jnp.sum(weights, axis=1, keepdims=True)
        head_out = jnp.dot(
            weights.astype(jnp.bfloat16),
            values_all[:, first_col:last_col],
            preferred_element_type=jnp.float32,
        )
        pieces.append(head_out / totals)
    return jnp.concatenate(pieces, axis=1).astype(jnp.bfloat16)


def slot_numbers(targets, capacity):
    n = targets.shape[0]
    same = targets[:, None] == targets[None, :]
    before = jnp.arange(n)[None, :] < jnp.arange(n)[:, None]
    return targets * capacity, jnp.sum((same & before).astype(jnp.int32), axis=1)


def by_gathers(
    tokens, qkv_weight, out_weight, merge_weight, ln_gains, segments, merge_rows, owners
):
    n_dp = lax.axis_size("dp")
    qkv_mine = lax.all_gather(qkv_weight, "dp", axis=1, tiled=True)
    out_mine = lax.all_gather(out_weight, "dp", axis=1, tiled=True)
    n_fsdp = lax.axis_size("fsdp")
    normed = normalize(tokens, ln_gains[0])
    group_normed = lax.all_gather(normed, "fsdp", axis=0, tiled=True)
    group_segs = lax.all_gather(segments, "fsdp", axis=1, tiled=True)
    queries, keys_all, values_all = (
        jnp.dot(group_normed, qkv_mine[n], preferred_element_type=jnp.float32).astype(jnp.bfloat16)
        for n in range(3)
    )
    attended_mine = attend(queries, keys_all, values_all, group_segs[0], group_segs[0])
    attended_local = lax.all_to_all(attended_mine, "fsdp", split_axis=0, concat_axis=1, tiled=True)
    out_full = lax.all_gather(out_mine, "fsdp", axis=0, tiled=True)
    update = jnp.dot(attended_local, out_full, preferred_element_type=jnp.float32)
    layer_out = (tokens.astype(jnp.float32) + update).astype(jnp.bfloat16)
    merge_in = normalize(layer_out, ln_gains[1])
    merge_count = tokens.shape[0] // 4
    stacked = jnp.take(merge_in, merge_rows[0], axis=0).reshape(merge_count, 4 * merge_in.shape[1])
    slice_rows = merge_weight.shape[0]
    part_rows = lax.all_gather(merge_weight, "dp", axis=0, tiled=True)
    blocks = stacked.reshape(merge_count, n_dp, n_fsdp * slice_rows)
    received = lax.all_to_all(blocks, "fsdp", split_axis=2, concat_axis=0, tiled=True)
    gathered_inputs = received.reshape(n_fsdp * merge_count, n_dp * slice_rows)
    merged = lax.psum_scatter(
        jnp.dot(gathered_inputs, part_rows, preferred_element_type=jnp.float32).astype(
            jnp.bfloat16
        ),
        "fsdp",
        scatter_dimension=0,
        tiled=True,
    )
    capacity = max(2, (2 * merge_count + n_dp - 1) // n_dp)
    first, rank = slot_numbers(owners[:, 0], capacity)
    placing = (
        jnp.arange(n_dp * capacity, dtype=jnp.int32)[:, None] == (first + rank)[None, :]
    ).astype(jnp.bfloat16)
    packed = jnp.dot(placing, merged, preferred_element_type=jnp.float32).astype(jnp.bfloat16)
    packed = packed.reshape(n_dp, capacity, merged.shape[1])
    arrived = lax.all_to_all(packed, "dp", split_axis=0, concat_axis=0, tiled=True)
    return arrived.reshape(n_dp * capacity, merged.shape[1])


def swap(value, axis, k):
    return lax.ppermute(value, axis, [(i, i ^ k) for i in range(lax.axis_size(axis))])


def after(value, other):
    return lax.optimization_barrier((value, other))[0]


ORDER = (0, 2, 4, 6, 1, 3, 5, 7)


def dot(a, b):
    return jnp.dot(a, b, preferred_element_type=jnp.float32)


def dot_turned(a, b):
    return lax.dot_general(a, b, (((1,), (1,)), ((), ())), preferred_element_type=jnp.float32)


def call(kernel, outs, operands, scratch=(), flops=0, smem=0, exps=0):
    moved = sum(math.prod(x.shape) * x.dtype.itemsize for x in (*operands, *outs))
    specs = [pl.BlockSpec(memory_space=pltpu.SMEM)] * smem
    specs += [pl.BlockSpec(memory_space=pltpu.VMEM)] * (len(operands) - smem)
    return pl.pallas_call(
        kernel,
        out_shape=tuple(outs),
        in_specs=specs,
        out_specs=tuple(pl.BlockSpec(memory_space=pltpu.VMEM) for _ in outs),
        scratch_shapes=list(scratch),
        compiler_params=pltpu.CompilerParams(vmem_limit_bytes=16 * 1024 * 1024),
        cost_estimate=pl.CostEstimate(
            flops=flops, bytes_accessed=moved, transcendentals=exps
        ),
    )(*operands)


def norm_kernel(gains_ref, *refs):
    tokens, out_ref = refs[0:4], refs[4]
    rows = tokens[0].shape[0] - 16
    for n in range(4):
        out_ref[n * rows : (n + 1) * rows, :] = normalize(tokens[n][0:rows, :], gains_ref[0:1, :])


def lay_out(me, blocks, part, whole):
    step = blocks[0].shape[1]
    for number, block in zip(ORDER, blocks):
        start = pl.multiple_of((me ^ number) * step, 32)
        whole[pl.ds(start, step), :] = block[part if block.shape[0] == 4 else part % 2]


def score_kernel(me_ref, rows_ref, *refs):
    marks, blocks = refs[0:4], refs[4:12]
    weights_ref, totals_ref, q_whole, k_whole = refs[12:]
    lay_out(me_ref[0], blocks, 0, q_whole)
    lay_out(me_ref[0], blocks, 1, k_whole)
    queries = dot(rows_ref[...], q_whole[...]).astype(jnp.bfloat16)
    keys = dot(rows_ref[...], k_whole[...]).astype(jnp.bfloat16)
    rows = marks[0].shape[0] - 16
    in_row = [t[rows : rows + 16, 0:rows].astype(jnp.float32)[0:1, :] for t in marks]
    in_col = [jnp.broadcast_to(s, (rows, rows)).T[:, 0:1] for s in in_row]
    allowed = jnp.concatenate(in_col, axis=0) == jnp.concatenate(in_row, axis=1)
    factor = 1.0 / math.sqrt(HD)
    for head in range(queries.shape[1] // HD):
        cols = slice(head * HD, (head + 1) * HD)
        scores = dot_turned(queries[:, cols], keys[:, cols]) * factor
        masked = jnp.where(allowed, scores, -jnp.inf)
        weights = jnp.exp(masked - jnp.max(masked, axis=1, keepdims=True))
        weights_ref[head] = weights.astype(jnp.bfloat16)
        totals_ref[head] = jnp.sum(weights, axis=1, keepdims=True)


def value_kernel(me_ref, rows_ref, weights_ref, totals_ref, *refs):
    blocks = refs[0:8]
    keep_ref, send_ref, v_whole, out_whole = refs[8:]
    lay_out(me_ref[0], blocks, 2, v_whole)
    lay_out(me_ref[0], blocks, 3, out_whole)
    values = dot(rows_ref[...], v_whole[...]).astype(jnp.bfloat16)
    pieces = []
    for head in range(values.shape[1] // HD):
        found = dot(weights_ref[head], values[:, head * HD : (head + 1) * HD])
        pieces.append(found / totals_ref[head])
    attended = jnp.concatenate(pieces, axis=1).astype(jnp.bfloat16)
    half = attended.shape[0] // 2
    send_ref[...] = dot_turned(attended[half:, :], out_whole[...]).astype(jnp.bfloat16)
    keep_ref[...] = dot_turned(attended[:half, :], out_whole[...])


def pass_kernel(keep_ref, got_ref, out_ref):
    rows = out_ref.shape[0]
    out_ref[...] = (keep_ref[rows:, :] + got_ref[rows:, :].astype(jnp.float32)).astype(jnp.bfloat16)


def layer_kernel(tokens_ref, keep_ref, core_ref, chip_ref, gains_ref, order_ref, *refs):
    (slices,) = refs
    rows, width = tokens_ref.shape
    summed = (
        tokens_ref[...].astype(jnp.float32)
        + keep_ref[0:rows, :]
        + core_ref[0:rows, :].astype(jnp.float32)
        + chip_ref[...].astype(jnp.float32)
    )
    merge_in = normalize(summed.astype(jnp.bfloat16), gains_ref[1:2, :])
    places = lax.broadcasted_iota(jnp.int32, (rows, rows), 1)
    picking = (order_ref[...] == places).astype(jnp.bfloat16)
    ordered = dot(picking, merge_in).astype(jnp.bfloat16)
    step, half = width // 8, width // 2
    for n in range(4):
        part = jnp.concatenate(
            [
                ordered[:, n * step : (n + 1) * step],
                ordered[:, half + n * step : half + (n + 1) * step],
            ],
            axis=1,
        )
        part = jnp.concatenate([part[: rows // 2, :], part[rows // 2 :, :]], axis=1)
        slices[n] = part
        slices[4 + n] = part


def merge_kernel(me_ref, at_ref, inputs, *refs):
    pieces, (keep_ref, *sends), total = refs[0:8], refs[8:12], refs[12]
    count, width = inputs.shape[1] // 2, inputs.shape[2] // 2
    z, y = me_ref[0] // 2, lax.rem(me_ref[0], 2)
    for number in range(4):
        position = z ^ number
        at = pl.multiple_of(lax.rem(position, 2) * count, 32)
        rows = inputs[:, pl.ds(at, count), :].reshape(8 * count, 2 * width)
        rows = jnp.where(position < 2, rows[:, :width], rows[:, width:])
        own, other = pieces[2 * number][...], pieces[2 * number + 1][...]
        block = jnp.concatenate(
            [jnp.where(y == 0, own, other), jnp.where(y == 0, other, own)], axis=0
        )
        found = dot(rows, block).reshape(total.shape)
        total[...] = found if number == 0 else total[...] + found
    for k in range(4):
        to = at_ref[0] ^ k
        share = jnp.concatenate([total[4 * y + to], total[4 * (1 - y) + to]], axis=0)
        if k == 0:
            keep_ref[...] = share
        else:
            sends[k - 1][...] = share.astype(jnp.bfloat16)


def pack_kernel(slots_ref, keep_ref, one_ref, two_ref, three_ref, out_ref):
    total = keep_ref[...]
    for got in (one_ref, two_ref, three_ref):
        total = total + got[...].astype(jnp.float32)
    shape = (out_ref.shape[0], total.shape[0])
    placing = (lax.broadcasted_iota(jnp.int32, shape, 0) == slots_ref[...]).astype(jnp.bfloat16)
    out_ref[...] = dot(placing, total.astype(jnp.bfloat16)).astype(jnp.bfloat16)


def by_permutes(
    tokens, qkv_weight, out_weight, merge_weight, ln_gains, segments, merge_rows, owners
):
    rows, width = tokens.shape
    count = rows // 4
    n_dp, n_fsdp = lax.axis_size("dp"), lax.axis_size("fsdp")
    me, at = lax.axis_index("dp"), lax.axis_index("fsdp")
    y = lax.rem(me, 2)
    me_cell, at_cell = me.reshape(1), at.reshape(1)
    bf16, f32 = jnp.bfloat16, jnp.float32
    shape = jax.ShapeDtypeStruct
    cols = qkv_weight.shape[2]
    group = n_fsdp * rows

    heads = jnp.concatenate([qkv_weight, out_weight.T[None]], axis=0)
    near, beside = swap(heads, "dp", 2), swap(heads, "dp", 1)
    first, second = heads[0:2], heads[2:4]
    first_far = swap(first, "dp", 4)
    second_far = swap(after(second, first_far), "dp", 4)
    first_last = swap(first_far, "dp", 2)
    second_last = swap(second_far, "dp", 2)
    near_y = swap(near, "dp", 1)
    blocks = [
        [heads, near, far, last, beside, near_y, swap(far, "dp", 1), swap(last, "dp", 1)]
        for far, last in ((first_far, first_last), (second_far, second_last))
    ]

    marks = jnp.pad(segments.astype(bf16), ((0, 15), (0, width - rows)))
    marked = after(jnp.concatenate([tokens, marks], axis=0), (near, beside))
    along_x = swap(marked, "fsdp", 2)
    group_rows = [marked, along_x, swap(marked, "fsdp", 1), swap(along_x, "fsdp", 1)]
    (normed,) = call(norm_kernel, [shape((group, width), bf16)], [ln_gains, *group_rows])

    half = merge_weight.shape[1] // 2
    low, high = merge_weight[:, :half], merge_weight[:, half:]
    lower = y == 0
    mine = jnp.where(lower, low, high)
    held = after(mine, (second_last, blocks[1][6], *blocks[0][5:8], *group_rows[2:]))
    merge_near, merge_far = swap(held, "dp", 2), swap(held, "dp", 4)
    theirs = swap(after(jnp.where(lower, high, low), blocks[0][7]), "dp", 1)
    theirs_far = swap(after(theirs, merge_far), "dp", 4)
    merge_pieces = [mine, theirs, merge_near, swap(after(theirs, merge_far), "dp", 2)]
    merge_pieces += [merge_far, theirs_far, swap(merge_far, "dp", 2), swap(theirs_far, "dp", 2)]

    capacity = max(2, (2 * count + n_dp - 1) // n_dp)
    mine = owners[:, 0]
    other = swap(owners, "dp", 1)[:, 0]
    slots = []
    for number, targets in enumerate((mine, other)):
        start, rank = slot_numbers(targets, 2 * capacity)
        slots.append(start + rank + (y ^ number) * capacity)
    slots = jnp.concatenate(slots).reshape(1, 2 * count)
    order = merge_rows.reshape(count, 4).T.reshape(rows, 1)

    found = cols // HD
    weights, totals = call(
        score_kernel,
        [shape((found, group, group), bf16), shape((found, group, 1), f32)],
        [me_cell, normed, *group_rows, *blocks[0]],
        [pltpu.VMEM((width, cols), bf16)] * 2,
        flops=4 * group * width * cols + 2 * group * group * cols,
        smem=1,
        exps=found * group * group,
    )
    keep, send = call(
        value_kernel,
        [shape((2 * rows, width), f32), shape((2 * rows, width), bf16)],
        [after(me_cell, merge_near), normed, weights, totals, *blocks[1]],
        [pltpu.VMEM((width, cols), bf16)] * 2,
        flops=4 * group * width * cols + 2 * group * group * cols,
        smem=1,
    )
    from_core = swap(send, "fsdp", 1)
    (onward,) = call(pass_kernel, [shape((rows, width), bf16)], [keep, from_core])
    from_chip = swap(onward, "fsdp", 2)
    (slices,) = call(
        layer_kernel,
        [shape((8, rows // 2, width // 2), bf16)],
        [tokens, keep, from_core, after(from_chip, merge_pieces[5:7]), ln_gains, order],
        flops=2 * rows * rows * width,
    )
    both = 2 * n_fsdp
    inputs = lax.all_to_all(
        slices,
        ("dp", "fsdp"),
        split_axis=0,
        concat_axis=0,
        tiled=True,
        axis_index_groups=[
            list(range(i, i + both)) for i in range(0, n_dp * n_fsdp, both)
        ],
    )
    shares = call(
        merge_kernel,
        [shape((2 * count, half), f32)] + [shape((2 * count, half), bf16)] * 3,
        [me_cell, at_cell, inputs, *merge_pieces],
        [pltpu.VMEM((8, count, half), f32)],
        flops=2 * 8 * count * width * half,
        smem=2,
    )
    got = [swap(shares[k], "fsdp", k) for k in range(1, 4)]
    (packed,) = call(
        pack_kernel,
        [shape((n_dp * 2 * capacity, half), bf16)],
        [slots, shares[0], *got],
        flops=2 * n_dp * 2 * capacity * 2 * count * half,
    )
    arrived = lax.all_to_all(
        packed.reshape(n_dp, 2 * capacity, half), "dp", split_axis=0, concat_axis=0, tiled=True
    )
    arrived = arrived.reshape(n_dp // 2, 2, 2, capacity, half).transpose(0, 2, 3, 1, 4)
    return arrived.reshape(n_dp * capacity, 2 * half)


def solution(mesh):
    small = mesh.shape["dp"] == 8 and mesh.shape["fsdp"] == 4
    return jax.shard_map(
        by_permutes if small else by_gathers,
        mesh=mesh,
        in_specs=(
            P(("dp", "fsdp"), None),
            P(None, "dp", "fsdp"),
            P("fsdp", "dp"),
            P(("dp", "fsdp"), None),
            P(),
            P("dp", "fsdp"),
            P(("dp", "fsdp"), None),
            P(("dp", "fsdp"), None),
        ),
        out_specs=P(("dp", "fsdp"), None),
        check_vma=False,
    )
```

```python
import functools
import math

import jax
import jax.numpy as jnp
from jax import lax
from jax.experimental import pallas as pl
from jax.experimental.pallas import tpu as pltpu
from jax.sharding import PartitionSpec as P

HD = 80


epsilon = 1e-06


def normalize(values_in, gain_row):
    widened = values_in.astype(jnp.float32)
    centered = widened - jnp.mean(widened, axis=1, keepdims=True)
    variance = jnp.mean(centered * centered, axis=1, keepdims=True)
    return (centered * lax.rsqrt(variance + epsilon) * gain_row).astype(jnp.bfloat16)


def attend(queries, keys_all, values_all, seg_rows, seg_cols):
    factor = 1.0 / math.sqrt(HD)
    allowed = seg_rows[:, None] == seg_cols[None, :]
    pieces = []
    for head_index in range(queries.shape[1] // HD):
        first_col = head_index * HD
        last_col = first_col + HD
        scores = (
            lax.dot_general(
                queries[:, first_col:last_col],
                keys_all[:, first_col:last_col],
                (((1,), (1,)), ((), ())),
                preferred_element_type=jnp.float32,
            )
            * factor
        )
        masked = jnp.where(allowed, scores, -jnp.inf)
        highest = jnp.max(masked, axis=1, keepdims=True)
        weights = jnp.exp(masked - highest)
        totals = jnp.sum(weights, axis=1, keepdims=True)
        head_out = jnp.dot(
            weights.astype(jnp.bfloat16),
            values_all[:, first_col:last_col],
            preferred_element_type=jnp.float32,
        )
        pieces.append(head_out / totals)
    return jnp.concatenate(pieces, axis=1).astype(jnp.bfloat16)


def slot_numbers(targets, capacity):
    n = targets.shape[0]
    same = targets[:, None] == targets[None, :]
    before = jnp.arange(n)[None, :] < jnp.arange(n)[:, None]
    return targets * capacity, jnp.sum((same & before).astype(jnp.int32), axis=1)


def by_gathers(
    tokens, qkv_weight, out_weight, merge_weight, ln_gains, segments, merge_rows, owners
):
    n_dp = lax.axis_size("dp")
    qkv_mine = lax.all_gather(qkv_weight, "dp", axis=1, tiled=True)
    out_mine = lax.all_gather(out_weight, "dp", axis=1, tiled=True)
    n_fsdp = lax.axis_size("fsdp")
    normed = normalize(tokens, ln_gains[0])
    group_normed = lax.all_gather(normed, "fsdp", axis=0, tiled=True)
    group_segs = lax.all_gather(segments, "fsdp", axis=1, tiled=True)
    queries, keys_all, values_all = (
        jnp.dot(group_normed, qkv_mine[n], preferred_element_type=jnp.float32).astype(jnp.bfloat16)
        for n in range(3)
    )
    attended_mine = attend(queries, keys_all, values_all, group_segs[0], group_segs[0])
    attended_local = lax.all_to_all(attended_mine, "fsdp", split_axis=0, concat_axis=1, tiled=True)
    out_full = lax.all_gather(out_mine, "fsdp", axis=0, tiled=True)
    update = jnp.dot(attended_local, out_full, preferred_element_type=jnp.float32)
    layer_out = (tokens.astype(jnp.float32) + update).astype(jnp.bfloat16)
    merge_in = normalize(layer_out, ln_gains[1])
    merge_count = tokens.shape[0] // 4
    stacked = jnp.take(merge_in, merge_rows[0], axis=0).reshape(merge_count, 4 * merge_in.shape[1])
    slice_rows = merge_weight.shape[0]
    part_rows = lax.all_gather(merge_weight, "dp", axis=0, tiled=True)
    blocks = stacked.reshape(merge_count, n_dp, n_fsdp * slice_rows)
    received = lax.all_to_all(blocks, "fsdp", split_axis=2, concat_axis=0, tiled=True)
    gathered_inputs = received.reshape(n_fsdp * merge_count, n_dp * slice_rows)
    merged = lax.psum_scatter(
        jnp.dot(gathered_inputs, part_rows, preferred_element_type=jnp.float32).astype(
            jnp.bfloat16
        ),
        "fsdp",
        scatter_dimension=0,
        tiled=True,
    )
    capacity = max(2, (2 * merge_count + n_dp - 1) // n_dp)
    first, rank = slot_numbers(owners[:, 0], capacity)
    placing = (
        jnp.arange(n_dp * capacity, dtype=jnp.int32)[:, None] == (first + rank)[None, :]
    ).astype(jnp.bfloat16)
    packed = jnp.dot(placing, merged, preferred_element_type=jnp.float32).astype(jnp.bfloat16)
    packed = packed.reshape(n_dp, capacity, merged.shape[1])
    arrived = lax.all_to_all(packed, "dp", split_axis=0, concat_axis=0, tiled=True)
    return arrived.reshape(n_dp * capacity, merged.shape[1])


def swap(value, axis, k):
    return lax.ppermute(value, axis, [(i, i ^ k) for i in range(lax.axis_size(axis))])


def after(value, other):
    return lax.optimization_barrier((value, other))[0]


ORDER = (0, 2, 4, 6, 1, 3, 5, 7)


def dot(a, b):
    return jnp.dot(a, b, preferred_element_type=jnp.float32)


def dot_turned(a, b):
    return lax.dot_general(a, b, (((1,), (1,)), ((), ())), preferred_element_type=jnp.float32)


def call(kernel, outs, operands, scratch=(), flops=0, smem=0, exps=0):
    moved = sum(math.prod(x.shape) * x.dtype.itemsize for x in (*operands, *outs))
    specs = [pl.BlockSpec(memory_space=pltpu.SMEM)] * smem
    specs += [pl.BlockSpec(memory_space=pltpu.VMEM)] * (len(operands) - smem)
    return pl.pallas_call(
        kernel,
        out_shape=tuple(outs),
        in_specs=specs,
        out_specs=tuple(pl.BlockSpec(memory_space=pltpu.VMEM) for _ in outs),
        scratch_shapes=list(scratch),
        compiler_params=pltpu.CompilerParams(vmem_limit_bytes=16 * 1024 * 1024),
        cost_estimate=pl.CostEstimate(
            flops=flops, bytes_accessed=moved, transcendentals=exps
        ),
    )(*operands)


def norm_kernel(gains_ref, *refs):
    tokens, out_ref = refs[0:4], refs[4]
    rows = tokens[0].shape[0] - 16
    for n in range(4):
        out_ref[n * rows : (n + 1) * rows, :] = normalize(tokens[n][0:rows, :], gains_ref[0:1, :])


def lay_out(me, blocks, part, whole):
    step = blocks[0].shape[1]
    for number, block in zip(ORDER, blocks):
        start = pl.multiple_of((me ^ number) * step, 32)
        whole[pl.ds(start, step), :] = block[part if block.shape[0] == 4 else part % 2]


def score_kernel(me_ref, rows_ref, *refs):
    marks, blocks = refs[0:4], refs[4:12]
    weights_ref, totals_ref, q_whole, k_whole = refs[12:]
    lay_out(me_ref[0], blocks, 0, q_whole)
    lay_out(me_ref[0], blocks, 1, k_whole)
    queries = dot(rows_ref[...], q_whole[...]).astype(jnp.bfloat16)
    keys = dot(rows_ref[...], k_whole[...]).astype(jnp.bfloat16)
    rows = marks[0].shape[0] - 16
    in_row = [t[rows : rows + 16, 0:rows].astype(jnp.float32)[0:1, :] for t in marks]
    in_col = [jnp.broadcast_to(s, (rows, rows)).T[:, 0:1] for s in in_row]
    allowed = jnp.concatenate(in_col, axis=0) == jnp.concatenate(in_row, axis=1)
    factor = 1.0 / math.sqrt(HD)
    for head in range(queries.shape[1] // HD):
        cols = slice(head * HD, (head + 1) * HD)
        scores = dot_turned(queries[:, cols], keys[:, cols]) * factor
        masked = jnp.where(allowed, scores, -jnp.inf)
        weights = jnp.exp(masked - jnp.max(masked, axis=1, keepdims=True))
        weights_ref[head] = weights.astype(jnp.bfloat16)
        totals_ref[head] = jnp.sum(weights, axis=1, keepdims=True)


def value_kernel(me_ref, rows_ref, weights_ref, totals_ref, *refs):
    blocks = refs[0:8]
    keep_ref, send_ref, v_whole, out_whole = refs[8:]
    lay_out(me_ref[0], blocks, 2, v_whole)
    lay_out(me_ref[0], blocks, 3, out_whole)
    values = dot(rows_ref[...], v_whole[...]).astype(jnp.bfloat16)
    pieces = []
    for head in range(values.shape[1] // HD):
        found = dot(weights_ref[head], values[:, head * HD : (head + 1) * HD])
        pieces.append(found / totals_ref[head])
    attended = jnp.concatenate(pieces, axis=1).astype(jnp.bfloat16)
    half = attended.shape[0] // 2
    send_ref[...] = dot_turned(attended[half:, :], out_whole[...]).astype(jnp.bfloat16)
    keep_ref[...] = dot_turned(attended[:half, :], out_whole[...])


def pass_kernel(keep_ref, got_ref, out_ref):
    rows = out_ref.shape[0]
    out_ref[...] = (keep_ref[rows:, :] + got_ref[rows:, :].astype(jnp.float32)).astype(jnp.bfloat16)


def layer_kernel(tokens_ref, keep_ref, core_ref, chip_ref, gains_ref, order_ref, *refs):
    (slices,) = refs
    rows, width = tokens_ref.shape
    summed = (
        tokens_ref[...].astype(jnp.float32)
        + keep_ref[0:rows, :]
        + core_ref[0:rows, :].astype(jnp.float32)
        + chip_ref[...].astype(jnp.float32)
    )
    merge_in = normalize(summed.astype(jnp.bfloat16), gains_ref[1:2, :])
    places = lax.broadcasted_iota(jnp.int32, (rows, rows), 1)
    picking = (order_ref[...] == places).astype(jnp.bfloat16)
    ordered = dot(picking, merge_in).astype(jnp.bfloat16)
    step, half = width // 8, width // 2
    for n in range(4):
        part = jnp.concatenate(
            [
                ordered[:, n * step : (n + 1) * step],
                ordered[:, half + n * step : half + (n + 1) * step],
            ],
            axis=1,
        )
        part = jnp.concatenate([part[: rows // 2, :], part[rows // 2 :, :]], axis=1)
        slices[n] = part
        slices[4 + n] = part


def merge_kernel(me_ref, at_ref, inputs, *refs):
    blocks, (keep_ref, *sends), total = refs[0:4], refs[4:8], refs[8]
    count, width = inputs.shape[1] // 2, inputs.shape[2] // 2
    z, y = me_ref[0] // 2, lax.rem(me_ref[0], 2)
    for number in range(4):
        position = z ^ number
        at = pl.multiple_of(lax.rem(position, 2) * count, 32)
        rows = inputs[:, pl.ds(at, count), :].reshape(8 * count, 2 * width)
        rows = jnp.where(position < 2, rows[:, :width], rows[:, width:])
        step = blocks[number].shape[0] // 2
        own, other = blocks[number][:step, :], blocks[number][step:, :]
        block = jnp.concatenate(
            [jnp.where(y == 0, own, other), jnp.where(y == 0, other, own)], axis=0
        )
        found = dot(rows, block).reshape(total.shape)
        total[...] = found if number == 0 else total[...] + found
    for k in range(4):
        to = at_ref[0] ^ k
        share = jnp.concatenate([total[4 * y + to], total[4 * (1 - y) + to]], axis=0)
        if k == 0:
            keep_ref[...] = share
        else:
            sends[k - 1][...] = share.astype(jnp.bfloat16)


def pack_kernel(slots_ref, keep_ref, one_ref, two_ref, three_ref, out_ref):
    total = keep_ref[...]
    for got in (one_ref, two_ref, three_ref):
        total = total + got[...].astype(jnp.float32)
    shape = (out_ref.shape[0], total.shape[0])
    placing = (lax.broadcasted_iota(jnp.int32, shape, 0) == slots_ref[...]).astype(jnp.bfloat16)
    out_ref[...] = dot(placing, total.astype(jnp.bfloat16)).astype(jnp.bfloat16)


def by_permutes(
    tokens, qkv_weight, out_weight, merge_weight, ln_gains, segments, merge_rows, owners
):
    rows, width = tokens.shape
    count = rows // 4
    n_dp, n_fsdp = lax.axis_size("dp"), lax.axis_size("fsdp")
    me, at = lax.axis_index("dp"), lax.axis_index("fsdp")
    y = lax.rem(me, 2)
    me_cell, at_cell = me.reshape(1), at.reshape(1)
    bf16, f32 = jnp.bfloat16, jnp.float32
    shape = jax.ShapeDtypeStruct
    cols = qkv_weight.shape[2]
    group = n_fsdp * rows

    heads = jnp.concatenate([qkv_weight, out_weight.T[None]], axis=0)
    near, beside = swap(heads, "dp", 2), swap(heads, "dp", 1)
    first, second = heads[0:2], heads[2:4]
    first_far = swap(first, "dp", 4)
    second_far = swap(after(second, first_far), "dp", 4)
    first_last = swap(after(first_far, near), "dp", 2)
    second_last = swap(second_far, "dp", 2)
    half = merge_weight.shape[1] // 2
    low, high = merge_weight[:, :half], merge_weight[:, half:]
    lower = y == 0
    mine = owners[:, 0]
    note = jnp.pad(owners.astype(bf16).T, ((0, 15), (0, half - count)))
    given = jnp.concatenate([jnp.where(lower, high, low), note], axis=0)
    theirs = swap(after(given, heads), "dp", 1)
    other = theirs[-16, :count].astype(jnp.int32)
    corner = swap(beside, "dp", 2)
    blocks = [
        [heads, near, far, last, beside, corner, swap(far, "dp", 1), swap(last, "dp", 1)]
        for far, last in ((first_far, first_last), (second_far, second_last))
    ]

    marks = jnp.pad(segments.astype(bf16), ((0, 15), (0, width - rows)))
    marked = after(jnp.concatenate([tokens, marks], axis=0), first)
    along_x = swap(marked, "fsdp", 2)
    group_rows = [marked, along_x, swap(marked, "fsdp", 1), swap(along_x, "fsdp", 1)]
    (normed,) = call(norm_kernel, [shape((group, width), bf16)], [ln_gains, *group_rows])

    pair = jnp.concatenate([jnp.where(lower, low, high), theirs[:-16]], axis=0)
    held = after(pair, (second_last, blocks[1][6], *blocks[0][5:8], *group_rows[2:]))
    merge_near, merge_far = swap(held, "dp", 2), swap(held, "dp", 4)

    capacity = max(2, (2 * count + n_dp - 1) // n_dp)
    slots = []
    for number, targets in enumerate((mine, other)):
        start, rank = slot_numbers(targets, 2 * capacity)
        slots.append(start + rank + (y ^ number) * capacity)
    slots = jnp.concatenate(slots).reshape(1, 2 * count)
    order = merge_rows.reshape(count, 4).T.reshape(rows, 1)

    found = cols // HD
    weights, totals = call(
        score_kernel,
        [shape((found, group, group), bf16), shape((found, group, 1), f32)],
        [after(me_cell, theirs), normed, *group_rows, *blocks[0]],
        [pltpu.VMEM((width, cols), bf16)] * 2,
        flops=4 * group * width * cols + 2 * group * group * cols,
        smem=1,
        exps=found * group * group,
    )
    keep, send = call(
        value_kernel,
        [shape((2 * rows, width), f32), shape((2 * rows, width), bf16)],
        [me_cell, normed, weights, totals, *blocks[1]],
        [pltpu.VMEM((width, cols), bf16)] * 2,
        flops=4 * group * width * cols + 2 * group * group * cols,
        smem=1,
    )
    from_core = swap(send, "fsdp", 1)
    (onward,) = call(pass_kernel, [shape((rows, width), bf16)], [keep, from_core])
    from_chip = swap(onward, "fsdp", 2)
    (slices,) = call(
        layer_kernel,
        [shape((8, rows // 2, width // 2), bf16)],
        [tokens, keep, from_core, from_chip, ln_gains, order],
        flops=2 * rows * rows * width,
    )
    merge_blocks = [pair, merge_near, merge_far, swap(after(merge_far, slices), "dp", 2)]
    both = 2 * n_fsdp
    inputs = lax.all_to_all(
        slices,
        ("dp", "fsdp"),
        split_axis=0,
        concat_axis=0,
        tiled=True,
        axis_index_groups=[
            list(range(i, i + both)) for i in range(0, n_dp * n_fsdp, both)
        ],
    )
    shares = call(
        merge_kernel,
        [shape((2 * count, half), f32)] + [shape((2 * count, half), bf16)] * 3,
        [me_cell, at_cell, inputs, *merge_blocks],
        [pltpu.VMEM((8, count, half), f32)],
        flops=2 * 8 * count * width * half,
        smem=2,
    )
    got = [swap(shares[k], "fsdp", k) for k in range(1, 4)]
    (packed,) = call(
        pack_kernel,
        [shape((n_dp * 2 * capacity, half), bf16)],
        [slots, shares[0], *got],
        flops=2 * n_dp * 2 * capacity * 2 * count * half,
    )
    arrived = lax.all_to_all(
        packed.reshape(n_dp, 2 * capacity, half), "dp", split_axis=0, concat_axis=0, tiled=True
    )
    arrived = arrived.reshape(n_dp // 2, 2, 2, capacity, half).transpose(0, 2, 3, 1, 4)
    return arrived.reshape(n_dp * capacity, 2 * half)


def solution(mesh):
    small = mesh.shape["dp"] == 8 and mesh.shape["fsdp"] == 4
    return jax.shard_map(
        by_permutes if small else by_gathers,
        mesh=mesh,
        in_specs=(
            P(("dp", "fsdp"), None),
            P(None, "dp", "fsdp"),
            P("fsdp", "dp"),
            P(("dp", "fsdp"), None),
            P(),
            P("dp", "fsdp"),
            P(("dp", "fsdp"), None),
            P(("dp", "fsdp"), None),
        ),
        out_specs=P(("dp", "fsdp"), None),
        check_vma=False,
    )
```

```python
import functools
import math

import jax
import jax.numpy as jnp
from jax import lax
from jax.experimental import pallas as pl
from jax.experimental.pallas import tpu as pltpu
from jax.sharding import PartitionSpec as P

HD = 80


epsilon = 1e-06


def normalize(values_in, gain_row):
    widened = values_in.astype(jnp.float32)
    centered = widened - jnp.mean(widened, axis=1, keepdims=True)
    variance = jnp.mean(centered * centered, axis=1, keepdims=True)
    return (centered * lax.rsqrt(variance + epsilon) * gain_row).astype(jnp.bfloat16)


def attend(queries, keys_all, values_all, seg_rows, seg_cols):
    factor = 1.0 / math.sqrt(HD)
    allowed = seg_rows[:, None] == seg_cols[None, :]
    pieces = []
    for head_index in range(queries.shape[1] // HD):
        first_col = head_index * HD
        last_col = first_col + HD
        scores = (
            lax.dot_general(
                queries[:, first_col:last_col],
                keys_all[:, first_col:last_col],
                (((1,), (1,)), ((), ())),
                preferred_element_type=jnp.float32,
            )
            * factor
        )
        masked = jnp.where(allowed, scores, -jnp.inf)
        highest = jnp.max(masked, axis=1, keepdims=True)
        weights = jnp.exp(masked - highest)
        totals = jnp.sum(weights, axis=1, keepdims=True)
        head_out = jnp.dot(
            weights.astype(jnp.bfloat16),
            values_all[:, first_col:last_col],
            preferred_element_type=jnp.float32,
        )
        pieces.append(head_out / totals)
    return jnp.concatenate(pieces, axis=1).astype(jnp.bfloat16)


def slot_numbers(targets, capacity):
    n = targets.shape[0]
    same = targets[:, None] == targets[None, :]
    before = jnp.arange(n)[None, :] < jnp.arange(n)[:, None]
    return targets * capacity, jnp.sum((same & before).astype(jnp.int32), axis=1)


def by_gathers(
    tokens, qkv_weight, out_weight, merge_weight, ln_gains, segments, merge_rows, owners
):
    n_dp = lax.axis_size("dp")
    qkv_mine = lax.all_gather(qkv_weight, "dp", axis=1, tiled=True)
    out_mine = lax.all_gather(out_weight, "dp", axis=1, tiled=True)
    n_fsdp = lax.axis_size("fsdp")
    normed = normalize(tokens, ln_gains[0])
    group_normed = lax.all_gather(normed, "fsdp", axis=0, tiled=True)
    group_segs = lax.all_gather(segments, "fsdp", axis=1, tiled=True)
    queries, keys_all, values_all = (
        jnp.dot(group_normed, qkv_mine[n], preferred_element_type=jnp.float32).astype(jnp.bfloat16)
        for n in range(3)
    )
    attended_mine = attend(queries, keys_all, values_all, group_segs[0], group_segs[0])
    attended_local = lax.all_to_all(attended_mine, "fsdp", split_axis=0, concat_axis=1, tiled=True)
    out_full = lax.all_gather(out_mine, "fsdp", axis=0, tiled=True)
    update = jnp.dot(attended_local, out_full, preferred_element_type=jnp.float32)
    layer_out = (tokens.astype(jnp.float32) + update).astype(jnp.bfloat16)
    merge_in = normalize(layer_out, ln_gains[1])
    merge_count = tokens.shape[0] // 4
    stacked = jnp.take(merge_in, merge_rows[0], axis=0).reshape(merge_count, 4 * merge_in.shape[1])
    slice_rows = merge_weight.shape[0]
    part_rows = lax.all_gather(merge_weight, "dp", axis=0, tiled=True)
    blocks = stacked.reshape(merge_count, n_dp, n_fsdp * slice_rows)
    received = lax.all_to_all(blocks, "fsdp", split_axis=2, concat_axis=0, tiled=True)
    gathered_inputs = received.reshape(n_fsdp * merge_count, n_dp * slice_rows)
    merged = lax.psum_scatter(
        jnp.dot(gathered_inputs, part_rows, preferred_element_type=jnp.float32).astype(
            jnp.bfloat16
        ),
        "fsdp",
        scatter_dimension=0,
        tiled=True,
    )
    capacity = max(2, (2 * merge_count + n_dp - 1) // n_dp)
    first, rank = slot_numbers(owners[:, 0], capacity)
    placing = (
        jnp.arange(n_dp * capacity, dtype=jnp.int32)[:, None] == (first + rank)[None, :]
    ).astype(jnp.bfloat16)
    packed = jnp.dot(placing, merged, preferred_element_type=jnp.float32).astype(jnp.bfloat16)
    packed = packed.reshape(n_dp, capacity, merged.shape[1])
    arrived = lax.all_to_all(packed, "dp", split_axis=0, concat_axis=0, tiled=True)
    return arrived.reshape(n_dp * capacity, merged.shape[1])


def swap(value, axis, k):
    return lax.ppermute(value, axis, [(i, i ^ k) for i in range(lax.axis_size(axis))])


def after(value, other):
    return lax.optimization_barrier((value, other))[0]


ORDER = (0, 2, 4, 6, 1, 3, 5, 7)


def dot(a, b):
    return jnp.dot(a, b, preferred_element_type=jnp.float32)


def dot_turned(a, b):
    return lax.dot_general(a, b, (((1,), (1,)), ((), ())), preferred_element_type=jnp.float32)


def call(kernel, outs, operands, scratch=(), flops=0, smem=0, exps=0):
    moved = sum(math.prod(x.shape) * x.dtype.itemsize for x in (*operands, *outs))
    specs = [pl.BlockSpec(memory_space=pltpu.SMEM)] * smem
    specs += [pl.BlockSpec(memory_space=pltpu.VMEM)] * (len(operands) - smem)
    return pl.pallas_call(
        kernel,
        out_shape=tuple(outs),
        in_specs=specs,
        out_specs=tuple(pl.BlockSpec(memory_space=pltpu.VMEM) for _ in outs),
        scratch_shapes=list(scratch),
        compiler_params=pltpu.CompilerParams(vmem_limit_bytes=16 * 1024 * 1024),
        cost_estimate=pl.CostEstimate(
            flops=flops, bytes_accessed=moved, transcendentals=exps
        ),
    )(*operands)


def norm_kernel(gains_ref, *refs):
    tokens, out_ref = refs[0:4], refs[4]
    rows = tokens[0].shape[0] - 16
    for n in range(4):
        out_ref[n * rows : (n + 1) * rows, :] = normalize(tokens[n][0:rows, :], gains_ref[0:1, :])


def lay_out(me, blocks, part, whole):
    step = blocks[0].shape[1]
    for number, block in zip(ORDER, blocks):
        start = pl.multiple_of((me ^ number) * step, 32)
        whole[pl.ds(start, step), :] = block[part if block.shape[0] == 4 else part % 2]


def score_kernel(me_ref, rows_ref, *refs):
    marks, blocks = refs[0:4], refs[4:12]
    weights_ref, totals_ref, q_whole, k_whole = refs[12:]
    lay_out(me_ref[0], blocks, 0, q_whole)
    lay_out(me_ref[0], blocks, 1, k_whole)
    queries = dot(rows_ref[...], q_whole[...]).astype(jnp.bfloat16)
    keys = dot(rows_ref[...], k_whole[...]).astype(jnp.bfloat16)
    rows = marks[0].shape[0] - 16
    in_row = [t[rows : rows + 16, 0:rows].astype(jnp.float32)[0:1, :] for t in marks]
    in_col = [jnp.broadcast_to(s, (rows, rows)).T[:, 0:1] for s in in_row]
    allowed = jnp.concatenate(in_col, axis=0) == jnp.concatenate(in_row, axis=1)
    factor = 1.0 / math.sqrt(HD)
    for head in range(queries.shape[1] // HD):
        cols = slice(head * HD, (head + 1) * HD)
        scores = dot_turned(queries[:, cols], keys[:, cols]) * factor
        masked = jnp.where(allowed, scores, -jnp.inf)
        weights = jnp.exp(masked - jnp.max(masked, axis=1, keepdims=True))
        weights_ref[head] = weights.astype(jnp.bfloat16)
        totals_ref[head] = jnp.sum(weights, axis=1, keepdims=True)


def value_kernel(me_ref, rows_ref, weights_ref, totals_ref, *refs):
    blocks = refs[0:8]
    keep_ref, send_ref, v_whole, out_whole = refs[8:]
    lay_out(me_ref[0], blocks, 2, v_whole)
    lay_out(me_ref[0], blocks, 3, out_whole)
    values = dot(rows_ref[...], v_whole[...]).astype(jnp.bfloat16)
    pieces = []
    for head in range(values.shape[1] // HD):
        found = dot(weights_ref[head], values[:, head * HD : (head + 1) * HD])
        pieces.append(found / totals_ref[head])
    attended = jnp.concatenate(pieces, axis=1).astype(jnp.bfloat16)
    half = attended.shape[0] // 2
    send_ref[...] = dot_turned(attended[half:, :], out_whole[...]).astype(jnp.bfloat16)
    keep_ref[...] = dot_turned(attended[:half, :], out_whole[...])


def pass_kernel(keep_ref, got_ref, out_ref):
    rows = out_ref.shape[0]
    out_ref[...] = (keep_ref[rows:, :] + got_ref[rows:, :].astype(jnp.float32)).astype(jnp.bfloat16)


def layer_kernel(tokens_ref, keep_ref, core_ref, chip_ref, gains_ref, order_ref, *refs):
    (slices,) = refs
    rows, width = tokens_ref.shape
    summed = (
        tokens_ref[...].astype(jnp.float32)
        + keep_ref[0:rows, :]
        + core_ref[0:rows, :].astype(jnp.float32)
        + chip_ref[...].astype(jnp.float32)
    )
    merge_in = normalize(summed.astype(jnp.bfloat16), gains_ref[1:2, :])
    places = lax.broadcasted_iota(jnp.int32, (rows, rows), 1)
    picking = (order_ref[...] == places).astype(jnp.bfloat16)
    ordered = dot(picking, merge_in).astype(jnp.bfloat16)
    step, half = width // 8, width // 2
    for n in range(4):
        part = jnp.concatenate(
            [
                ordered[:, n * step : (n + 1) * step],
                ordered[:, half + n * step : half + (n + 1) * step],
            ],
            axis=1,
        )
        part = jnp.concatenate([part[: rows // 2, :], part[rows // 2 :, :]], axis=1)
        slices[n] = part
        slices[4 + n] = part


def merge_kernel(me_ref, at_ref, inputs, *refs):
    blocks, (keep_ref, *sends), total = refs[0:4], refs[4:8], refs[8]
    count, width = inputs.shape[1] // 2, inputs.shape[2] // 2
    z, y = me_ref[0] // 2, lax.rem(me_ref[0], 2)
    for number in range(4):
        position = z ^ number
        at = pl.multiple_of(lax.rem(position, 2) * count, 32)
        rows = inputs[:, pl.ds(at, count), :].reshape(8 * count, 2 * width)
        rows = jnp.where(position < 2, rows[:, :width], rows[:, width:])
        step = blocks[number].shape[0] // 2
        own, other = blocks[number][:step, :], blocks[number][step:, :]
        block = jnp.concatenate(
            [jnp.where(y == 0, own, other), jnp.where(y == 0, other, own)], axis=0
        )
        found = dot(rows, block).reshape(total.shape)
        total[...] = found if number == 0 else total[...] + found
    for k in range(4):
        to = at_ref[0] ^ k
        share = jnp.concatenate([total[4 * y + to], total[4 * (1 - y) + to]], axis=0)
        if k == 0:
            keep_ref[...] = share
        else:
            sends[k - 1][...] = share.astype(jnp.bfloat16)


def pack_kernel(slots_ref, keep_ref, one_ref, two_ref, three_ref, out_ref):
    total = keep_ref[...]
    for got in (one_ref, two_ref, three_ref):
        total = total + got[...].astype(jnp.float32)
    shape = (out_ref.shape[0], total.shape[0])
    placing = (lax.broadcasted_iota(jnp.int32, shape, 0) == slots_ref[...]).astype(jnp.bfloat16)
    out_ref[...] = dot(placing, total.astype(jnp.bfloat16)).astype(jnp.bfloat16)


def by_permutes(
    tokens, qkv_weight, out_weight, merge_weight, ln_gains, segments, merge_rows, owners
):
    rows, width = tokens.shape
    count = rows // 4
    n_dp, n_fsdp = lax.axis_size("dp"), lax.axis_size("fsdp")
    me, at = lax.axis_index("dp"), lax.axis_index("fsdp")
    y = lax.rem(me, 2)
    me_cell, at_cell = me.reshape(1), at.reshape(1)
    bf16, f32 = jnp.bfloat16, jnp.float32
    shape = jax.ShapeDtypeStruct
    cols = qkv_weight.shape[2]
    group = n_fsdp * rows

    heads = jnp.concatenate([qkv_weight, out_weight.T[None]], axis=0)
    near, beside = swap(heads, "dp", 2), swap(heads, "dp", 1)
    first, second = heads[0:2], heads[2:4]
    first_far = swap(first, "dp", 4)
    first_far_y = swap(after(first_far, (near, beside)), "dp", 1)
    first_last = swap(first_far, "dp", 2)
    corner = swap(beside, "dp", 2)
    second_far = swap(after(second, first_far), "dp", 4)

    marks = jnp.pad(segments.astype(bf16), ((0, 15), (0, width - rows)))
    marked = after(jnp.concatenate([tokens, marks], axis=0), first)
    along_x = swap(marked, "fsdp", 2)
    group_rows = [marked, along_x]
    group_rows += [swap(after(part, (first_far_y, first_last, second_far)), "fsdp", 1) for part in (marked, along_x)]
    (normed,) = call(norm_kernel, [shape((group, width), bf16)], [ln_gains, *group_rows])

    second_far_y = swap(second_far, "dp", 1)
    second_last = swap(second_far, "dp", 2)
    blocks = [
        [heads, near, far, last, beside, corner, far_y, swap(after(last, corner), "dp", 1)]
        for far, last, far_y in (
            (first_far, first_last, first_far_y),
            (second_far, second_last, second_far_y),
        )
    ]

    half = merge_weight.shape[1] // 2
    low, high = merge_weight[:, :half], merge_weight[:, half:]
    lower = y == 0
    mine = owners[:, 0]
    note = jnp.pad(owners.astype(bf16).T, ((0, 15), (0, half - count)))
    given = jnp.concatenate([jnp.where(lower, high, low), note], axis=0)
    theirs = swap(after(given, second_far_y), "dp", 1)
    other = theirs[-16, :count].astype(jnp.int32)
    pair = jnp.concatenate([jnp.where(lower, low, high), theirs[:-16]], axis=0)
    held = after(pair, (second_last, second_far_y, blocks[0][7]))
    merge_near, merge_far = swap(held, "dp", 2), swap(held, "dp", 4)

    capacity = max(2, (2 * count + n_dp - 1) // n_dp)
    slots = []
    for number, targets in enumerate((mine, other)):
        start, rank = slot_numbers(targets, 2 * capacity)
        slots.append(start + rank + (y ^ number) * capacity)
    slots = jnp.concatenate(slots).reshape(1, 2 * count)
    order = merge_rows.reshape(count, 4).T.reshape(rows, 1)

    found = cols // HD
    weights, totals = call(
        score_kernel,
        [shape((found, group, group), bf16), shape((found, group, 1), f32)],
        [after(me_cell, theirs), normed, *group_rows, *blocks[0]],
        [pltpu.VMEM((width, cols), bf16)] * 2,
        flops=4 * group * width * cols + 2 * group * group * cols,
        smem=1,
        exps=found * group * group,
    )
    keep, send = call(
        value_kernel,
        [shape((2 * rows, width), f32), shape((2 * rows, width), bf16)],
        [me_cell, normed, weights, totals, *blocks[1]],
        [pltpu.VMEM((width, cols), bf16)] * 2,
        flops=4 * group * width * cols + 2 * group * group * cols,
        smem=1,
    )
    from_core = swap(send, "fsdp", 1)
    (onward,) = call(pass_kernel, [shape((rows, width), bf16)], [keep, from_core])
    from_chip = swap(onward, "fsdp", 2)
    (slices,) = call(
        layer_kernel,
        [shape((8, rows // 2, width // 2), bf16)],
        [tokens, keep, from_core, from_chip, ln_gains, order],
        flops=2 * rows * rows * width,
    )
    merge_blocks = [pair, merge_near, merge_far, swap(after(merge_far, (slices, merge_near)), "dp", 2)]
    both = 2 * n_fsdp
    inputs = lax.all_to_all(
        slices,
        ("dp", "fsdp"),
        split_axis=0,
        concat_axis=0,
        tiled=True,
        axis_index_groups=[
            list(range(i, i + both)) for i in range(0, n_dp * n_fsdp, both)
        ],
    )
    shares = call(
        merge_kernel,
        [shape((2 * count, half), f32)] + [shape((2 * count, half), bf16)] * 3,
        [me_cell, at_cell, inputs, *merge_blocks],
        [pltpu.VMEM((8, count, half), f32)],
        flops=2 * 8 * count * width * half,
        smem=2,
    )
    got = [swap(shares[k], "fsdp", k) for k in range(1, 4)]
    (packed,) = call(
        pack_kernel,
        [shape((n_dp * 2 * capacity, half), bf16)],
        [slots, shares[0], *got],
        flops=2 * n_dp * 2 * capacity * 2 * count * half,
    )
    arrived = lax.all_to_all(
        packed.reshape(n_dp, 2 * capacity, half), "dp", split_axis=0, concat_axis=0, tiled=True
    )
    arrived = arrived.reshape(n_dp // 2, 2, 2, capacity, half).transpose(0, 2, 3, 1, 4)
    return arrived.reshape(n_dp * capacity, 2 * half)


def solution(mesh):
    small = mesh.shape["dp"] == 8 and mesh.shape["fsdp"] == 4
    return jax.shard_map(
        by_permutes if small else by_gathers,
        mesh=mesh,
        in_specs=(
            P(("dp", "fsdp"), None),
            P(None, "dp", "fsdp"),
            P("fsdp", "dp"),
            P(("dp", "fsdp"), None),
            P(),
            P("dp", "fsdp"),
            P(("dp", "fsdp"), None),
            P(("dp", "fsdp"), None),
        ),
        out_specs=P(("dp", "fsdp"), None),
        check_vma=False,
    )
```

```python
import functools
import math

import jax
import jax.numpy as jnp
from jax import lax
from jax.experimental import pallas as pl
from jax.experimental.pallas import tpu as pltpu
from jax.sharding import PartitionSpec as P

HD = 80


epsilon = 1e-06


def normalize(values_in, gain_row):
    widened = values_in.astype(jnp.float32)
    centered = widened - jnp.mean(widened, axis=1, keepdims=True)
    variance = jnp.mean(centered * centered, axis=1, keepdims=True)
    return (centered * lax.rsqrt(variance + epsilon) * gain_row).astype(jnp.bfloat16)


def attend(queries, keys_all, values_all, seg_rows, seg_cols):
    factor = 1.0 / math.sqrt(HD)
    allowed = seg_rows[:, None] == seg_cols[None, :]
    pieces = []
    for head_index in range(queries.shape[1] // HD):
        first_col = head_index * HD
        last_col = first_col + HD
        scores = (
            lax.dot_general(
                queries[:, first_col:last_col],
                keys_all[:, first_col:last_col],
                (((1,), (1,)), ((), ())),
                preferred_element_type=jnp.float32,
            )
            * factor
        )
        masked = jnp.where(allowed, scores, -jnp.inf)
        highest = jnp.max(masked, axis=1, keepdims=True)
        weights = jnp.exp(masked - highest)
        totals = jnp.sum(weights, axis=1, keepdims=True)
        head_out = jnp.dot(
            weights.astype(jnp.bfloat16),
            values_all[:, first_col:last_col],
            preferred_element_type=jnp.float32,
        )
        pieces.append(head_out / totals)
    return jnp.concatenate(pieces, axis=1).astype(jnp.bfloat16)


def slot_numbers(targets, capacity):
    n = targets.shape[0]
    same = targets[:, None] == targets[None, :]
    before = jnp.arange(n)[None, :] < jnp.arange(n)[:, None]
    return targets * capacity, jnp.sum((same & before).astype(jnp.int32), axis=1)


def by_gathers(
    tokens, qkv_weight, out_weight, merge_weight, ln_gains, segments, merge_rows, owners
):
    n_dp = lax.axis_size("dp")
    qkv_mine = lax.all_gather(qkv_weight, "dp", axis=1, tiled=True)
    out_mine = lax.all_gather(out_weight, "dp", axis=1, tiled=True)
    n_fsdp = lax.axis_size("fsdp")
    normed = normalize(tokens, ln_gains[0])
    group_normed = lax.all_gather(normed, "fsdp", axis=0, tiled=True)
    group_segs = lax.all_gather(segments, "fsdp", axis=1, tiled=True)
    queries, keys_all, values_all = (
        jnp.dot(group_normed, qkv_mine[n], preferred_element_type=jnp.float32).astype(jnp.bfloat16)
        for n in range(3)
    )
    attended_mine = attend(queries, keys_all, values_all, group_segs[0], group_segs[0])
    attended_local = lax.all_to_all(attended_mine, "fsdp", split_axis=0, concat_axis=1, tiled=True)
    out_full = lax.all_gather(out_mine, "fsdp", axis=0, tiled=True)
    update = jnp.dot(attended_local, out_full, preferred_element_type=jnp.float32)
    layer_out = (tokens.astype(jnp.float32) + update).astype(jnp.bfloat16)
    merge_in = normalize(layer_out, ln_gains[1])
    merge_count = tokens.shape[0] // 4
    stacked = jnp.take(merge_in, merge_rows[0], axis=0).reshape(merge_count, 4 * merge_in.shape[1])
    slice_rows = merge_weight.shape[0]
    part_rows = lax.all_gather(merge_weight, "dp", axis=0, tiled=True)
    blocks = stacked.reshape(merge_count, n_dp, n_fsdp * slice_rows)
    received = lax.all_to_all(blocks, "fsdp", split_axis=2, concat_axis=0, tiled=True)
    gathered_inputs = received.reshape(n_fsdp * merge_count, n_dp * slice_rows)
    merged = lax.psum_scatter(
        jnp.dot(gathered_inputs, part_rows, preferred_element_type=jnp.float32).astype(
            jnp.bfloat16
        ),
        "fsdp",
        scatter_dimension=0,
        tiled=True,
    )
    capacity = max(2, (2 * merge_count + n_dp - 1) // n_dp)
    first, rank = slot_numbers(owners[:, 0], capacity)
    placing = (
        jnp.arange(n_dp * capacity, dtype=jnp.int32)[:, None] == (first + rank)[None, :]
    ).astype(jnp.bfloat16)
    packed = jnp.dot(placing, merged, preferred_element_type=jnp.float32).astype(jnp.bfloat16)
    packed = packed.reshape(n_dp, capacity, merged.shape[1])
    arrived = lax.all_to_all(packed, "dp", split_axis=0, concat_axis=0, tiled=True)
    return arrived.reshape(n_dp * capacity, merged.shape[1])


def swap(value, axis, k):
    return lax.ppermute(value, axis, [(i, i ^ k) for i in range(lax.axis_size(axis))])


def after(value, other):
    return lax.optimization_barrier((value, other))[0]


ORDER = (0, 2, 4, 6, 1, 3, 5, 7)


def dot(a, b):
    return jnp.dot(a, b, preferred_element_type=jnp.float32)


def dot_turned(a, b):
    return lax.dot_general(a, b, (((1,), (1,)), ((), ())), preferred_element_type=jnp.float32)


def call(kernel, outs, operands, scratch=(), flops=0, smem=0, exps=0):
    moved = sum(math.prod(x.shape) * x.dtype.itemsize for x in (*operands, *outs))
    specs = [pl.BlockSpec(memory_space=pltpu.SMEM)] * smem
    specs += [pl.BlockSpec(memory_space=pltpu.VMEM)] * (len(operands) - smem)
    return pl.pallas_call(
        kernel,
        out_shape=tuple(outs),
        in_specs=specs,
        out_specs=tuple(pl.BlockSpec(memory_space=pltpu.VMEM) for _ in outs),
        scratch_shapes=list(scratch),
        compiler_params=pltpu.CompilerParams(vmem_limit_bytes=16 * 1024 * 1024),
        cost_estimate=pl.CostEstimate(
            flops=flops, bytes_accessed=moved, transcendentals=exps
        ),
    )(*operands)


def norm_kernel(gains_ref, *refs):
    tokens, out_ref = refs[0:4], refs[4]
    rows = tokens[0].shape[0] - 16
    for n in range(4):
        out_ref[n * rows : (n + 1) * rows, :] = normalize(tokens[n][0:rows, :], gains_ref[0:1, :])


def lay_out(me, blocks, part, whole):
    step = blocks[0].shape[1]
    for number, block in zip(ORDER, blocks):
        start = pl.multiple_of((me ^ number) * step, 32)
        whole[pl.ds(start, step), :] = block[part if block.shape[0] == 4 else part % 2]


def score_kernel(me_ref, rows_ref, *refs):
    marks, blocks = refs[0:4], refs[4:12]
    weights_ref, totals_ref, q_whole, k_whole = refs[12:]
    lay_out(me_ref[0], blocks, 0, q_whole)
    lay_out(me_ref[0], blocks, 1, k_whole)
    queries = dot(rows_ref[...], q_whole[...]).astype(jnp.bfloat16)
    keys = dot(rows_ref[...], k_whole[...]).astype(jnp.bfloat16)
    rows = marks[0].shape[0] - 16
    in_row = [t[rows : rows + 16, 0:rows].astype(jnp.float32)[0:1, :] for t in marks]
    in_col = [jnp.broadcast_to(s, (rows, rows)).T[:, 0:1] for s in in_row]
    allowed = jnp.concatenate(in_col, axis=0) == jnp.concatenate(in_row, axis=1)
    factor = 1.0 / math.sqrt(HD)
    for head in range(queries.shape[1] // HD):
        cols = slice(head * HD, (head + 1) * HD)
        scores = dot_turned(queries[:, cols], keys[:, cols]) * factor
        masked = jnp.where(allowed, scores, -jnp.inf)
        weights = jnp.exp(masked - jnp.max(masked, axis=1, keepdims=True))
        weights_ref[head] = weights.astype(jnp.bfloat16)
        totals_ref[head] = jnp.sum(weights, axis=1, keepdims=True)


def value_kernel(me_ref, rows_ref, weights_ref, totals_ref, *refs):
    blocks = refs[0:8]
    attended_ref, send_ref, v_whole, out_whole = refs[8:]
    lay_out(me_ref[0], blocks, 2, v_whole)
    lay_out(me_ref[0], blocks, 3, out_whole)
    values = dot(rows_ref[...], v_whole[...]).astype(jnp.bfloat16)
    pieces = []
    for head in range(values.shape[1] // HD):
        found = dot(weights_ref[head], values[:, head * HD : (head + 1) * HD])
        pieces.append(found / totals_ref[head])
    attended = jnp.concatenate(pieces, axis=1).astype(jnp.bfloat16)
    half = attended.shape[0] // 2
    attended_ref[...] = attended[:half, :]
    send_ref[...] = dot_turned(attended[half:, :], out_whole[...]).astype(jnp.bfloat16)


def keep_kernel(me_ref, attended_ref, *refs):
    blocks, (keep_ref, out_whole) = refs[0:8], refs[8:]
    lay_out(me_ref[0], blocks, 3, out_whole)
    keep_ref[...] = dot_turned(attended_ref[...], out_whole[...])


def pass_kernel(keep_ref, got_ref, out_ref):
    rows = out_ref.shape[0]
    out_ref[...] = (keep_ref[rows:, :] + got_ref[rows:, :].astype(jnp.float32)).astype(jnp.bfloat16)


def layer_kernel(tokens_ref, keep_ref, core_ref, chip_ref, gains_ref, order_ref, *refs):
    (slices,) = refs
    rows, width = tokens_ref.shape[0] - 16, tokens_ref.shape[1]
    summed = (
        tokens_ref[0:rows, :].astype(jnp.float32)
        + keep_ref[0:rows, :]
        + core_ref[0:rows, :].astype(jnp.float32)
        + chip_ref[...].astype(jnp.float32)
    )
    merge_in = normalize(summed.astype(jnp.bfloat16), gains_ref[1:2, :])
    places = lax.broadcasted_iota(jnp.int32, (rows, rows), 1)
    picking = (order_ref[...] == places).astype(jnp.bfloat16)
    ordered = dot(picking, merge_in).astype(jnp.bfloat16)
    step, half = width // 8, width // 2
    for n in range(4):
        part = jnp.concatenate(
            [
                ordered[:, n * step : (n + 1) * step],
                ordered[:, half + n * step : half + (n + 1) * step],
            ],
            axis=1,
        )
        part = jnp.concatenate([part[: rows // 2, :], part[rows // 2 :, :]], axis=1)
        slices[n] = part
        slices[4 + n] = part


def merge_kernel(me_ref, at_ref, inputs, *refs):
    blocks, (keep_ref, *sends), total = refs[0:4], refs[4:8], refs[8]
    count, width = inputs.shape[1] // 2, inputs.shape[2] // 2
    z, y = me_ref[0] // 2, lax.rem(me_ref[0], 2)
    for number in range(4):
        position = z ^ number
        at = pl.multiple_of(lax.rem(position, 2) * count, 32)
        rows = inputs[:, pl.ds(at, count), :].reshape(8 * count, 2 * width)
        rows = jnp.where(position < 2, rows[:, :width], rows[:, width:])
        step = blocks[number].shape[0] // 2
        own, other = blocks[number][:step, :], blocks[number][step:, :]
        block = jnp.concatenate(
            [jnp.where(y == 0, own, other), jnp.where(y == 0, other, own)], axis=0
        )
        found = dot(rows, block).reshape(total.shape)
        total[...] = found if number == 0 else total[...] + found
    for k in range(4):
        to = at_ref[0] ^ k
        share = jnp.concatenate([total[4 * y + to], total[4 * (1 - y) + to]], axis=0)
        if k == 0:
            keep_ref[...] = share
        else:
            sends[k - 1][...] = share.astype(jnp.bfloat16)


def pack_kernel(slots_ref, keep_ref, one_ref, two_ref, three_ref, out_ref):
    total = keep_ref[...]
    for got in (one_ref, two_ref, three_ref):
        total = total + got[...].astype(jnp.float32)
    shape = (out_ref.shape[0], total.shape[0])
    placing = (lax.broadcasted_iota(jnp.int32, shape, 0) == slots_ref[...]).astype(jnp.bfloat16)
    out_ref[...] = dot(placing, total.astype(jnp.bfloat16)).astype(jnp.bfloat16)


def by_permutes(
    tokens, qkv_weight, out_weight, merge_weight, ln_gains, segments, merge_rows, owners
):
    rows, width = tokens.shape
    count = rows // 4
    n_dp, n_fsdp = lax.axis_size("dp"), lax.axis_size("fsdp")
    me, at = lax.axis_index("dp"), lax.axis_index("fsdp")
    y = lax.rem(me, 2)
    me_cell, at_cell = me.reshape(1), at.reshape(1)
    bf16, f32 = jnp.bfloat16, jnp.float32
    shape = jax.ShapeDtypeStruct
    cols = qkv_weight.shape[2]
    group = n_fsdp * rows

    marks = jnp.pad(segments.astype(bf16), ((0, 15), (0, width - rows)))
    marked = jnp.concatenate([tokens, marks], axis=0)
    first = qkv_weight[0:2]
    out_turned = after(out_weight, first).T[None]
    heads = jnp.concatenate([qkv_weight, out_turned], axis=0)
    beside = swap(heads, "dp", 1)
    first_far, first_near = swap(first, "dp", 4), swap(first, "dp", 2)
    second = jnp.concatenate([qkv_weight[2:3], out_turned], axis=0)
    first_far_y = swap(first_far, "dp", 1)
    first_last = swap(first_far, "dp", 2)
    corner = swap(beside, "dp", 2)
    second_far = swap(after(second, first_far), "dp", 4)

    marked = after(marked, heads)
    along_x = swap(marked, "fsdp", 2)
    group_rows = [marked, along_x]
    group_rows += [swap(after(part, (first_near, beside, first_far_y, first_last, second_far)), "fsdp", 1) for part in (marked, along_x)]
    (normed,) = call(norm_kernel, [shape((group, width), bf16)], [ln_gains, *group_rows])

    second_near = swap(after(second, first_last), "dp", 2)
    second_far_y = swap(second_far, "dp", 1)
    second_last = swap(second_far, "dp", 2)
    blocks = [
        [heads, near, far, last, beside, corner, far_y, swap(after(last, corner), "dp", 1)]
        for near, far, last, far_y in (
            (first_near, first_far, first_last, first_far_y),
            (second_near, second_far, second_last, second_far_y),
        )
    ]

    half = merge_weight.shape[1] // 2
    low, high = merge_weight[:, :half], merge_weight[:, half:]
    lower = y == 0
    mine = owners[:, 0]
    note = jnp.pad(owners.astype(bf16).T, ((0, 15), (0, half - count)))
    given = jnp.concatenate([jnp.where(lower, high, low), note], axis=0)
    theirs = swap(after(given, second_far_y), "dp", 1)
    other = theirs[-16, :count].astype(jnp.int32)
    pair = jnp.concatenate([jnp.where(lower, low, high), theirs[:-16]], axis=0)
    held = after(pair, (second_last, second_far_y, blocks[0][7]))
    merge_near, merge_far = swap(held, "dp", 2), swap(held, "dp", 4)

    capacity = max(2, (2 * count + n_dp - 1) // n_dp)
    slots = []
    for number, targets in enumerate((mine, other)):
        start, rank = slot_numbers(targets, 2 * capacity)
        slots.append(start + rank + (y ^ number) * capacity)
    slots = jnp.concatenate(slots).reshape(1, 2 * count)
    order = merge_rows.reshape(count, 4).T.reshape(rows, 1)

    found = cols // HD
    weights, totals = call(
        score_kernel,
        [shape((found, group, group), bf16), shape((found, group, 1), f32)],
        [after(me_cell, theirs), normed, *group_rows, *blocks[0]],
        [pltpu.VMEM((width, cols), bf16)] * 2,
        flops=4 * group * width * cols + 2 * group * group * cols,
        smem=1,
        exps=found * group * group,
    )
    attended, send = call(
        value_kernel,
        [shape((2 * rows, cols), bf16), shape((2 * rows, width), bf16)],
        [me_cell, normed, weights, totals, *blocks[1]],
        [pltpu.VMEM((width, cols), bf16)] * 2,
        flops=4 * group * width * cols + 2 * group * group * cols,
        smem=1,
    )
    from_core = swap(send, "fsdp", 1)
    (keep,) = call(
        keep_kernel,
        [shape((2 * rows, width), f32)],
        [me_cell, attended, *blocks[1]],
        [pltpu.VMEM((width, cols), bf16)],
        flops=4 * rows * width * cols,
        smem=1,
    )
    (onward,) = call(pass_kernel, [shape((rows, width), bf16)], [keep, from_core])
    from_chip = swap(onward, "fsdp", 2)
    (slices,) = call(
        layer_kernel,
        [shape((8, rows // 2, width // 2), bf16)],
        [marked, keep, from_core, from_chip, ln_gains, order],
        flops=2 * rows * rows * width,
    )
    merge_blocks = [pair, merge_near, merge_far, swap(after(merge_far, (slices, merge_near)), "dp", 2)]
    both = 2 * n_fsdp
    inputs = lax.all_to_all(
        slices,
        ("dp", "fsdp"),
        split_axis=0,
        concat_axis=0,
        tiled=True,
        axis_index_groups=[
            list(range(i, i + both)) for i in range(0, n_dp * n_fsdp, both)
        ],
    )
    shares = call(
        merge_kernel,
        [shape((2 * count, half), f32)] + [shape((2 * count, half), bf16)] * 3,
        [me_cell, at_cell, inputs, *merge_blocks],
        [pltpu.VMEM((8, count, half), f32)],
        flops=2 * 8 * count * width * half,
        smem=2,
    )
    got = [swap(shares[k], "fsdp", k) for k in range(1, 4)]
    (packed,) = call(
        pack_kernel,
        [shape((n_dp * 2 * capacity, half), bf16)],
        [slots, shares[0], *got],
        flops=2 * n_dp * 2 * capacity * 2 * count * half,
    )
    arrived = lax.all_to_all(
        packed.reshape(n_dp, 2 * capacity, half), "dp", split_axis=0, concat_axis=0, tiled=True
    )
    arrived = arrived.reshape(n_dp // 2, 2, 2, capacity, half).transpose(0, 2, 3, 1, 4)
    return arrived.reshape(n_dp * capacity, 2 * half)


def solution(mesh):
    small = mesh.shape["dp"] == 8 and mesh.shape["fsdp"] == 4
    return jax.shard_map(
        by_permutes if small else by_gathers,
        mesh=mesh,
        in_specs=(
            P(("dp", "fsdp"), None),
            P(None, "dp", "fsdp"),
            P("fsdp", "dp"),
            P(("dp", "fsdp"), None),
            P(),
            P("dp", "fsdp"),
            P(("dp", "fsdp"), None),
            P(("dp", "fsdp"), None),
        ),
        out_specs=P(("dp", "fsdp"), None),
        check_vma=False,
    )
```

```python
import functools
import math

import jax
import jax.numpy as jnp
from jax import lax
from jax.experimental import pallas as pl
from jax.experimental.pallas import tpu as pltpu
from jax.sharding import PartitionSpec as P

HD = 80


epsilon = 1e-06


def normalize(values_in, gain_row):
    widened = values_in.astype(jnp.float32)
    centered = widened - jnp.mean(widened, axis=1, keepdims=True)
    variance = jnp.mean(centered * centered, axis=1, keepdims=True)
    return (centered * lax.rsqrt(variance + epsilon) * gain_row).astype(jnp.bfloat16)


def attend(queries, keys_all, values_all, seg_rows, seg_cols):
    factor = 1.0 / math.sqrt(HD)
    allowed = seg_rows[:, None] == seg_cols[None, :]
    pieces = []
    for head_index in range(queries.shape[1] // HD):
        first_col = head_index * HD
        last_col = first_col + HD
        scores = (
            lax.dot_general(
                queries[:, first_col:last_col],
                keys_all[:, first_col:last_col],
                (((1,), (1,)), ((), ())),
                preferred_element_type=jnp.float32,
            )
            * factor
        )
        masked = jnp.where(allowed, scores, -jnp.inf)
        highest = jnp.max(masked, axis=1, keepdims=True)
        weights = jnp.exp(masked - highest)
        totals = jnp.sum(weights, axis=1, keepdims=True)
        head_out = jnp.dot(
            weights.astype(jnp.bfloat16),
            values_all[:, first_col:last_col],
            preferred_element_type=jnp.float32,
        )
        pieces.append(head_out / totals)
    return jnp.concatenate(pieces, axis=1).astype(jnp.bfloat16)


def slot_numbers(targets, capacity):
    n = targets.shape[0]
    same = targets[:, None] == targets[None, :]
    before = jnp.arange(n)[None, :] < jnp.arange(n)[:, None]
    return targets * capacity, jnp.sum((same & before).astype(jnp.int32), axis=1)


def by_gathers(
    tokens, qkv_weight, out_weight, merge_weight, ln_gains, segments, merge_rows, owners
):
    n_dp = lax.axis_size("dp")
    qkv_mine = lax.all_gather(qkv_weight, "dp", axis=1, tiled=True)
    out_mine = lax.all_gather(out_weight, "dp", axis=1, tiled=True)
    n_fsdp = lax.axis_size("fsdp")
    normed = normalize(tokens, ln_gains[0])
    group_normed = lax.all_gather(normed, "fsdp", axis=0, tiled=True)
    group_segs = lax.all_gather(segments, "fsdp", axis=1, tiled=True)
    queries, keys_all, values_all = (
        jnp.dot(group_normed, qkv_mine[n], preferred_element_type=jnp.float32).astype(jnp.bfloat16)
        for n in range(3)
    )
    attended_mine = attend(queries, keys_all, values_all, group_segs[0], group_segs[0])
    attended_local = lax.all_to_all(attended_mine, "fsdp", split_axis=0, concat_axis=1, tiled=True)
    out_full = lax.all_gather(out_mine, "fsdp", axis=0, tiled=True)
    update = jnp.dot(attended_local, out_full, preferred_element_type=jnp.float32)
    layer_out = (tokens.astype(jnp.float32) + update).astype(jnp.bfloat16)
    merge_in = normalize(layer_out, ln_gains[1])
    merge_count = tokens.shape[0] // 4
    stacked = jnp.take(merge_in, merge_rows[0], axis=0).reshape(merge_count, 4 * merge_in.shape[1])
    slice_rows = merge_weight.shape[0]
    part_rows = lax.all_gather(merge_weight, "dp", axis=0, tiled=True)
    blocks = stacked.reshape(merge_count, n_dp, n_fsdp * slice_rows)
    received = lax.all_to_all(blocks, "fsdp", split_axis=2, concat_axis=0, tiled=True)
    gathered_inputs = received.reshape(n_fsdp * merge_count, n_dp * slice_rows)
    merged = lax.psum_scatter(
        jnp.dot(gathered_inputs, part_rows, preferred_element_type=jnp.float32).astype(
            jnp.bfloat16
        ),
        "fsdp",
        scatter_dimension=0,
        tiled=True,
    )
    capacity = max(2, (2 * merge_count + n_dp - 1) // n_dp)
    first, rank = slot_numbers(owners[:, 0], capacity)
    placing = (
        jnp.arange(n_dp * capacity, dtype=jnp.int32)[:, None] == (first + rank)[None, :]
    ).astype(jnp.bfloat16)
    packed = jnp.dot(placing, merged, preferred_element_type=jnp.float32).astype(jnp.bfloat16)
    packed = packed.reshape(n_dp, capacity, merged.shape[1])
    arrived = lax.all_to_all(packed, "dp", split_axis=0, concat_axis=0, tiled=True)
    return arrived.reshape(n_dp * capacity, merged.shape[1])


def swap(value, axis, k):
    return lax.ppermute(value, axis, [(i, i ^ k) for i in range(lax.axis_size(axis))])


def after(value, other):
    return lax.optimization_barrier((value, other))[0]


ORDER = (0, 2, 4, 6, 1, 3, 5, 7)


def dot(a, b):
    return jnp.dot(a, b, preferred_element_type=jnp.float32)


def dot_turned(a, b):
    return lax.dot_general(a, b, (((1,), (1,)), ((), ())), preferred_element_type=jnp.float32)


def call(kernel, outs, operands, scratch=(), flops=0, smem=0, exps=0):
    moved = sum(math.prod(x.shape) * x.dtype.itemsize for x in (*operands, *outs))
    specs = [pl.BlockSpec(memory_space=pltpu.SMEM)] * smem
    specs += [pl.BlockSpec(memory_space=pltpu.VMEM)] * (len(operands) - smem)
    return pl.pallas_call(
        kernel,
        out_shape=tuple(outs),
        in_specs=specs,
        out_specs=tuple(pl.BlockSpec(memory_space=pltpu.VMEM) for _ in outs),
        scratch_shapes=list(scratch),
        compiler_params=pltpu.CompilerParams(vmem_limit_bytes=16 * 1024 * 1024),
        cost_estimate=pl.CostEstimate(
            flops=flops, bytes_accessed=moved, transcendentals=exps
        ),
    )(*operands)


def norm_kernel(gains_ref, *refs):
    tokens, out_ref = refs[0:4], refs[4]
    rows = tokens[0].shape[0] - 16
    for n in range(4):
        out_ref[n * rows : (n + 1) * rows, :] = normalize(tokens[n][0:rows, :], gains_ref[0:1, :])


def lay_out(me, blocks, part, whole):
    step = blocks[0].shape[1]
    for number, block in zip(ORDER, blocks):
        start = pl.multiple_of((me ^ number) * step, 32)
        whole[pl.ds(start, step), :] = block[part if part < block.shape[0] else 0]


def attention_kernel(me_ref, rows_ref, *refs):
    marks, blocks, out_blocks = refs[0:4], refs[4:12], refs[12:20]
    attended_ref, send_ref, q_whole, k_whole, v_whole, out_whole = refs[20:]
    lay_out(me_ref[0], blocks, 0, q_whole)
    lay_out(me_ref[0], blocks, 1, k_whole)
    lay_out(me_ref[0], blocks, 2, v_whole)
    lay_out(me_ref[0], out_blocks, 3, out_whole)
    queries = dot(rows_ref[...], q_whole[...]).astype(jnp.bfloat16)
    keys = dot(rows_ref[...], k_whole[...]).astype(jnp.bfloat16)
    values = dot(rows_ref[...], v_whole[...]).astype(jnp.bfloat16)
    rows = marks[0].shape[0] - 16
    in_row = [t[rows : rows + 16, 0:rows].astype(jnp.float32)[0:1, :] for t in marks]
    in_col = [jnp.broadcast_to(s, (rows, rows)).T[:, 0:1] for s in in_row]
    allowed = jnp.concatenate(in_col, axis=0) == jnp.concatenate(in_row, axis=1)
    factor = 1.0 / math.sqrt(HD)
    pieces = []
    for head in range(queries.shape[1] // HD):
        cols = slice(head * HD, (head + 1) * HD)
        scores = dot_turned(queries[:, cols], keys[:, cols]) * factor
        masked = jnp.where(allowed, scores, -jnp.inf)
        weights = jnp.exp(masked - jnp.max(masked, axis=1, keepdims=True))
        totals = jnp.sum(weights, axis=1, keepdims=True)
        pieces.append(dot(weights.astype(jnp.bfloat16), values[:, cols]) / totals)
    attended = jnp.concatenate(pieces, axis=1).astype(jnp.bfloat16)
    half = attended.shape[0] // 2
    attended_ref[...] = attended[:half, :]
    send_ref[...] = dot_turned(attended[half:, :], out_whole[...]).astype(jnp.bfloat16)


def keep_kernel(me_ref, attended_ref, *refs):
    blocks, (keep_ref, out_whole) = refs[0:8], refs[8:]
    lay_out(me_ref[0], blocks, 3, out_whole)
    keep_ref[...] = dot_turned(attended_ref[...], out_whole[...])


def pass_kernel(keep_ref, got_ref, out_ref):
    rows = out_ref.shape[0]
    out_ref[...] = (keep_ref[rows:, :] + got_ref[rows:, :].astype(jnp.float32)).astype(jnp.bfloat16)


def layer_kernel(tokens_ref, keep_ref, core_ref, chip_ref, gains_ref, order_ref, *refs):
    (slices,) = refs
    rows, width = tokens_ref.shape[0] - 16, tokens_ref.shape[1]
    summed = (
        tokens_ref[0:rows, :].astype(jnp.float32)
        + keep_ref[0:rows, :]
        + core_ref[0:rows, :].astype(jnp.float32)
        + chip_ref[...].astype(jnp.float32)
    )
    merge_in = normalize(summed.astype(jnp.bfloat16), gains_ref[1:2, :])
    places = lax.broadcasted_iota(jnp.int32, (rows, rows), 1)
    picking = (order_ref[...] == places).astype(jnp.bfloat16)
    ordered = dot(picking, merge_in).astype(jnp.bfloat16)
    step, half = width // 8, width // 2
    for n in range(4):
        part = jnp.concatenate(
            [
                ordered[:, n * step : (n + 1) * step],
                ordered[:, half + n * step : half + (n + 1) * step],
            ],
            axis=1,
        )
        part = jnp.concatenate([part[: rows // 2, :], part[rows // 2 :, :]], axis=1)
        slices[n] = part
        slices[4 + n] = part


def merge_kernel(me_ref, at_ref, inputs, *refs):
    blocks, (keep_ref, *sends), total = refs[0:4], refs[4:8], refs[8]
    count, width = inputs.shape[1] // 2, inputs.shape[2] // 2
    z, y = me_ref[0] // 2, lax.rem(me_ref[0], 2)
    for number in range(4):
        position = z ^ number
        at = pl.multiple_of(lax.rem(position, 2) * count, 32)
        rows = inputs[:, pl.ds(at, count), :].reshape(8 * count, 2 * width)
        rows = jnp.where(position < 2, rows[:, :width], rows[:, width:])
        step = blocks[number].shape[0] // 2
        own, other = blocks[number][:step, :], blocks[number][step:, :]
        block = jnp.concatenate(
            [jnp.where(y == 0, own, other), jnp.where(y == 0, other, own)], axis=0
        )
        found = dot(rows, block).reshape(total.shape)
        total[...] = found if number == 0 else total[...] + found
    for k in range(4):
        to = at_ref[0] ^ k
        share = jnp.concatenate([total[4 * y + to], total[4 * (1 - y) + to]], axis=0)
        if k == 0:
            keep_ref[...] = share
        else:
            sends[k - 1][...] = share.astype(jnp.bfloat16)


def pack_kernel(slots_ref, keep_ref, one_ref, two_ref, three_ref, out_ref):
    total = keep_ref[...]
    for got in (one_ref, two_ref, three_ref):
        total = total + got[...].astype(jnp.float32)
    shape = (out_ref.shape[0], total.shape[0])
    placing = (lax.broadcasted_iota(jnp.int32, shape, 0) == slots_ref[...]).astype(jnp.bfloat16)
    out_ref[...] = dot(placing, total.astype(jnp.bfloat16)).astype(jnp.bfloat16)


def by_permutes(
    tokens, qkv_weight, out_weight, merge_weight, ln_gains, segments, merge_rows, owners
):
    rows, width = tokens.shape
    count = rows // 4
    n_dp, n_fsdp = lax.axis_size("dp"), lax.axis_size("fsdp")
    me, at = lax.axis_index("dp"), lax.axis_index("fsdp")
    y = lax.rem(me, 2)
    me_cell, at_cell = me.reshape(1), at.reshape(1)
    bf16, f32 = jnp.bfloat16, jnp.float32
    shape = jax.ShapeDtypeStruct
    cols = qkv_weight.shape[2]
    group = n_fsdp * rows

    far = swap(qkv_weight, "dp", 4)
    out_turned = out_weight.T[None]
    heads = jnp.concatenate([qkv_weight, out_turned], axis=0)
    near, beside = swap(heads, "dp", 2), swap(heads, "dp", 1)
    far_y, last = swap(far, "dp", 1), swap(after(far, beside), "dp", 2)
    last_y = swap(last, "dp", 1)
    corner = swap(after(beside, last), "dp", 2)
    half = merge_weight.shape[1] // 2
    low, high = merge_weight[:, :half], merge_weight[:, half:]
    lower = y == 0
    mine = owners[:, 0]
    note = jnp.pad(owners.astype(bf16).T, ((0, 15), (0, half - count)))
    given = jnp.concatenate([jnp.where(lower, high, low), note], axis=0)
    theirs = swap(after(given, heads), "dp", 1)
    other = theirs[-16, :count].astype(jnp.int32)
    out_far = swap(after(out_turned, (far, near)), "dp", 4)
    out_far_y, out_last = swap(out_far, "dp", 1), swap(after(out_far, last), "dp", 2)
    blocks = [heads, near, far, last, beside, corner, far_y, last_y]
    out_blocks = [heads, near, out_far, out_last, beside, corner, out_far_y]
    out_blocks += [swap(out_last, "dp", 1)]

    marks = jnp.pad(segments.astype(bf16), ((0, 15), (0, width - rows)))
    marked = after(jnp.concatenate([tokens, marks], axis=0), heads)
    along_x = swap(marked, "fsdp", 2)
    group_rows = [marked, along_x]
    group_rows += [swap(after(part, (far_y, last, theirs, out_far)), "fsdp", 1) for part in (marked, along_x)]
    (normed,) = call(norm_kernel, [shape((group, width), bf16)], [ln_gains, *group_rows])

    pair = jnp.concatenate([jnp.where(lower, low, high), theirs[:-16]], axis=0)
    held = after(pair, (last, out_last))
    merge_near, merge_far = swap(held, "dp", 2), swap(held, "dp", 4)

    capacity = max(2, (2 * count + n_dp - 1) // n_dp)
    slots = []
    for number, targets in enumerate((mine, other)):
        start, rank = slot_numbers(targets, 2 * capacity)
        slots.append(start + rank + (y ^ number) * capacity)
    slots = jnp.concatenate(slots).reshape(1, 2 * count)
    order = merge_rows.reshape(count, 4).T.reshape(rows, 1)

    attended, send = call(
        attention_kernel,
        [shape((2 * rows, cols), bf16), shape((2 * rows, width), bf16)],
        [after(me_cell, pair), normed, *group_rows, *blocks, *out_blocks],
        [pltpu.VMEM((width, cols), bf16)] * 4,
        flops=8 * group * width * cols + 4 * group * group * cols,
        smem=1,
        exps=cols // HD * group * group,
    )
    from_core = swap(send, "fsdp", 1)
    (keep,) = call(
        keep_kernel,
        [shape((2 * rows, width), f32)],
        [me_cell, attended, *out_blocks],
        [pltpu.VMEM((width, cols), bf16)],
        flops=4 * rows * width * cols,
        smem=1,
    )
    (onward,) = call(pass_kernel, [shape((rows, width), bf16)], [keep, from_core])
    from_chip = swap(onward, "fsdp", 2)
    (slices,) = call(
        layer_kernel,
        [shape((8, rows // 2, width // 2), bf16)],
        [marked, keep, from_core, from_chip, ln_gains, order],
        flops=2 * rows * rows * width,
    )
    merge_blocks = [pair, merge_near, merge_far, swap(after(merge_far, (slices, merge_near)), "dp", 2)]
    both = 2 * n_fsdp
    inputs = lax.all_to_all(
        slices,
        ("dp", "fsdp"),
        split_axis=0,
        concat_axis=0,
        tiled=True,
        axis_index_groups=[
            list(range(i, i + both)) for i in range(0, n_dp * n_fsdp, both)
        ],
    )
    shares = call(
        merge_kernel,
        [shape((2 * count, half), f32)] + [shape((2 * count, half), bf16)] * 3,
        [me_cell, at_cell, inputs, *merge_blocks],
        [pltpu.VMEM((8, count, half), f32)],
        flops=2 * 8 * count * width * half,
        smem=2,
    )
    got = [swap(shares[k], "fsdp", k) for k in range(1, 4)]
    (packed,) = call(
        pack_kernel,
        [shape((n_dp * 2 * capacity, half), bf16)],
        [slots, shares[0], *got],
        flops=2 * n_dp * 2 * capacity * 2 * count * half,
    )
    arrived = lax.all_to_all(
        packed.reshape(n_dp, 2 * capacity, half), "dp", split_axis=0, concat_axis=0, tiled=True
    )
    arrived = arrived.reshape(n_dp // 2, 2, 2, capacity, half).transpose(0, 2, 3, 1, 4)
    return arrived.reshape(n_dp * capacity, 2 * half)


def solution(mesh):
    small = mesh.shape["dp"] == 8 and mesh.shape["fsdp"] == 4
    return jax.shard_map(
        by_permutes if small else by_gathers,
        mesh=mesh,
        in_specs=(
            P(("dp", "fsdp"), None),
            P(None, "dp", "fsdp"),
            P("fsdp", "dp"),
            P(("dp", "fsdp"), None),
            P(),
            P("dp", "fsdp"),
            P(("dp", "fsdp"), None),
            P(("dp", "fsdp"), None),
        ),
        out_specs=P(("dp", "fsdp"), None),
        check_vma=False,
    )
```

```python
import functools
import math

import jax
import jax.numpy as jnp
from jax import lax
from jax.experimental import pallas as pl
from jax.experimental.pallas import tpu as pltpu
from jax.sharding import PartitionSpec as P

HD = 80


epsilon = 1e-06


def normalize(values_in, gain_row):
    widened = values_in.astype(jnp.float32)
    centered = widened - jnp.mean(widened, axis=1, keepdims=True)
    variance = jnp.mean(centered * centered, axis=1, keepdims=True)
    return (centered * lax.rsqrt(variance + epsilon) * gain_row).astype(jnp.bfloat16)


def attend(queries, keys_all, values_all, seg_rows, seg_cols):
    factor = 1.0 / math.sqrt(HD)
    allowed = seg_rows[:, None] == seg_cols[None, :]
    pieces = []
    for head_index in range(queries.shape[1] // HD):
        first_col = head_index * HD
        last_col = first_col + HD
        scores = (
            lax.dot_general(
                queries[:, first_col:last_col],
                keys_all[:, first_col:last_col],
                (((1,), (1,)), ((), ())),
                preferred_element_type=jnp.float32,
            )
            * factor
        )
        masked = jnp.where(allowed, scores, -jnp.inf)
        highest = jnp.max(masked, axis=1, keepdims=True)
        weights = jnp.exp(masked - highest)
        totals = jnp.sum(weights, axis=1, keepdims=True)
        head_out = jnp.dot(
            weights.astype(jnp.bfloat16),
            values_all[:, first_col:last_col],
            preferred_element_type=jnp.float32,
        )
        pieces.append(head_out / totals)
    return jnp.concatenate(pieces, axis=1).astype(jnp.bfloat16)


def slot_numbers(targets, capacity):
    n = targets.shape[0]
    same = targets[:, None] == targets[None, :]
    before = jnp.arange(n)[None, :] < jnp.arange(n)[:, None]
    return targets * capacity, jnp.sum((same & before).astype(jnp.int32), axis=1)


def by_gathers(
    tokens, qkv_weight, out_weight, merge_weight, ln_gains, segments, merge_rows, owners
):
    n_dp = lax.axis_size("dp")
    qkv_mine = lax.all_gather(qkv_weight, "dp", axis=1, tiled=True)
    out_mine = lax.all_gather(out_weight, "dp", axis=1, tiled=True)
    n_fsdp = lax.axis_size("fsdp")
    normed = normalize(tokens, ln_gains[0])
    group_normed = lax.all_gather(normed, "fsdp", axis=0, tiled=True)
    group_segs = lax.all_gather(segments, "fsdp", axis=1, tiled=True)
    queries, keys_all, values_all = (
        jnp.dot(group_normed, qkv_mine[n], preferred_element_type=jnp.float32).astype(jnp.bfloat16)
        for n in range(3)
    )
    attended_mine = attend(queries, keys_all, values_all, group_segs[0], group_segs[0])
    attended_local = lax.all_to_all(attended_mine, "fsdp", split_axis=0, concat_axis=1, tiled=True)
    out_full = lax.all_gather(out_mine, "fsdp", axis=0, tiled=True)
    update = jnp.dot(attended_local, out_full, preferred_element_type=jnp.float32)
    layer_out = (tokens.astype(jnp.float32) + update).astype(jnp.bfloat16)
    merge_in = normalize(layer_out, ln_gains[1])
    merge_count = tokens.shape[0] // 4
    stacked = jnp.take(merge_in, merge_rows[0], axis=0).reshape(merge_count, 4 * merge_in.shape[1])
    slice_rows = merge_weight.shape[0]
    part_rows = lax.all_gather(merge_weight, "dp", axis=0, tiled=True)
    blocks = stacked.reshape(merge_count, n_dp, n_fsdp * slice_rows)
    received = lax.all_to_all(blocks, "fsdp", split_axis=2, concat_axis=0, tiled=True)
    gathered_inputs = received.reshape(n_fsdp * merge_count, n_dp * slice_rows)
    merged = lax.psum_scatter(
        jnp.dot(gathered_inputs, part_rows, preferred_element_type=jnp.float32).astype(
            jnp.bfloat16
        ),
        "fsdp",
        scatter_dimension=0,
        tiled=True,
    )
    capacity = max(2, (2 * merge_count + n_dp - 1) // n_dp)
    first, rank = slot_numbers(owners[:, 0], capacity)
    placing = (
        jnp.arange(n_dp * capacity, dtype=jnp.int32)[:, None] == (first + rank)[None, :]
    ).astype(jnp.bfloat16)
    packed = jnp.dot(placing, merged, preferred_element_type=jnp.float32).astype(jnp.bfloat16)
    packed = packed.reshape(n_dp, capacity, merged.shape[1])
    arrived = lax.all_to_all(packed, "dp", split_axis=0, concat_axis=0, tiled=True)
    return arrived.reshape(n_dp * capacity, merged.shape[1])


def swap(value, axis, k):
    return lax.ppermute(value, axis, [(i, i ^ k) for i in range(lax.axis_size(axis))])


def after(value, other):
    return lax.optimization_barrier((value, other))[0]


ORDER = (0, 2, 4, 6, 1, 3, 5, 7)


def dot(a, b):
    return jnp.dot(a, b, preferred_element_type=jnp.float32)


def dot_turned(a, b):
    return lax.dot_general(a, b, (((1,), (1,)), ((), ())), preferred_element_type=jnp.float32)


def call(kernel, outs, operands, scratch=(), flops=0, smem=0, exps=0, moved=None):
    moved = moved or sum(math.prod(x.shape) * x.dtype.itemsize for x in (*operands, *outs))
    specs = [pl.BlockSpec(memory_space=pltpu.SMEM)] * smem
    specs += [pl.BlockSpec(memory_space=pltpu.VMEM)] * (len(operands) - smem)
    return pl.pallas_call(
        kernel,
        out_shape=tuple(outs),
        in_specs=specs,
        out_specs=tuple(pl.BlockSpec(memory_space=pltpu.VMEM) for _ in outs),
        scratch_shapes=list(scratch),
        compiler_params=pltpu.CompilerParams(vmem_limit_bytes=16 * 1024 * 1024),
        cost_estimate=pl.CostEstimate(
            flops=flops, bytes_accessed=moved, transcendentals=exps
        ),
    )(*operands)


def norm_kernel(gains_ref, *refs):
    tokens, out_ref = refs[0:4], refs[4]
    rows = tokens[0].shape[0] - 16
    for n in range(4):
        out_ref[n * rows : (n + 1) * rows, :] = normalize(tokens[n][0:rows, :], gains_ref[0:1, :])


def lay_out(me, blocks, part, whole):
    step = blocks[0].shape[1]
    for number, block in zip(ORDER, blocks):
        start = pl.multiple_of((me ^ number) * step, 32)
        whole[pl.ds(start, step), :] = block[part if block.shape[0] == 4 else part % 2]


def score_kernel(me_ref, rows_ref, *refs):
    marks, blocks = refs[0:4], refs[4:12]
    weights_ref, totals_ref, q_whole, k_whole = refs[12:]
    lay_out(me_ref[0], blocks, 0, q_whole)
    lay_out(me_ref[0], blocks, 1, k_whole)
    queries = dot(rows_ref[...], q_whole[...]).astype(jnp.bfloat16)
    keys = dot(rows_ref[...], k_whole[...]).astype(jnp.bfloat16)
    rows = marks[0].shape[0] - 16
    in_row = [t[rows : rows + 16, 0:rows].astype(jnp.float32)[0:1, :] for t in marks]
    in_col = [jnp.broadcast_to(s, (rows, rows)).T[:, 0:1] for s in in_row]
    allowed = jnp.concatenate(in_col, axis=0) == jnp.concatenate(in_row, axis=1)
    factor = 1.0 / math.sqrt(HD)
    for head in range(queries.shape[1] // HD):
        cols = slice(head * HD, (head + 1) * HD)
        scores = dot_turned(queries[:, cols], keys[:, cols]) * factor
        masked = jnp.where(allowed, scores, -jnp.inf)
        weights = jnp.exp(masked - jnp.max(masked, axis=1, keepdims=True))
        weights_ref[head] = weights.astype(jnp.bfloat16)
        totals_ref[head] = jnp.sum(weights, axis=1, keepdims=True)


def value_kernel(me_ref, rows_ref, weights_ref, totals_ref, *refs):
    blocks = refs[0:8]
    keep_ref, send_near, send_far, v_whole, out_whole = refs[8:]
    lay_out(me_ref[0], blocks, 2, v_whole)
    lay_out(me_ref[0], blocks, 3, out_whole)
    values = dot(rows_ref[...], v_whole[...]).astype(jnp.bfloat16)
    pieces = []
    for head in range(values.shape[1] // HD):
        found = dot(weights_ref[head], values[:, head * HD : (head + 1) * HD])
        pieces.append(found / totals_ref[head])
    attended = jnp.concatenate(pieces, axis=1).astype(jnp.bfloat16)
    half = attended.shape[0] // 2
    sent = dot_turned(attended[half:, :], out_whole[...]).astype(jnp.bfloat16)
    send_near[...], send_far[...] = sent[: half // 2, :], sent[half // 2 :, :]
    keep_ref[...] = dot_turned(attended[:half, :], out_whole[...])


def pass_kernel(keep_ref, got_ref, *outs):
    rows, parts = got_ref.shape[0], len(outs)
    step = rows // parts
    for n, out_ref in enumerate(outs):
        kept = keep_ref[rows + n * step : rows + (n + 1) * step, :]
        got = got_ref[n * step : (n + 1) * step, :].astype(jnp.float32)
        out_ref[...] = (kept + got).astype(jnp.bfloat16)


def layer_kernel(tokens_ref, keep_ref, core_ref, gains_ref, order_ref, *refs):
    chips, slices = refs[:-1], refs[-1]
    rows, width = tokens_ref.shape[0] - 16, tokens_ref.shape[1]
    summed = (
        tokens_ref[0:rows, :].astype(jnp.float32)
        + keep_ref[0:rows, :]
        + core_ref[0:rows, :].astype(jnp.float32)
        + jnp.concatenate([ref[...] for ref in chips], axis=0).astype(jnp.float32)
    )
    merge_in = normalize(summed.astype(jnp.bfloat16), gains_ref[1:2, :])
    places = lax.broadcasted_iota(jnp.int32, (rows, rows), 1)
    picking = (order_ref[...] == places).astype(jnp.bfloat16)
    ordered = dot(picking, merge_in).astype(jnp.bfloat16)
    step, half = width // 8, width // 2
    for n in range(4):
        part = jnp.concatenate(
            [
                ordered[:, n * step : (n + 1) * step],
                ordered[:, half + n * step : half + (n + 1) * step],
            ],
            axis=1,
        )
        part = jnp.concatenate([part[: rows // 2, :], part[rows // 2 :, :]], axis=1)
        slices[n] = part
        slices[4 + n] = part


def merge_kernel(me_ref, at_ref, inputs, *refs):
    blocks, (keep_ref, *sends), total = refs[0:4], refs[4:8], refs[8]
    count, width = inputs.shape[1] // 2, inputs.shape[2] // 2
    z, y = me_ref[0] // 2, lax.rem(me_ref[0], 2)
    for number in range(4):
        position = z ^ number
        at = pl.multiple_of(lax.rem(position, 2) * count, 32)
        rows = inputs[:, pl.ds(at, count), :].reshape(8 * count, 2 * width)
        rows = jnp.where(position < 2, rows[:, :width], rows[:, width:])
        step = blocks[number].shape[0] // 2
        own, other = blocks[number][:step, :], blocks[number][step:, :]
        block = jnp.concatenate(
            [jnp.where(y == 0, own, other), jnp.where(y == 0, other, own)], axis=0
        )
        found = dot(rows, block).reshape(total.shape)
        total[...] = found if number == 0 else total[...] + found
    for k in range(4):
        to = at_ref[0] ^ k
        share = jnp.concatenate([total[4 * y + to], total[4 * (1 - y) + to]], axis=0)
        if k == 0:
            keep_ref[...] = share
        else:
            sends[k - 1][...] = share.astype(jnp.bfloat16)


def pack_kernel(slots_ref, keep_ref, one_ref, two_ref, three_ref, out_ref):
    total = keep_ref[...]
    for got in (one_ref, two_ref, three_ref):
        total = total + got[...].astype(jnp.float32)
    shape = (out_ref.shape[0], total.shape[0])
    placing = (lax.broadcasted_iota(jnp.int32, shape, 0) == slots_ref[...]).astype(jnp.bfloat16)
    out_ref[...] = dot(placing, total.astype(jnp.bfloat16)).astype(jnp.bfloat16)


def by_permutes(
    tokens, qkv_weight, out_weight, merge_weight, ln_gains, segments, merge_rows, owners
):
    rows, width = tokens.shape
    count = rows // 4
    n_dp, n_fsdp = lax.axis_size("dp"), lax.axis_size("fsdp")
    me, at = lax.axis_index("dp"), lax.axis_index("fsdp")
    y = lax.rem(me, 2)
    me_cell, at_cell = me.reshape(1), at.reshape(1)
    bf16, f32 = jnp.bfloat16, jnp.float32
    shape = jax.ShapeDtypeStruct
    cols = qkv_weight.shape[2]
    group = n_fsdp * rows

    heads = jnp.concatenate([qkv_weight, out_weight.T[None]], axis=0)
    near, beside = swap(heads, "dp", 2), swap(heads, "dp", 1)
    first, second = heads[0:2], heads[2:4]
    first_far = swap(first, "dp", 4)
    half = merge_weight.shape[1] // 2
    low, high = merge_weight[:, :half], merge_weight[:, half:]
    lower = y == 0
    mine = owners[:, 0]
    note = jnp.pad(owners.astype(bf16).T, ((0, 15), (0, half - count)))
    given = jnp.concatenate([jnp.where(lower, high, low), note], axis=0)
    theirs = swap(after(given, first), "dp", 1)
    other = theirs[-16, :count].astype(jnp.int32)
    first_far_y = swap(after(first_far, (near, beside, theirs)), "dp", 1)
    first_last = swap(first_far, "dp", 2)
    corner = swap(beside, "dp", 2)
    second_far = swap(after(second, first_far), "dp", 4)

    marks = jnp.pad(segments.astype(bf16), ((0, 15), (0, width - rows)))
    marked = after(jnp.concatenate([tokens, marks], axis=0), first)
    along_x = swap(marked, "fsdp", 2)
    group_rows = [marked, along_x]
    group_rows += [swap(after(part, (first_far_y, first_last, second_far)), "fsdp", 1) for part in (marked, along_x)]
    (normed,) = call(norm_kernel, [shape((group, width), bf16)], [ln_gains, *group_rows])

    second_far_y = swap(second_far, "dp", 1)
    second_last = swap(second_far, "dp", 2)
    blocks = [
        [heads, near, far, last, beside, corner, far_y, swap(after(last, corner), "dp", 1)]
        for far, last, far_y in (
            (first_far, first_last, first_far_y),
            (second_far, second_last, second_far_y),
        )
    ]

    pair = jnp.concatenate([jnp.where(lower, low, high), theirs[:-16]], axis=0)
    held = after(pair, (second_last, second_far_y, blocks[0][7]))
    merge_near, merge_far = swap(held, "dp", 2), swap(held, "dp", 4)

    capacity = max(2, (2 * count + n_dp - 1) // n_dp)
    slots = []
    for number, targets in enumerate((mine, other)):
        start, rank = slot_numbers(targets, 2 * capacity)
        slots.append(start + rank + (y ^ number) * capacity)
    slots = jnp.concatenate(slots).reshape(1, 2 * count)
    order = merge_rows.reshape(count, 4).T.reshape(rows, 1)

    found = cols // HD
    weights, totals = call(
        score_kernel,
        [shape((found, group, group), bf16), shape((found, group, 1), f32)],
        [after(me_cell, theirs), normed, *group_rows, *blocks[0]],
        [pltpu.VMEM((width, cols), bf16)] * 2,
        flops=4 * group * width * cols + 2 * group * group * cols,
        smem=1,
        exps=found * group * group,
    )
    keep, *send = call(
        value_kernel,
        [shape((2 * rows, width), f32)] + [shape((rows, width), bf16)] * 2,
        [me_cell, normed, weights, totals, *blocks[1]],
        [pltpu.VMEM((width, cols), bf16)] * 2,
        flops=4 * group * width * cols + 2 * group * group * cols,
        smem=1,
    )
    from_core = [swap(part, "fsdp", 1) for part in send]
    parts = 2
    onward = call(
        pass_kernel, [shape((rows // parts, width), bf16)] * parts, [keep, from_core[1]], moved=1
    )
    from_chip = [swap(part, "fsdp", 2) for part in onward]
    (slices,) = call(
        layer_kernel,
        [shape((8, rows // 2, width // 2), bf16)],
        [marked, keep, from_core[0], ln_gains, order, *from_chip],
        moved=1,
    )
    merge_blocks = [pair, merge_near, merge_far, swap(after(merge_far, (slices, merge_near)), "dp", 2)]
    both = 2 * n_fsdp
    inputs = lax.all_to_all(
        slices,
        ("dp", "fsdp"),
        split_axis=0,
        concat_axis=0,
        tiled=True,
        axis_index_groups=[
            list(range(i, i + both)) for i in range(0, n_dp * n_fsdp, both)
        ],
    )
    shares = call(
        merge_kernel,
        [shape((2 * count, half), f32)] + [shape((2 * count, half), bf16)] * 3,
        [me_cell, at_cell, inputs, *merge_blocks],
        [pltpu.VMEM((8, count, half), f32)],
        flops=2 * 8 * count * width * half,
        smem=2,
    )
    got = [swap(shares[k], "fsdp", k) for k in range(1, 4)]
    (packed,) = call(
        pack_kernel,
        [shape((n_dp * 2 * capacity, half), bf16)],
        [slots, shares[0], *got],
        flops=2 * n_dp * 2 * capacity * 2 * count * half,
    )
    arrived = lax.all_to_all(
        packed.reshape(n_dp, 2 * capacity, half), "dp", split_axis=0, concat_axis=0, tiled=True
    )
    arrived = arrived.reshape(n_dp // 2, 2, 2, capacity, half).transpose(0, 2, 3, 1, 4)
    return arrived.reshape(n_dp * capacity, 2 * half)


def solution(mesh):
    small = mesh.shape["dp"] == 8 and mesh.shape["fsdp"] == 4
    return jax.shard_map(
        by_permutes if small else by_gathers,
        mesh=mesh,
        in_specs=(
            P(("dp", "fsdp"), None),
            P(None, "dp", "fsdp"),
            P("fsdp", "dp"),
            P(("dp", "fsdp"), None),
            P(),
            P("dp", "fsdp"),
            P(("dp", "fsdp"), None),
            P(("dp", "fsdp"), None),
        ),
        out_specs=P(("dp", "fsdp"), None),
        check_vma=False,
    )
```

```python
import functools
import math

import jax
import jax.numpy as jnp
from jax import lax
from jax.experimental import pallas as pl
from jax.experimental.pallas import tpu as pltpu
from jax.sharding import PartitionSpec as P

HD = 80


epsilon = 1e-06


def normalize(values_in, gain_row):
    widened = values_in.astype(jnp.float32)
    centered = widened - jnp.mean(widened, axis=1, keepdims=True)
    variance = jnp.mean(centered * centered, axis=1, keepdims=True)
    return (centered * lax.rsqrt(variance + epsilon) * gain_row).astype(jnp.bfloat16)


def attend(queries, keys_all, values_all, seg_rows, seg_cols):
    factor = 1.0 / math.sqrt(HD)
    allowed = seg_rows[:, None] == seg_cols[None, :]
    pieces = []
    for head_index in range(queries.shape[1] // HD):
        first_col = head_index * HD
        last_col = first_col + HD
        scores = (
            lax.dot_general(
                queries[:, first_col:last_col],
                keys_all[:, first_col:last_col],
                (((1,), (1,)), ((), ())),
                preferred_element_type=jnp.float32,
            )
            * factor
        )
        masked = jnp.where(allowed, scores, -jnp.inf)
        highest = jnp.max(masked, axis=1, keepdims=True)
        weights = jnp.exp(masked - highest)
        totals = jnp.sum(weights, axis=1, keepdims=True)
        head_out = jnp.dot(
            weights.astype(jnp.bfloat16),
            values_all[:, first_col:last_col],
            preferred_element_type=jnp.float32,
        )
        pieces.append(head_out / totals)
    return jnp.concatenate(pieces, axis=1).astype(jnp.bfloat16)


def slot_numbers(targets, capacity):
    n = targets.shape[0]
    same = targets[:, None] == targets[None, :]
    before = jnp.arange(n)[None, :] < jnp.arange(n)[:, None]
    return targets * capacity, jnp.sum((same & before).astype(jnp.int32), axis=1)


def by_gathers(
    tokens, qkv_weight, out_weight, merge_weight, ln_gains, segments, merge_rows, owners
):
    n_dp = lax.axis_size("dp")
    qkv_mine = lax.all_gather(qkv_weight, "dp", axis=1, tiled=True)
    out_mine = lax.all_gather(out_weight, "dp", axis=1, tiled=True)
    n_fsdp = lax.axis_size("fsdp")
    normed = normalize(tokens, ln_gains[0])
    group_normed = lax.all_gather(normed, "fsdp", axis=0, tiled=True)
    group_segs = lax.all_gather(segments, "fsdp", axis=1, tiled=True)
    queries, keys_all, values_all = (
        jnp.dot(group_normed, qkv_mine[n], preferred_element_type=jnp.float32).astype(jnp.bfloat16)
        for n in range(3)
    )
    attended_mine = attend(queries, keys_all, values_all, group_segs[0], group_segs[0])
    attended_local = lax.all_to_all(attended_mine, "fsdp", split_axis=0, concat_axis=1, tiled=True)
    out_full = lax.all_gather(out_mine, "fsdp", axis=0, tiled=True)
    update = jnp.dot(attended_local, out_full, preferred_element_type=jnp.float32)
    layer_out = (tokens.astype(jnp.float32) + update).astype(jnp.bfloat16)
    merge_in = normalize(layer_out, ln_gains[1])
    merge_count = tokens.shape[0] // 4
    stacked = jnp.take(merge_in, merge_rows[0], axis=0).reshape(merge_count, 4 * merge_in.shape[1])
    slice_rows = merge_weight.shape[0]
    part_rows = lax.all_gather(merge_weight, "dp", axis=0, tiled=True)
    blocks = stacked.reshape(merge_count, n_dp, n_fsdp * slice_rows)
    received = lax.all_to_all(blocks, "fsdp", split_axis=2, concat_axis=0, tiled=True)
    gathered_inputs = received.reshape(n_fsdp * merge_count, n_dp * slice_rows)
    merged = lax.psum_scatter(
        jnp.dot(gathered_inputs, part_rows, preferred_element_type=jnp.float32).astype(
            jnp.bfloat16
        ),
        "fsdp",
        scatter_dimension=0,
        tiled=True,
    )
    capacity = max(2, (2 * merge_count + n_dp - 1) // n_dp)
    first, rank = slot_numbers(owners[:, 0], capacity)
    placing = (
        jnp.arange(n_dp * capacity, dtype=jnp.int32)[:, None] == (first + rank)[None, :]
    ).astype(jnp.bfloat16)
    packed = jnp.dot(placing, merged, preferred_element_type=jnp.float32).astype(jnp.bfloat16)
    packed = packed.reshape(n_dp, capacity, merged.shape[1])
    arrived = lax.all_to_all(packed, "dp", split_axis=0, concat_axis=0, tiled=True)
    return arrived.reshape(n_dp * capacity, merged.shape[1])


def swap(value, axis, k):
    return lax.ppermute(value, axis, [(i, i ^ k) for i in range(lax.axis_size(axis))])


def after(value, other):
    return lax.optimization_barrier((value, other))[0]


ORDER = (0, 2, 4, 6, 1, 3, 5, 7)


def dot(a, b):
    return jnp.dot(a, b, preferred_element_type=jnp.float32)


def dot_turned(a, b):
    return lax.dot_general(a, b, (((1,), (1,)), ((), ())), preferred_element_type=jnp.float32)


def call(kernel, outs, operands, scratch=(), flops=0, smem=0, exps=0, moved=None):
    moved = moved or sum(math.prod(x.shape) * x.dtype.itemsize for x in (*operands, *outs))
    specs = [pl.BlockSpec(memory_space=pltpu.SMEM)] * smem
    specs += [pl.BlockSpec(memory_space=pltpu.VMEM)] * (len(operands) - smem)
    return pl.pallas_call(
        kernel,
        out_shape=tuple(outs),
        in_specs=specs,
        out_specs=tuple(pl.BlockSpec(memory_space=pltpu.VMEM) for _ in outs),
        scratch_shapes=list(scratch),
        compiler_params=pltpu.CompilerParams(vmem_limit_bytes=16 * 1024 * 1024),
        cost_estimate=pl.CostEstimate(
            flops=flops, bytes_accessed=moved, transcendentals=exps
        ),
    )(*operands)


def norm_kernel(gains_ref, *refs):
    tokens, out_ref = refs[0:4], refs[4]
    rows = tokens[0].shape[0] - 16
    for n in range(4):
        out_ref[n * rows : (n + 1) * rows, :] = normalize(tokens[n][0:rows, :], gains_ref[0:1, :])


def lay_out(me, blocks, part, whole):
    step = blocks[0].shape[1]
    for number, block in zip(ORDER, blocks):
        start = pl.multiple_of((me ^ number) * step, 32)
        whole[pl.ds(start, step), :] = block[part if block.shape[0] == 4 else part % 2]


def score_kernel(me_ref, rows_ref, *refs):
    marks, blocks = refs[0:4], refs[4:12]
    weights_ref, totals_ref, q_whole, k_whole = refs[12:]
    lay_out(me_ref[0], blocks, 0, q_whole)
    lay_out(me_ref[0], blocks, 1, k_whole)
    queries = dot(rows_ref[...], q_whole[...]).astype(jnp.bfloat16)
    keys = dot(rows_ref[...], k_whole[...]).astype(jnp.bfloat16)
    rows = marks[0].shape[0] - 16
    in_row = [t[rows : rows + 16, 0:rows].astype(jnp.float32)[0:1, :] for t in marks]
    in_col = [jnp.broadcast_to(s, (rows, rows)).T[:, 0:1] for s in in_row]
    allowed = jnp.concatenate(in_col, axis=0) == jnp.concatenate(in_row, axis=1)
    factor = 1.0 / math.sqrt(HD)
    for head in range(queries.shape[1] // HD):
        cols = slice(head * HD, (head + 1) * HD)
        scores = dot_turned(queries[:, cols], keys[:, cols]) * factor
        masked = jnp.where(allowed, scores, -jnp.inf)
        weights = jnp.exp(masked - jnp.max(masked, axis=1, keepdims=True))
        weights_ref[head] = weights.astype(jnp.bfloat16)
        totals_ref[head] = jnp.sum(weights, axis=1, keepdims=True)


def value_kernel(me_ref, rows_ref, weights_ref, totals_ref, *refs):
    blocks = refs[0:8]
    keep_ref, send_near, send_far, v_whole, out_whole = refs[8:]
    lay_out(me_ref[0], blocks, 2, v_whole)
    lay_out(me_ref[0], blocks, 3, out_whole)
    values = dot(rows_ref[...], v_whole[...]).astype(jnp.bfloat16)
    pieces = []
    for head in range(values.shape[1] // HD):
        found = dot(weights_ref[head], values[:, head * HD : (head + 1) * HD])
        pieces.append(found / totals_ref[head])
    attended = jnp.concatenate(pieces, axis=1).astype(jnp.bfloat16)
    half = attended.shape[0] // 2
    sent = dot_turned(attended[half:, :], out_whole[...]).astype(jnp.bfloat16)
    send_near[...], send_far[...] = sent[: half // 2, :], sent[half // 2 :, :]
    keep_ref[...] = dot_turned(attended[:half, :], out_whole[...])


def pass_kernel(keep_ref, got_ref, *outs):
    rows, parts = got_ref.shape[0], len(outs)
    step = rows // parts
    for n, out_ref in enumerate(outs):
        kept = keep_ref[rows + n * step : rows + (n + 1) * step, :]
        got = got_ref[n * step : (n + 1) * step, :].astype(jnp.float32)
        out_ref[...] = (kept + got).astype(jnp.bfloat16)


def layer_kernel(tokens_ref, keep_ref, core_ref, gains_ref, order_ref, *refs):
    chips, slices = refs[:-1], refs[-1]
    rows, width = tokens_ref.shape[0] - 16, tokens_ref.shape[1]
    summed = (
        tokens_ref[0:rows, :].astype(jnp.float32)
        + keep_ref[0:rows, :]
        + core_ref[0:rows, :].astype(jnp.float32)
        + jnp.concatenate([ref[...] for ref in chips], axis=0).astype(jnp.float32)
    )
    merge_in = normalize(summed.astype(jnp.bfloat16), gains_ref[1:2, :])
    places = lax.broadcasted_iota(jnp.int32, (rows, rows), 1)
    picking = (order_ref[...] == places).astype(jnp.bfloat16)
    ordered = dot(picking, merge_in).astype(jnp.bfloat16)
    step, half = width // 8, width // 2
    for n in range(4):
        part = jnp.concatenate(
            [
                ordered[:, n * step : (n + 1) * step],
                ordered[:, half + n * step : half + (n + 1) * step],
            ],
            axis=1,
        )
        part = jnp.concatenate([part[: rows // 2, :], part[rows // 2 :, :]], axis=1)
        slices[n] = part
        slices[4 + n] = part


def merge_kernel(me_ref, at_ref, inputs, *refs):
    blocks, (keep_ref, *sends), total = refs[0:4], refs[4:8], refs[8]
    count, width = inputs.shape[1] // 2, inputs.shape[2] // 2
    z, y = me_ref[0] // 2, lax.rem(me_ref[0], 2)
    for number in range(4):
        position = z ^ number
        at = pl.multiple_of(lax.rem(position, 2) * count, 32)
        rows = inputs[:, pl.ds(at, count), :].reshape(8 * count, 2 * width)
        rows = jnp.where(position < 2, rows[:, :width], rows[:, width:])
        step = blocks[number].shape[0] // 2
        own, other = blocks[number][:step, :], blocks[number][step:, :]
        block = jnp.concatenate(
            [jnp.where(y == 0, own, other), jnp.where(y == 0, other, own)], axis=0
        )
        found = dot(rows, block).reshape(total.shape)
        total[...] = found if number == 0 else total[...] + found
    for k in range(4):
        to = at_ref[0] ^ k
        share = jnp.concatenate([total[4 * y + to], total[4 * (1 - y) + to]], axis=0)
        if k == 0:
            keep_ref[...] = share
        else:
            sends[k - 1][...] = share.astype(jnp.bfloat16)


def pack_kernel(slots_ref, keep_ref, one_ref, two_ref, three_ref, out_ref):
    total = keep_ref[...]
    for got in (one_ref, two_ref, three_ref):
        total = total + got[...].astype(jnp.float32)
    shape = (out_ref.shape[0], total.shape[0])
    placing = (lax.broadcasted_iota(jnp.int32, shape, 0) == slots_ref[...]).astype(jnp.bfloat16)
    out_ref[...] = dot(placing, total.astype(jnp.bfloat16)).astype(jnp.bfloat16)


def by_permutes(
    tokens, qkv_weight, out_weight, merge_weight, ln_gains, segments, merge_rows, owners
):
    rows, width = tokens.shape
    count = rows // 4
    n_dp, n_fsdp = lax.axis_size("dp"), lax.axis_size("fsdp")
    me, at = lax.axis_index("dp"), lax.axis_index("fsdp")
    y = lax.rem(me, 2)
    me_cell, at_cell = me.reshape(1), at.reshape(1)
    bf16, f32 = jnp.bfloat16, jnp.float32
    shape = jax.ShapeDtypeStruct
    cols = qkv_weight.shape[2]
    group = n_fsdp * rows

    heads = jnp.concatenate([qkv_weight, out_weight.T[None]], axis=0)
    near, beside = swap(heads, "dp", 2), swap(heads, "dp", 1)
    first, second = heads[0:2], heads[2:4]
    first_far = swap(first, "dp", 4)
    first_far_y = swap(after(first_far, (near, beside)), "dp", 1)
    first_last = swap(first_far, "dp", 2)
    corner = swap(after(beside, first_last), "dp", 2)
    second_far = swap(after(second, first_far), "dp", 4)

    marks = jnp.pad(segments.astype(bf16), ((0, 15), (0, width - rows)))
    marked = after(jnp.concatenate([tokens, marks], axis=0), first)
    along_x = swap(marked, "fsdp", 2)
    group_rows = [marked, along_x]
    group_rows += [swap(after(part, (first_far_y, first_last, second_far)), "fsdp", 1) for part in (marked, along_x)]
    (normed,) = call(norm_kernel, [shape((group, width), bf16)], [ln_gains, *group_rows])

    second_far_y = swap(second_far, "dp", 1)
    second_last = swap(second_far, "dp", 2)
    blocks = [
        [heads, near, far, last, beside, corner, far_y, swap(after(last, corner), "dp", 1)]
        for far, last, far_y in (
            (first_far, first_last, first_far_y),
            (second_far, second_last, second_far_y),
        )
    ]

    half = merge_weight.shape[1] // 2
    low, high = merge_weight[:, :half], merge_weight[:, half:]
    lower = y == 0
    mine = owners[:, 0]
    note = jnp.pad(owners.astype(bf16).T, ((0, 15), (0, half - count)))
    given = jnp.concatenate([jnp.where(lower, high, low), note], axis=0)
    theirs = swap(after(given, second_far_y), "dp", 1)
    other = theirs[-16, :count].astype(jnp.int32)
    pair = jnp.concatenate([jnp.where(lower, low, high), theirs[:-16]], axis=0)
    held = after(pair, (second_last, second_far_y, blocks[0][7]))
    merge_near, merge_far = swap(held, "dp", 2), swap(held, "dp", 4)

    capacity = max(2, (2 * count + n_dp - 1) // n_dp)
    slots = []
    for number, targets in enumerate((mine, other)):
        start, rank = slot_numbers(targets, 2 * capacity)
        slots.append(start + rank + (y ^ number) * capacity)
    slots = jnp.concatenate(slots).reshape(1, 2 * count)
    order = merge_rows.reshape(count, 4).T.reshape(rows, 1)

    found = cols // HD
    weights, totals = call(
        score_kernel,
        [shape((found, group, group), bf16), shape((found, group, 1), f32)],
        [after(me_cell, theirs), normed, *group_rows, *blocks[0]],
        [pltpu.VMEM((width, cols), bf16)] * 2,
        flops=4 * group * width * cols + 2 * group * group * cols,
        smem=1,
        exps=found * group * group,
    )
    keep, *send = call(
        value_kernel,
        [shape((2 * rows, width), f32)] + [shape((rows, width), bf16)] * 2,
        [me_cell, normed, weights, totals, *blocks[1]],
        [pltpu.VMEM((width, cols), bf16)] * 2,
        flops=4 * group * width * cols + 2 * group * group * cols,
        smem=1,
    )
    from_core = [swap(part, "fsdp", 1) for part in send]
    parts = 2
    onward = call(
        pass_kernel, [shape((rows // parts, width), bf16)] * parts, [keep, from_core[1]], moved=1
    )
    from_chip = [swap(part, "fsdp", 2) for part in onward]
    (slices,) = call(
        layer_kernel,
        [shape((8, rows // 2, width // 2), bf16)],
        [marked, keep, from_core[0], ln_gains, order, *from_chip],
        moved=1,
    )
    merge_blocks = [pair, merge_near, merge_far, swap(after(merge_far, (slices, merge_near)), "dp", 2)]
    both = 2 * n_fsdp
    inputs = lax.all_to_all(
        slices,
        ("dp", "fsdp"),
        split_axis=0,
        concat_axis=0,
        tiled=True,
        axis_index_groups=[
            list(range(i, i + both)) for i in range(0, n_dp * n_fsdp, both)
        ],
    )
    shares = call(
        merge_kernel,
        [shape((2 * count, half), f32)] + [shape((2 * count, half), bf16)] * 3,
        [me_cell, at_cell, inputs, *merge_blocks],
        [pltpu.VMEM((8, count, half), f32)],
        flops=2 * 8 * count * width * half,
        smem=2,
    )
    got = [swap(shares[k], "fsdp", k) for k in range(1, 4)]
    (packed,) = call(
        pack_kernel,
        [shape((n_dp * 2 * capacity, half), bf16)],
        [slots, shares[0], *got],
        flops=2 * n_dp * 2 * capacity * 2 * count * half,
    )
    arrived = lax.all_to_all(
        packed.reshape(n_dp, 2 * capacity, half), "dp", split_axis=0, concat_axis=0, tiled=True
    )
    arrived = arrived.reshape(n_dp // 2, 2, 2, capacity, half).transpose(0, 2, 3, 1, 4)
    return arrived.reshape(n_dp * capacity, 2 * half)


def solution(mesh):
    small = mesh.shape["dp"] == 8 and mesh.shape["fsdp"] == 4
    return jax.shard_map(
        by_permutes if small else by_gathers,
        mesh=mesh,
        in_specs=(
            P(("dp", "fsdp"), None),
            P(None, "dp", "fsdp"),
            P("fsdp", "dp"),
            P(("dp", "fsdp"), None),
            P(),
            P("dp", "fsdp"),
            P(("dp", "fsdp"), None),
            P(("dp", "fsdp"), None),
        ),
        out_specs=P(("dp", "fsdp"), None),
        check_vma=False,
    )
```

```python
import functools
import math

import jax
import jax.numpy as jnp
from jax import lax
from jax.experimental import pallas as pl
from jax.experimental.pallas import tpu as pltpu
from jax.sharding import PartitionSpec as P

HD = 80


epsilon = 1e-06


def normalize(values_in, gain_row):
    widened = values_in.astype(jnp.float32)
    centered = widened - jnp.mean(widened, axis=1, keepdims=True)
    variance = jnp.mean(centered * centered, axis=1, keepdims=True)
    return (centered * lax.rsqrt(variance + epsilon) * gain_row).astype(jnp.bfloat16)


def attend(queries, keys_all, values_all, seg_rows, seg_cols):
    factor = 1.0 / math.sqrt(HD)
    allowed = seg_rows[:, None] == seg_cols[None, :]
    pieces = []
    for head_index in range(queries.shape[1] // HD):
        first_col = head_index * HD
        last_col = first_col + HD
        scores = (
            lax.dot_general(
                queries[:, first_col:last_col],
                keys_all[:, first_col:last_col],
                (((1,), (1,)), ((), ())),
                preferred_element_type=jnp.float32,
            )
            * factor
        )
        masked = jnp.where(allowed, scores, -jnp.inf)
        highest = jnp.max(masked, axis=1, keepdims=True)
        weights = jnp.exp(masked - highest)
        totals = jnp.sum(weights, axis=1, keepdims=True)
        head_out = jnp.dot(
            weights.astype(jnp.bfloat16),
            values_all[:, first_col:last_col],
            preferred_element_type=jnp.float32,
        )
        pieces.append(head_out / totals)
    return jnp.concatenate(pieces, axis=1).astype(jnp.bfloat16)


def slot_numbers(targets, capacity):
    n = targets.shape[0]
    same = targets[:, None] == targets[None, :]
    before = jnp.arange(n)[None, :] < jnp.arange(n)[:, None]
    return targets * capacity, jnp.sum((same & before).astype(jnp.int32), axis=1)


def by_gathers(
    tokens, qkv_weight, out_weight, merge_weight, ln_gains, segments, merge_rows, owners
):
    n_dp = lax.axis_size("dp")
    qkv_mine = lax.all_gather(qkv_weight, "dp", axis=1, tiled=True)
    out_mine = lax.all_gather(out_weight, "dp", axis=1, tiled=True)
    n_fsdp = lax.axis_size("fsdp")
    normed = normalize(tokens, ln_gains[0])
    group_normed = lax.all_gather(normed, "fsdp", axis=0, tiled=True)
    group_segs = lax.all_gather(segments, "fsdp", axis=1, tiled=True)
    queries, keys_all, values_all = (
        jnp.dot(group_normed, qkv_mine[n], preferred_element_type=jnp.float32).astype(jnp.bfloat16)
        for n in range(3)
    )
    attended_mine = attend(queries, keys_all, values_all, group_segs[0], group_segs[0])
    attended_local = lax.all_to_all(attended_mine, "fsdp", split_axis=0, concat_axis=1, tiled=True)
    out_full = lax.all_gather(out_mine, "fsdp", axis=0, tiled=True)
    update = jnp.dot(attended_local, out_full, preferred_element_type=jnp.float32)
    layer_out = (tokens.astype(jnp.float32) + update).astype(jnp.bfloat16)
    merge_in = normalize(layer_out, ln_gains[1])
    merge_count = tokens.shape[0] // 4
    stacked = jnp.take(merge_in, merge_rows[0], axis=0).reshape(merge_count, 4 * merge_in.shape[1])
    slice_rows = merge_weight.shape[0]
    part_rows = lax.all_gather(merge_weight, "dp", axis=0, tiled=True)
    blocks = stacked.reshape(merge_count, n_dp, n_fsdp * slice_rows)
    received = lax.all_to_all(blocks, "fsdp", split_axis=2, concat_axis=0, tiled=True)
    gathered_inputs = received.reshape(n_fsdp * merge_count, n_dp * slice_rows)
    merged = lax.psum_scatter(
        jnp.dot(gathered_inputs, part_rows, preferred_element_type=jnp.float32).astype(
            jnp.bfloat16
        ),
        "fsdp",
        scatter_dimension=0,
        tiled=True,
    )
    capacity = max(2, (2 * merge_count + n_dp - 1) // n_dp)
    first, rank = slot_numbers(owners[:, 0], capacity)
    placing = (
        jnp.arange(n_dp * capacity, dtype=jnp.int32)[:, None] == (first + rank)[None, :]
    ).astype(jnp.bfloat16)
    packed = jnp.dot(placing, merged, preferred_element_type=jnp.float32).astype(jnp.bfloat16)
    packed = packed.reshape(n_dp, capacity, merged.shape[1])
    arrived = lax.all_to_all(packed, "dp", split_axis=0, concat_axis=0, tiled=True)
    return arrived.reshape(n_dp * capacity, merged.shape[1])


def swap(value, axis, k):
    return lax.ppermute(value, axis, [(i, i ^ k) for i in range(lax.axis_size(axis))])


def after(value, other):
    return lax.optimization_barrier((value, other))[0]


ORDER = (0, 2, 4, 6, 1, 3, 5, 7)


def dot(a, b):
    return jnp.dot(a, b, preferred_element_type=jnp.float32)


def dot_turned(a, b):
    return lax.dot_general(a, b, (((1,), (1,)), ((), ())), preferred_element_type=jnp.float32)


def call(kernel, outs, operands, scratch=(), flops=0, smem=0, exps=0, moved=None):
    moved = moved or sum(math.prod(x.shape) * x.dtype.itemsize for x in (*operands, *outs))
    specs = [pl.BlockSpec(memory_space=pltpu.SMEM)] * smem
    specs += [pl.BlockSpec(memory_space=pltpu.VMEM)] * (len(operands) - smem)
    return pl.pallas_call(
        kernel,
        out_shape=tuple(outs),
        in_specs=specs,
        out_specs=tuple(pl.BlockSpec(memory_space=pltpu.VMEM) for _ in outs),
        scratch_shapes=list(scratch),
        compiler_params=pltpu.CompilerParams(vmem_limit_bytes=16 * 1024 * 1024),
        cost_estimate=pl.CostEstimate(
            flops=flops, bytes_accessed=moved, transcendentals=exps
        ),
    )(*operands)


def norm_kernel(gains_ref, *refs):
    tokens, out_ref = refs[0:4], refs[4]
    rows = tokens[0].shape[0] - 16
    for n in range(4):
        out_ref[n * rows : (n + 1) * rows, :] = normalize(tokens[n][0:rows, :], gains_ref[0:1, :])


def lay_out(me, blocks, part, whole):
    step = blocks[0].shape[1]
    for number, block in zip(ORDER, blocks):
        start = pl.multiple_of((me ^ number) * step, 32)
        whole[pl.ds(start, step), :] = block[part if block.shape[0] == 4 else part % 2]


def score_kernel(me_ref, rows_ref, *refs):
    marks, blocks = refs[0:4], refs[4:12]
    weights_ref, totals_ref, q_whole, k_whole = refs[12:]
    lay_out(me_ref[0], blocks, 0, q_whole)
    lay_out(me_ref[0], blocks, 1, k_whole)
    queries = dot(rows_ref[...], q_whole[...]).astype(jnp.bfloat16)
    keys = dot(rows_ref[...], k_whole[...]).astype(jnp.bfloat16)
    rows = marks[0].shape[0] - 16
    in_row = [t[rows : rows + 16, 0:rows].astype(jnp.float32)[0:1, :] for t in marks]
    in_col = [jnp.broadcast_to(s, (rows, rows)).T[:, 0:1] for s in in_row]
    allowed = jnp.concatenate(in_col, axis=0) == jnp.concatenate(in_row, axis=1)
    factor = 1.0 / math.sqrt(HD)
    for head in range(queries.shape[1] // HD):
        cols = slice(head * HD, (head + 1) * HD)
        scores = dot_turned(queries[:, cols], keys[:, cols]) * factor
        masked = jnp.where(allowed, scores, -jnp.inf)
        weights = jnp.exp(masked - jnp.max(masked, axis=1, keepdims=True))
        weights_ref[head] = weights.astype(jnp.bfloat16)
        totals_ref[head] = jnp.sum(weights, axis=1, keepdims=True)


def value_kernel(me_ref, rows_ref, weights_ref, totals_ref, *refs):
    blocks = refs[0:8]
    keep_ref, send_near, send_far, v_whole, out_whole = refs[8:]
    lay_out(me_ref[0], blocks, 2, v_whole)
    lay_out(me_ref[0], blocks, 3, out_whole)
    values = dot(rows_ref[...], v_whole[...]).astype(jnp.bfloat16)
    pieces = []
    for head in range(values.shape[1] // HD):
        found = dot(weights_ref[head], values[:, head * HD : (head + 1) * HD])
        pieces.append(found / totals_ref[head])
    attended = jnp.concatenate(pieces, axis=1).astype(jnp.bfloat16)
    half = attended.shape[0] // 2
    sent = dot_turned(attended[half:, :], out_whole[...]).astype(jnp.bfloat16)
    send_near[...], send_far[...] = sent[: half // 2, :], sent[half // 2 :, :]
    keep_ref[...] = dot_turned(attended[:half, :], out_whole[...])


def pass_kernel(keep_ref, got_ref, *outs):
    rows, parts = got_ref.shape[0], len(outs)
    step = rows // parts
    for n, out_ref in enumerate(outs):
        kept = keep_ref[rows + n * step : rows + (n + 1) * step, :]
        got = got_ref[n * step : (n + 1) * step, :].astype(jnp.float32)
        out_ref[...] = (kept + got).astype(jnp.bfloat16)


def layer_kernel(tokens_ref, keep_ref, core_ref, gains_ref, order_ref, *refs):
    chips, slices = refs[:-1], refs[-1]
    rows, width = tokens_ref.shape[0] - 16, tokens_ref.shape[1]
    summed = (
        tokens_ref[0:rows, :].astype(jnp.float32)
        + keep_ref[0:rows, :]
        + core_ref[0:rows, :].astype(jnp.float32)
        + jnp.concatenate([ref[...] for ref in chips], axis=0).astype(jnp.float32)
    )
    merge_in = normalize(summed.astype(jnp.bfloat16), gains_ref[1:2, :])
    places = lax.broadcasted_iota(jnp.int32, (rows, rows), 1)
    picking = (order_ref[...] == places).astype(jnp.bfloat16)
    ordered = dot(picking, merge_in).astype(jnp.bfloat16)
    step, half = width // 8, width // 2
    for n in range(4):
        part = jnp.concatenate(
            [
                ordered[:, n * step : (n + 1) * step],
                ordered[:, half + n * step : half + (n + 1) * step],
            ],
            axis=1,
        )
        part = jnp.concatenate([part[: rows // 2, :], part[rows // 2 :, :]], axis=1)
        slices[n] = part
        slices[4 + n] = part


def merge_kernel(me_ref, at_ref, inputs, *refs):
    blocks, (keep_ref, *sends), total = refs[0:4], refs[4:8], refs[8]
    count, width = inputs.shape[1] // 2, inputs.shape[2] // 2
    z, y = me_ref[0] // 2, lax.rem(me_ref[0], 2)
    for number in range(4):
        position = z ^ number
        at = pl.multiple_of(lax.rem(position, 2) * count, 32)
        rows = inputs[:, pl.ds(at, count), :].reshape(8 * count, 2 * width)
        rows = jnp.where(position < 2, rows[:, :width], rows[:, width:])
        step = blocks[number].shape[0] // 2
        own, other = blocks[number][:step, :], blocks[number][step:, :]
        block = jnp.concatenate(
            [jnp.where(y == 0, own, other), jnp.where(y == 0, other, own)], axis=0
        )
        found = dot(rows, block).reshape(total.shape)
        total[...] = found if number == 0 else total[...] + found
    for k in range(4):
        to = at_ref[0] ^ k
        share = jnp.concatenate([total[4 * y + to], total[4 * (1 - y) + to]], axis=0)
        if k == 0:
            keep_ref[...] = share
        else:
            sends[k - 1][...] = share.astype(jnp.bfloat16)


def pack_kernel(slots_ref, keep_ref, one_ref, two_ref, three_ref, out_ref):
    total = keep_ref[...]
    for got in (one_ref, two_ref, three_ref):
        total = total + got[...].astype(jnp.float32)
    shape = (out_ref.shape[0], total.shape[0])
    placing = (lax.broadcasted_iota(jnp.int32, shape, 0) == slots_ref[...]).astype(jnp.bfloat16)
    out_ref[...] = dot(placing, total.astype(jnp.bfloat16)).astype(jnp.bfloat16)


def by_permutes(
    tokens, qkv_weight, out_weight, merge_weight, ln_gains, segments, merge_rows, owners
):
    rows, width = tokens.shape
    count = rows // 4
    n_dp, n_fsdp = lax.axis_size("dp"), lax.axis_size("fsdp")
    me, at = lax.axis_index("dp"), lax.axis_index("fsdp")
    y = lax.rem(me, 2)
    me_cell, at_cell = me.reshape(1), at.reshape(1)
    bf16, f32 = jnp.bfloat16, jnp.float32
    shape = jax.ShapeDtypeStruct
    cols = qkv_weight.shape[2]
    group = n_fsdp * rows

    heads = jnp.concatenate([qkv_weight, out_weight.T[None]], axis=0)
    near, beside = swap(heads, "dp", 2), swap(heads, "dp", 1)
    first, second = heads[0:2], heads[2:4]
    first_far = swap(first, "dp", 4)
    first_far_y = swap(after(first_far, (near, beside)), "dp", 1)
    first_last = swap(first_far, "dp", 2)
    corner = swap(after(beside[0:2], first_last), "dp", 2)
    second_far = swap(after(second, first_far), "dp", 4)

    marks = jnp.pad(segments.astype(bf16), ((0, 15), (0, width - rows)))
    marked = after(jnp.concatenate([tokens, marks], axis=0), first)
    along_x = swap(marked, "fsdp", 2)
    group_rows = [marked, along_x]
    group_rows += [swap(after(part, (first_far_y, first_last, second_far)), "fsdp", 1) for part in (marked, along_x)]
    (normed,) = call(norm_kernel, [shape((group, width), bf16)], [ln_gains, *group_rows])

    second_far_y = swap(second_far, "dp", 1)
    second_last = swap(second_far, "dp", 2)
    other_corner = swap(beside[2:4], "dp", 2)
    blocks = [
        [heads, near, far, last, beside, part, far_y, swap(after(last, corner), "dp", 1)]
        for far, last, far_y, part in (
            (first_far, first_last, first_far_y, corner),
            (second_far, second_last, second_far_y, other_corner),
        )
    ]

    half = merge_weight.shape[1] // 2
    low, high = merge_weight[:, :half], merge_weight[:, half:]
    lower = y == 0
    mine = owners[:, 0]
    note = jnp.pad(owners.astype(bf16).T, ((0, 15), (0, half - count)))
    given = jnp.concatenate([jnp.where(lower, high, low), note], axis=0)
    theirs = swap(after(given, second_far_y), "dp", 1)
    other = theirs[-16, :count].astype(jnp.int32)
    pair = jnp.concatenate([jnp.where(lower, low, high), theirs[:-16]], axis=0)
    held = after(pair, (second_last, second_far_y, blocks[0][7]))
    merge_near, merge_far = swap(held, "dp", 2), swap(held, "dp", 4)

    capacity = max(2, (2 * count + n_dp - 1) // n_dp)
    slots = []
    for number, targets in enumerate((mine, other)):
        start, rank = slot_numbers(targets, 2 * capacity)
        slots.append(start + rank + (y ^ number) * capacity)
    slots = jnp.concatenate(slots).reshape(1, 2 * count)
    order = merge_rows.reshape(count, 4).T.reshape(rows, 1)

    found = cols // HD
    weights, totals = call(
        score_kernel,
        [shape((found, group, group), bf16), shape((found, group, 1), f32)],
        [after(me_cell, theirs), normed, *group_rows, *blocks[0]],
        [pltpu.VMEM((width, cols), bf16)] * 2,
        flops=4 * group * width * cols + 2 * group * group * cols,
        smem=1,
        exps=found * group * group,
    )
    keep, *send = call(
        value_kernel,
        [shape((2 * rows, width), f32)] + [shape((rows, width), bf16)] * 2,
        [me_cell, normed, weights, totals, *blocks[1]],
        [pltpu.VMEM((width, cols), bf16)] * 2,
        flops=4 * group * width * cols + 2 * group * group * cols,
        smem=1,
    )
    from_core = [swap(part, "fsdp", 1) for part in send]
    parts = 2
    onward = call(
        pass_kernel, [shape((rows // parts, width), bf16)] * parts, [keep, from_core[1]], moved=1
    )
    from_chip = [swap(part, "fsdp", 2) for part in onward]
    (slices,) = call(
        layer_kernel,
        [shape((8, rows // 2, width // 2), bf16)],
        [marked, keep, from_core[0], ln_gains, order, *from_chip],
        moved=1,
    )
    merge_blocks = [pair, merge_near, merge_far, swap(after(merge_far, (slices, merge_near)), "dp", 2)]
    both = 2 * n_fsdp
    inputs = lax.all_to_all(
        slices,
        ("dp", "fsdp"),
        split_axis=0,
        concat_axis=0,
        tiled=True,
        axis_index_groups=[
            list(range(i, i + both)) for i in range(0, n_dp * n_fsdp, both)
        ],
    )
    shares = call(
        merge_kernel,
        [shape((2 * count, half), f32)] + [shape((2 * count, half), bf16)] * 3,
        [me_cell, at_cell, inputs, *merge_blocks],
        [pltpu.VMEM((8, count, half), f32)],
        flops=2 * 8 * count * width * half,
        smem=2,
    )
    got = [swap(shares[k], "fsdp", k) for k in range(1, 4)]
    (packed,) = call(
        pack_kernel,
        [shape((n_dp * 2 * capacity, half), bf16)],
        [slots, shares[0], *got],
        flops=2 * n_dp * 2 * capacity * 2 * count * half,
    )
    arrived = lax.all_to_all(
        packed.reshape(n_dp, 2 * capacity, half), "dp", split_axis=0, concat_axis=0, tiled=True
    )
    arrived = arrived.reshape(n_dp // 2, 2, 2, capacity, half).transpose(0, 2, 3, 1, 4)
    return arrived.reshape(n_dp * capacity, 2 * half)


def solution(mesh):
    small = mesh.shape["dp"] == 8 and mesh.shape["fsdp"] == 4
    return jax.shard_map(
        by_permutes if small else by_gathers,
        mesh=mesh,
        in_specs=(
            P(("dp", "fsdp"), None),
            P(None, "dp", "fsdp"),
            P("fsdp", "dp"),
            P(("dp", "fsdp"), None),
            P(),
            P("dp", "fsdp"),
            P(("dp", "fsdp"), None),
            P(("dp", "fsdp"), None),
        ),
        out_specs=P(("dp", "fsdp"), None),
        check_vma=False,
    )
```

```python
import functools
import math

import jax
import jax.numpy as jnp
from jax import lax
from jax.experimental import pallas as pl
from jax.experimental.pallas import tpu as pltpu
from jax.sharding import PartitionSpec as P

HD = 80


epsilon = 1e-06


def normalize(values_in, gain_row):
    widened = values_in.astype(jnp.float32)
    centered = widened - jnp.mean(widened, axis=1, keepdims=True)
    variance = jnp.mean(centered * centered, axis=1, keepdims=True)
    return (centered * lax.rsqrt(variance + epsilon) * gain_row).astype(jnp.bfloat16)


def attend(queries, keys_all, values_all, seg_rows, seg_cols):
    factor = 1.0 / math.sqrt(HD)
    allowed = seg_rows[:, None] == seg_cols[None, :]
    pieces = []
    for head_index in range(queries.shape[1] // HD):
        first_col = head_index * HD
        last_col = first_col + HD
        scores = (
            lax.dot_general(
                queries[:, first_col:last_col],
                keys_all[:, first_col:last_col],
                (((1,), (1,)), ((), ())),
                preferred_element_type=jnp.float32,
            )
            * factor
        )
        masked = jnp.where(allowed, scores, -jnp.inf)
        highest = jnp.max(masked, axis=1, keepdims=True)
        weights = jnp.exp(masked - highest)
        totals = jnp.sum(weights, axis=1, keepdims=True)
        head_out = jnp.dot(
            weights.astype(jnp.bfloat16),
            values_all[:, first_col:last_col],
            preferred_element_type=jnp.float32,
        )
        pieces.append(head_out / totals)
    return jnp.concatenate(pieces, axis=1).astype(jnp.bfloat16)


def slot_numbers(targets, capacity):
    n = targets.shape[0]
    same = targets[:, None] == targets[None, :]
    before = jnp.arange(n)[None, :] < jnp.arange(n)[:, None]
    return targets * capacity, jnp.sum((same & before).astype(jnp.int32), axis=1)


def by_gathers(
    tokens, qkv_weight, out_weight, merge_weight, ln_gains, segments, merge_rows, owners
):
    n_dp = lax.axis_size("dp")
    qkv_mine = lax.all_gather(qkv_weight, "dp", axis=1, tiled=True)
    out_mine = lax.all_gather(out_weight, "dp", axis=1, tiled=True)
    n_fsdp = lax.axis_size("fsdp")
    normed = normalize(tokens, ln_gains[0])
    group_normed = lax.all_gather(normed, "fsdp", axis=0, tiled=True)
    group_segs = lax.all_gather(segments, "fsdp", axis=1, tiled=True)
    queries, keys_all, values_all = (
        jnp.dot(group_normed, qkv_mine[n], preferred_element_type=jnp.float32).astype(jnp.bfloat16)
        for n in range(3)
    )
    attended_mine = attend(queries, keys_all, values_all, group_segs[0], group_segs[0])
    attended_local = lax.all_to_all(attended_mine, "fsdp", split_axis=0, concat_axis=1, tiled=True)
    out_full = lax.all_gather(out_mine, "fsdp", axis=0, tiled=True)
    update = jnp.dot(attended_local, out_full, preferred_element_type=jnp.float32)
    layer_out = (tokens.astype(jnp.float32) + update).astype(jnp.bfloat16)
    merge_in = normalize(layer_out, ln_gains[1])
    merge_count = tokens.shape[0] // 4
    stacked = jnp.take(merge_in, merge_rows[0], axis=0).reshape(merge_count, 4 * merge_in.shape[1])
    slice_rows = merge_weight.shape[0]
    part_rows = lax.all_gather(merge_weight, "dp", axis=0, tiled=True)
    blocks = stacked.reshape(merge_count, n_dp, n_fsdp * slice_rows)
    received = lax.all_to_all(blocks, "fsdp", split_axis=2, concat_axis=0, tiled=True)
    gathered_inputs = received.reshape(n_fsdp * merge_count, n_dp * slice_rows)
    merged = lax.psum_scatter(
        jnp.dot(gathered_inputs, part_rows, preferred_element_type=jnp.float32).astype(
            jnp.bfloat16
        ),
        "fsdp",
        scatter_dimension=0,
        tiled=True,
    )
    capacity = max(2, (2 * merge_count + n_dp - 1) // n_dp)
    first, rank = slot_numbers(owners[:, 0], capacity)
    placing = (
        jnp.arange(n_dp * capacity, dtype=jnp.int32)[:, None] == (first + rank)[None, :]
    ).astype(jnp.bfloat16)
    packed = jnp.dot(placing, merged, preferred_element_type=jnp.float32).astype(jnp.bfloat16)
    packed = packed.reshape(n_dp, capacity, merged.shape[1])
    arrived = lax.all_to_all(packed, "dp", split_axis=0, concat_axis=0, tiled=True)
    return arrived.reshape(n_dp * capacity, merged.shape[1])


def swap(value, axis, k):
    return lax.ppermute(value, axis, [(i, i ^ k) for i in range(lax.axis_size(axis))])


def after(value, other):
    return lax.optimization_barrier((value, other))[0]


ORDER = (0, 2, 4, 6, 1, 3, 5, 7)


def dot(a, b):
    return jnp.dot(a, b, preferred_element_type=jnp.float32)


def dot_turned(a, b):
    return lax.dot_general(a, b, (((1,), (1,)), ((), ())), preferred_element_type=jnp.float32)


def call(kernel, outs, operands, scratch=(), flops=0, smem=0, exps=0, moved=None):
    moved = moved or sum(math.prod(x.shape) * x.dtype.itemsize for x in (*operands, *outs))
    specs = [pl.BlockSpec(memory_space=pltpu.SMEM)] * smem
    specs += [pl.BlockSpec(memory_space=pltpu.VMEM)] * (len(operands) - smem)
    return pl.pallas_call(
        kernel,
        out_shape=tuple(outs),
        in_specs=specs,
        out_specs=tuple(pl.BlockSpec(memory_space=pltpu.VMEM) for _ in outs),
        scratch_shapes=list(scratch),
        compiler_params=pltpu.CompilerParams(vmem_limit_bytes=16 * 1024 * 1024),
        cost_estimate=pl.CostEstimate(
            flops=flops, bytes_accessed=moved, transcendentals=exps
        ),
    )(*operands)


def norm_kernel(gains_ref, *refs):
    tokens, out_ref = refs[0:4], refs[4]
    rows = tokens[0].shape[0] - 16
    for n in range(4):
        out_ref[n * rows : (n + 1) * rows, :] = normalize(tokens[n][0:rows, :], gains_ref[0:1, :])


def lay_out(me, blocks, part, whole):
    step = blocks[0].shape[1]
    for number, block in zip(ORDER, blocks):
        start = pl.multiple_of((me ^ number) * step, 32)
        whole[pl.ds(start, step), :] = block[part if block.shape[0] == 4 else part % 2]


def score_kernel(me_ref, rows_ref, *refs):
    marks, blocks = refs[0:4], refs[4:12]
    weights_ref, totals_ref, q_whole, k_whole = refs[12:]
    lay_out(me_ref[0], blocks, 0, q_whole)
    lay_out(me_ref[0], blocks, 1, k_whole)
    queries = dot(rows_ref[...], q_whole[...]).astype(jnp.bfloat16)
    keys = dot(rows_ref[...], k_whole[...]).astype(jnp.bfloat16)
    rows = marks[0].shape[0] - 16
    in_row = [t[rows : rows + 16, 0:rows].astype(jnp.float32)[0:1, :] for t in marks]
    in_col = [jnp.broadcast_to(s, (rows, rows)).T[:, 0:1] for s in in_row]
    allowed = jnp.concatenate(in_col, axis=0) == jnp.concatenate(in_row, axis=1)
    factor = 1.0 / math.sqrt(HD)
    for head in range(queries.shape[1] // HD):
        cols = slice(head * HD, (head + 1) * HD)
        scores = dot_turned(queries[:, cols], keys[:, cols]) * factor
        masked = jnp.where(allowed, scores, -jnp.inf)
        weights = jnp.exp(masked - jnp.max(masked, axis=1, keepdims=True))
        weights_ref[head] = weights.astype(jnp.bfloat16)
        totals_ref[head] = jnp.sum(weights, axis=1, keepdims=True)


def value_kernel(me_ref, rows_ref, weights_ref, totals_ref, *refs):
    blocks = refs[0:8]
    keep_ref, send_near, send_far, v_whole, out_whole = refs[8:]
    lay_out(me_ref[0], blocks, 2, v_whole)
    lay_out(me_ref[0], blocks, 3, out_whole)
    values = dot(rows_ref[...], v_whole[...]).astype(jnp.bfloat16)
    pieces = []
    for head in range(values.shape[1] // HD):
        found = dot(weights_ref[head], values[:, head * HD : (head + 1) * HD])
        pieces.append(found / totals_ref[head])
    attended = jnp.concatenate(pieces, axis=1).astype(jnp.bfloat16)
    half = attended.shape[0] // 2
    sent = dot_turned(attended[half:, :], out_whole[...]).astype(jnp.bfloat16)
    send_near[...], send_far[...] = sent[: half // 2, :], sent[half // 2 :, :]
    keep_ref[...] = dot_turned(attended[:half, :], out_whole[...])


def pass_kernel(keep_ref, got_ref, *outs):
    rows, parts = got_ref.shape[0], len(outs)
    step = rows // parts
    for n, out_ref in enumerate(outs):
        kept = keep_ref[rows + n * step : rows + (n + 1) * step, :]
        got = got_ref[n * step : (n + 1) * step, :].astype(jnp.float32)
        out_ref[...] = (kept + got).astype(jnp.bfloat16)


def layer_kernel(tokens_ref, keep_ref, core_ref, gains_ref, order_ref, *refs):
    chips, slices = refs[:-1], refs[-1]
    rows, width = tokens_ref.shape[0] - 16, tokens_ref.shape[1]
    summed = (
        tokens_ref[0:rows, :].astype(jnp.float32)
        + keep_ref[0:rows, :]
        + core_ref[0:rows, :].astype(jnp.float32)
        + jnp.concatenate([ref[...] for ref in chips], axis=0).astype(jnp.float32)
    )
    merge_in = normalize(summed.astype(jnp.bfloat16), gains_ref[1:2, :])
    places = lax.broadcasted_iota(jnp.int32, (rows, rows), 1)
    picking = (order_ref[...] == places).astype(jnp.bfloat16)
    ordered = dot(picking, merge_in).astype(jnp.bfloat16)
    step, half = width // 8, width // 2
    for n in range(4):
        part = jnp.concatenate(
            [
                ordered[:, n * step : (n + 1) * step],
                ordered[:, half + n * step : half + (n + 1) * step],
            ],
            axis=1,
        )
        part = jnp.concatenate([part[: rows // 2, :], part[rows // 2 :, :]], axis=1)
        slices[n] = part
        slices[4 + n] = part


def merge_kernel(me_ref, at_ref, inputs, *refs):
    blocks, (keep_ref, *sends), total = refs[0:4], refs[4:8], refs[8]
    count, width = inputs.shape[1] // 2, inputs.shape[2] // 2
    z, y = me_ref[0] // 2, lax.rem(me_ref[0], 2)
    for number in range(4):
        position = z ^ number
        at = pl.multiple_of(lax.rem(position, 2) * count, 32)
        rows = inputs[:, pl.ds(at, count), :].reshape(8 * count, 2 * width)
        rows = jnp.where(position < 2, rows[:, :width], rows[:, width:])
        step = blocks[number].shape[0] // 2
        own, other = blocks[number][:step, :], blocks[number][step:, :]
        block = jnp.concatenate(
            [jnp.where(y == 0, own, other), jnp.where(y == 0, other, own)], axis=0
        )
        found = dot(rows, block).reshape(total.shape)
        total[...] = found if number == 0 else total[...] + found
    for k in range(4):
        to = at_ref[0] ^ k
        share = jnp.concatenate([total[4 * y + to], total[4 * (1 - y) + to]], axis=0)
        if k == 0:
            keep_ref[...] = share
        else:
            sends[k - 1][...] = share.astype(jnp.bfloat16)


def pack_kernel(slots_ref, keep_ref, one_ref, two_ref, three_ref, out_ref):
    total = keep_ref[...]
    for got in (one_ref, two_ref, three_ref):
        total = total + got[...].astype(jnp.float32)
    shape = (out_ref.shape[0], total.shape[0])
    placing = (lax.broadcasted_iota(jnp.int32, shape, 0) == slots_ref[...]).astype(jnp.bfloat16)
    out_ref[...] = dot(placing, total.astype(jnp.bfloat16)).astype(jnp.bfloat16)


def by_permutes(
    tokens, qkv_weight, out_weight, merge_weight, ln_gains, segments, merge_rows, owners
):
    rows, width = tokens.shape
    count = rows // 4
    n_dp, n_fsdp = lax.axis_size("dp"), lax.axis_size("fsdp")
    me, at = lax.axis_index("dp"), lax.axis_index("fsdp")
    y = lax.rem(me, 2)
    me_cell, at_cell = me.reshape(1), at.reshape(1)
    bf16, f32 = jnp.bfloat16, jnp.float32
    shape = jax.ShapeDtypeStruct
    cols = qkv_weight.shape[2]
    group = n_fsdp * rows

    heads = jnp.concatenate([qkv_weight, out_weight.T[None]], axis=0)
    near, beside = swap(heads, "dp", 2), swap(heads, "dp", 1)
    first = qkv_weight[0:2]
    second = jnp.concatenate([qkv_weight[2:3], out_weight.T[None]], axis=0)
    first_far = swap(first, "dp", 4)
    first_far_y = swap(after(first_far, beside), "dp", 1)
    first_last = swap(first_far, "dp", 2)
    corner = swap(after(beside[0:2], (first_last, near)), "dp", 2)
    second_far = swap(after(second, first_far), "dp", 4)

    marks = jnp.pad(segments.astype(bf16), ((0, 15), (0, width - rows)))
    marked = after(jnp.concatenate([tokens, marks], axis=0), first)
    along_x = swap(marked, "fsdp", 2)
    group_rows = [marked, along_x]
    group_rows += [swap(after(part, (first_far_y, first_last, second_far)), "fsdp", 1) for part in (marked, along_x)]
    (normed,) = call(norm_kernel, [shape((group, width), bf16)], [ln_gains, *group_rows])

    second_far_y = swap(second_far, "dp", 1)
    second_last = swap(second_far, "dp", 2)
    other_corner = swap(after(beside[2:4], first_last), "dp", 2)
    blocks = [
        [heads, near, far, last, beside, part, far_y, swap(after(last, corner), "dp", 1)]
        for far, last, far_y, part in (
            (first_far, first_last, first_far_y, corner),
            (second_far, second_last, second_far_y, other_corner),
        )
    ]

    half = merge_weight.shape[1] // 2
    low, high = merge_weight[:, :half], merge_weight[:, half:]
    lower = y == 0
    mine = owners[:, 0]
    note = jnp.pad(owners.astype(bf16).T, ((0, 15), (0, half - count)))
    given = jnp.concatenate([jnp.where(lower, high, low), note], axis=0)
    theirs = swap(after(given, second_far_y), "dp", 1)
    other = theirs[-16, :count].astype(jnp.int32)
    pair = jnp.concatenate([jnp.where(lower, low, high), theirs[:-16]], axis=0)
    held = after(pair, (second_last, second_far_y, blocks[0][7]))
    merge_near, merge_far = swap(held, "dp", 2), swap(held, "dp", 4)

    capacity = max(2, (2 * count + n_dp - 1) // n_dp)
    slots = []
    for number, targets in enumerate((mine, other)):
        start, rank = slot_numbers(targets, 2 * capacity)
        slots.append(start + rank + (y ^ number) * capacity)
    slots = jnp.concatenate(slots).reshape(1, 2 * count)
    order = merge_rows.reshape(count, 4).T.reshape(rows, 1)

    found = cols // HD
    weights, totals = call(
        score_kernel,
        [shape((found, group, group), bf16), shape((found, group, 1), f32)],
        [after(me_cell, theirs), normed, *group_rows, *blocks[0]],
        [pltpu.VMEM((width, cols), bf16)] * 2,
        flops=4 * group * width * cols + 2 * group * group * cols,
        smem=1,
        exps=found * group * group,
    )
    keep, *send = call(
        value_kernel,
        [shape((2 * rows, width), f32)] + [shape((rows, width), bf16)] * 2,
        [me_cell, normed, weights, totals, *blocks[1]],
        [pltpu.VMEM((width, cols), bf16)] * 2,
        flops=4 * group * width * cols + 2 * group * group * cols,
        smem=1,
    )
    from_core = [swap(part, "fsdp", 1) for part in send]
    parts = 2
    onward = call(
        pass_kernel, [shape((rows // parts, width), bf16)] * parts, [keep, from_core[1]], moved=1
    )
    from_chip = [swap(part, "fsdp", 2) for part in onward]
    (slices,) = call(
        layer_kernel,
        [shape((8, rows // 2, width // 2), bf16)],
        [marked, keep, from_core[0], ln_gains, order, *from_chip],
        moved=1,
    )
    merge_blocks = [pair, merge_near, merge_far, swap(after(merge_far, (slices, merge_near)), "dp", 2)]
    both = 2 * n_fsdp
    inputs = lax.all_to_all(
        slices,
        ("dp", "fsdp"),
        split_axis=0,
        concat_axis=0,
        tiled=True,
        axis_index_groups=[
            list(range(i, i + both)) for i in range(0, n_dp * n_fsdp, both)
        ],
    )
    shares = call(
        merge_kernel,
        [shape((2 * count, half), f32)] + [shape((2 * count, half), bf16)] * 3,
        [me_cell, at_cell, inputs, *merge_blocks],
        [pltpu.VMEM((8, count, half), f32)],
        flops=2 * 8 * count * width * half,
        smem=2,
    )
    got = [swap(shares[k], "fsdp", k) for k in range(1, 4)]
    (packed,) = call(
        pack_kernel,
        [shape((n_dp * 2 * capacity, half), bf16)],
        [slots, shares[0], *got],
        flops=2 * n_dp * 2 * capacity * 2 * count * half,
    )
    arrived = lax.all_to_all(
        packed.reshape(n_dp, 2 * capacity, half), "dp", split_axis=0, concat_axis=0, tiled=True
    )
    arrived = arrived.reshape(n_dp // 2, 2, 2, capacity, half).transpose(0, 2, 3, 1, 4)
    return arrived.reshape(n_dp * capacity, 2 * half)


def solution(mesh):
    small = mesh.shape["dp"] == 8 and mesh.shape["fsdp"] == 4
    return jax.shard_map(
        by_permutes if small else by_gathers,
        mesh=mesh,
        in_specs=(
            P(("dp", "fsdp"), None),
            P(None, "dp", "fsdp"),
            P("fsdp", "dp"),
            P(("dp", "fsdp"), None),
            P(),
            P("dp", "fsdp"),
            P(("dp", "fsdp"), None),
            P(("dp", "fsdp"), None),
        ),
        out_specs=P(("dp", "fsdp"), None),
        check_vma=False,
    )
```

```python
import functools
import math

import jax
import jax.numpy as jnp
from jax import lax
from jax.experimental import pallas as pl
from jax.experimental.pallas import tpu as pltpu
from jax.sharding import PartitionSpec as P

HD = 80


epsilon = 1e-06


def normalize(values_in, gain_row):
    widened = values_in.astype(jnp.float32)
    centered = widened - jnp.mean(widened, axis=1, keepdims=True)
    variance = jnp.mean(centered * centered, axis=1, keepdims=True)
    return (centered * lax.rsqrt(variance + epsilon) * gain_row).astype(jnp.bfloat16)


def attend(queries, keys_all, values_all, seg_rows, seg_cols):
    factor = 1.0 / math.sqrt(HD)
    allowed = seg_rows[:, None] == seg_cols[None, :]
    pieces = []
    for head_index in range(queries.shape[1] // HD):
        first_col = head_index * HD
        last_col = first_col + HD
        scores = (
            lax.dot_general(
                queries[:, first_col:last_col],
                keys_all[:, first_col:last_col],
                (((1,), (1,)), ((), ())),
                preferred_element_type=jnp.float32,
            )
            * factor
        )
        masked = jnp.where(allowed, scores, -jnp.inf)
        highest = jnp.max(masked, axis=1, keepdims=True)
        weights = jnp.exp(masked - highest)
        totals = jnp.sum(weights, axis=1, keepdims=True)
        head_out = jnp.dot(
            weights.astype(jnp.bfloat16),
            values_all[:, first_col:last_col],
            preferred_element_type=jnp.float32,
        )
        pieces.append(head_out / totals)
    return jnp.concatenate(pieces, axis=1).astype(jnp.bfloat16)


def slot_numbers(targets, capacity):
    n = targets.shape[0]
    same = targets[:, None] == targets[None, :]
    before = jnp.arange(n)[None, :] < jnp.arange(n)[:, None]
    return targets * capacity, jnp.sum((same & before).astype(jnp.int32), axis=1)


def by_gathers(
    tokens, qkv_weight, out_weight, merge_weight, ln_gains, segments, merge_rows, owners
):
    n_dp = lax.axis_size("dp")
    qkv_mine = lax.all_gather(qkv_weight, "dp", axis=1, tiled=True)
    out_mine = lax.all_gather(out_weight, "dp", axis=1, tiled=True)
    n_fsdp = lax.axis_size("fsdp")
    normed = normalize(tokens, ln_gains[0])
    group_normed = lax.all_gather(normed, "fsdp", axis=0, tiled=True)
    group_segs = lax.all_gather(segments, "fsdp", axis=1, tiled=True)
    queries, keys_all, values_all = (
        jnp.dot(group_normed, qkv_mine[n], preferred_element_type=jnp.float32).astype(jnp.bfloat16)
        for n in range(3)
    )
    attended_mine = attend(queries, keys_all, values_all, group_segs[0], group_segs[0])
    attended_local = lax.all_to_all(attended_mine, "fsdp", split_axis=0, concat_axis=1, tiled=True)
    out_full = lax.all_gather(out_mine, "fsdp", axis=0, tiled=True)
    update = jnp.dot(attended_local, out_full, preferred_element_type=jnp.float32)
    layer_out = (tokens.astype(jnp.float32) + update).astype(jnp.bfloat16)
    merge_in = normalize(layer_out, ln_gains[1])
    merge_count = tokens.shape[0] // 4
    stacked = jnp.take(merge_in, merge_rows[0], axis=0).reshape(merge_count, 4 * merge_in.shape[1])
    slice_rows = merge_weight.shape[0]
    part_rows = lax.all_gather(merge_weight, "dp", axis=0, tiled=True)
    blocks = stacked.reshape(merge_count, n_dp, n_fsdp * slice_rows)
    received = lax.all_to_all(blocks, "fsdp", split_axis=2, concat_axis=0, tiled=True)
    gathered_inputs = received.reshape(n_fsdp * merge_count, n_dp * slice_rows)
    merged = lax.psum_scatter(
        jnp.dot(gathered_inputs, part_rows, preferred_element_type=jnp.float32).astype(
            jnp.bfloat16
        ),
        "fsdp",
        scatter_dimension=0,
        tiled=True,
    )
    capacity = max(2, (2 * merge_count + n_dp - 1) // n_dp)
    first, rank = slot_numbers(owners[:, 0], capacity)
    placing = (
        jnp.arange(n_dp * capacity, dtype=jnp.int32)[:, None] == (first + rank)[None, :]
    ).astype(jnp.bfloat16)
    packed = jnp.dot(placing, merged, preferred_element_type=jnp.float32).astype(jnp.bfloat16)
    packed = packed.reshape(n_dp, capacity, merged.shape[1])
    arrived = lax.all_to_all(packed, "dp", split_axis=0, concat_axis=0, tiled=True)
    return arrived.reshape(n_dp * capacity, merged.shape[1])


def swap(value, axis, k):
    return lax.ppermute(value, axis, [(i, i ^ k) for i in range(lax.axis_size(axis))])


def after(value, other):
    return lax.optimization_barrier((value, other))[0]


ORDER = (0, 2, 4, 6, 1, 3, 5, 7)


def dot(a, b):
    return jnp.dot(a, b, preferred_element_type=jnp.float32)


def dot_turned(a, b):
    return lax.dot_general(a, b, (((1,), (1,)), ((), ())), preferred_element_type=jnp.float32)


def call(kernel, outs, operands, scratch=(), flops=0, smem=0, exps=0, moved=None):
    moved = moved or sum(math.prod(x.shape) * x.dtype.itemsize for x in (*operands, *outs))
    specs = [pl.BlockSpec(memory_space=pltpu.SMEM)] * smem
    specs += [pl.BlockSpec(memory_space=pltpu.VMEM)] * (len(operands) - smem)
    return pl.pallas_call(
        kernel,
        out_shape=tuple(outs),
        in_specs=specs,
        out_specs=tuple(pl.BlockSpec(memory_space=pltpu.VMEM) for _ in outs),
        scratch_shapes=list(scratch),
        compiler_params=pltpu.CompilerParams(vmem_limit_bytes=16 * 1024 * 1024),
        cost_estimate=pl.CostEstimate(
            flops=flops, bytes_accessed=moved, transcendentals=exps
        ),
    )(*operands)


def norm_kernel(gains_ref, *refs):
    tokens, out_ref = refs[0:4], refs[4]
    rows = tokens[0].shape[0] - 16
    for n in range(4):
        out_ref[n * rows : (n + 1) * rows, :] = normalize(tokens[n][0:rows, :], gains_ref[0:1, :])


def lay_out(me, blocks, part, whole):
    step = blocks[0].shape[1]
    for number, block in zip(ORDER, blocks):
        start = pl.multiple_of((me ^ number) * step, 32)
        whole[pl.ds(start, step), :] = block[part if block.shape[0] == 4 else part % 2]


def score_kernel(me_ref, rows_ref, *refs):
    marks, blocks = refs[0:4], refs[4:12]
    weights_ref, totals_ref, q_whole, k_whole = refs[12:]
    lay_out(me_ref[0], blocks, 0, q_whole)
    lay_out(me_ref[0], blocks, 1, k_whole)
    queries = dot(rows_ref[...], q_whole[...]).astype(jnp.bfloat16)
    keys = dot(rows_ref[...], k_whole[...]).astype(jnp.bfloat16)
    rows = marks[0].shape[0] - 16
    in_row = [t[rows : rows + 16, 0:rows].astype(jnp.float32)[0:1, :] for t in marks]
    in_col = [jnp.broadcast_to(s, (rows, rows)).T[:, 0:1] for s in in_row]
    allowed = jnp.concatenate(in_col, axis=0) == jnp.concatenate(in_row, axis=1)
    factor = math.log2(math.e) / math.sqrt(HD)
    for head in range(queries.shape[1] // HD):
        cols = slice(head * HD, (head + 1) * HD)
        scores = dot_turned(queries[:, cols], keys[:, cols]) * factor
        masked = jnp.where(allowed, scores, -jnp.inf)
        weights = jnp.exp2(masked - jnp.max(masked, axis=1, keepdims=True))
        weights_ref[head] = weights.astype(jnp.bfloat16)
        totals_ref[head] = jnp.sum(weights, axis=1, keepdims=True)


def value_kernel(me_ref, rows_ref, weights_ref, totals_ref, *refs):
    blocks = refs[0:8]
    keep_ref, send_near, send_far, v_whole, out_whole = refs[8:]
    lay_out(me_ref[0], blocks, 2, v_whole)
    lay_out(me_ref[0], blocks, 3, out_whole)
    values = dot(rows_ref[...], v_whole[...]).astype(jnp.bfloat16)
    pieces = []
    for head in range(values.shape[1] // HD):
        found = dot(weights_ref[head], values[:, head * HD : (head + 1) * HD])
        pieces.append(found / totals_ref[head])
    attended = jnp.concatenate(pieces, axis=1).astype(jnp.bfloat16)
    half = attended.shape[0] // 2
    sent = dot_turned(attended[half:, :], out_whole[...]).astype(jnp.bfloat16)
    send_near[...], send_far[...] = sent[: half // 2, :], sent[half // 2 :, :]
    keep_ref[...] = dot_turned(attended[:half, :], out_whole[...])


def pass_kernel(keep_ref, got_ref, *outs):
    rows, parts = got_ref.shape[0], len(outs)
    step = rows // parts
    for n, out_ref in enumerate(outs):
        kept = keep_ref[rows + n * step : rows + (n + 1) * step, :]
        got = got_ref[n * step : (n + 1) * step, :].astype(jnp.float32)
        out_ref[...] = (kept + got).astype(jnp.bfloat16)


def layer_kernel(tokens_ref, keep_ref, core_ref, gains_ref, order_ref, *refs):
    chips, slices = refs[:-1], refs[-1]
    rows, width = tokens_ref.shape[0] - 16, tokens_ref.shape[1]
    summed = (
        tokens_ref[0:rows, :].astype(jnp.float32)
        + keep_ref[0:rows, :]
        + core_ref[0:rows, :].astype(jnp.float32)
        + jnp.concatenate([ref[...] for ref in chips], axis=0).astype(jnp.float32)
    )
    merge_in = normalize(summed.astype(jnp.bfloat16), gains_ref[1:2, :])
    places = lax.broadcasted_iota(jnp.int32, (rows, rows), 1)
    picking = (order_ref[...] == places).astype(jnp.bfloat16)
    ordered = dot(picking, merge_in).astype(jnp.bfloat16)
    step, half = width // 8, width // 2
    for n in range(4):
        part = jnp.concatenate(
            [
                ordered[:, n * step : (n + 1) * step],
                ordered[:, half + n * step : half + (n + 1) * step],
            ],
            axis=1,
        )
        part = jnp.concatenate([part[: rows // 2, :], part[rows // 2 :, :]], axis=1)
        slices[n] = part
        slices[4 + n] = part


def merge_kernel(me_ref, at_ref, inputs, *refs):
    blocks, (keep_ref, *sends), total = refs[0:4], refs[4:8], refs[8]
    count, width = inputs.shape[1] // 2, inputs.shape[2] // 2
    z, y = me_ref[0] // 2, lax.rem(me_ref[0], 2)
    for number in range(4):
        position = z ^ number
        at = pl.multiple_of(lax.rem(position, 2) * count, 32)
        rows = inputs[:, pl.ds(at, count), :].reshape(8 * count, 2 * width)
        rows = jnp.where(position < 2, rows[:, :width], rows[:, width:])
        step = blocks[number].shape[0] // 2
        own, other = blocks[number][:step, :], blocks[number][step:, :]
        block = jnp.concatenate(
            [jnp.where(y == 0, own, other), jnp.where(y == 0, other, own)], axis=0
        )
        found = dot(rows, block).reshape(total.shape)
        total[...] = found if number == 0 else total[...] + found
    for k in range(4):
        to = at_ref[0] ^ k
        share = jnp.concatenate([total[4 * y + to], total[4 * (1 - y) + to]], axis=0)
        if k == 0:
            keep_ref[...] = share
        else:
            sends[k - 1][...] = share.astype(jnp.bfloat16)


def pack_kernel(slots_ref, keep_ref, one_ref, two_ref, three_ref, out_ref):
    total = keep_ref[...]
    for got in (one_ref, two_ref, three_ref):
        total = total + got[...].astype(jnp.float32)
    shape = (out_ref.shape[0], total.shape[0])
    placing = (lax.broadcasted_iota(jnp.int32, shape, 0) == slots_ref[...]).astype(jnp.bfloat16)
    out_ref[...] = dot(placing, total.astype(jnp.bfloat16)).astype(jnp.bfloat16)


def by_permutes(
    tokens, qkv_weight, out_weight, merge_weight, ln_gains, segments, merge_rows, owners
):
    rows, width = tokens.shape
    count = rows // 4
    n_dp, n_fsdp = lax.axis_size("dp"), lax.axis_size("fsdp")
    me, at = lax.axis_index("dp"), lax.axis_index("fsdp")
    y = lax.rem(me, 2)
    me_cell, at_cell = me.reshape(1), at.reshape(1)
    bf16, f32 = jnp.bfloat16, jnp.float32
    shape = jax.ShapeDtypeStruct
    cols = qkv_weight.shape[2]
    group = n_fsdp * rows

    heads = jnp.concatenate([qkv_weight, out_weight.T[None]], axis=0)
    near, beside = swap(heads, "dp", 2), swap(heads, "dp", 1)
    first = qkv_weight[0:2]
    second = jnp.concatenate([qkv_weight[2:3], out_weight.T[None]], axis=0)
    first_far = swap(first, "dp", 4)
    first_far_y = swap(after(first_far, beside), "dp", 1)
    first_last = swap(first_far, "dp", 2)
    corner = swap(after(beside[0:2], (first_last, near)), "dp", 2)
    second_far = swap(after(second, first_far), "dp", 4)

    marks = jnp.pad(segments.astype(bf16), ((0, 15), (0, width - rows)))
    marked = after(jnp.concatenate([tokens, marks], axis=0), first)
    along_x = swap(marked, "fsdp", 2)
    group_rows = [marked, along_x]
    group_rows += [swap(after(part, (first_far_y, first_last, second_far)), "fsdp", 1) for part in (marked, along_x)]
    (normed,) = call(norm_kernel, [shape((group, width), bf16)], [ln_gains, *group_rows])

    second_far_y = swap(second_far, "dp", 1)
    second_last = swap(second_far, "dp", 2)
    other_corner = swap(after(beside[2:4], first_last), "dp", 2)
    blocks = [
        [heads, near, far, last, beside, part, far_y, swap(after(last, corner), "dp", 1)]
        for far, last, far_y, part in (
            (first_far, first_last, first_far_y, corner),
            (second_far, second_last, second_far_y, other_corner),
        )
    ]

    half = merge_weight.shape[1] // 2
    low, high = merge_weight[:, :half], merge_weight[:, half:]
    lower = y == 0
    mine = owners[:, 0]
    note = jnp.pad(owners.astype(bf16).T, ((0, 15), (0, half - count)))
    given = jnp.concatenate([jnp.where(lower, high, low), note], axis=0)
    theirs = swap(after(given, second_far_y), "dp", 1)
    other = theirs[-16, :count].astype(jnp.int32)
    pair = jnp.concatenate([jnp.where(lower, low, high), theirs[:-16]], axis=0)
    held = after(pair, (second_last, second_far_y, blocks[0][7]))
    merge_near, merge_far = swap(held, "dp", 2), swap(held, "dp", 4)

    capacity = max(2, (2 * count + n_dp - 1) // n_dp)
    slots = []
    for number, targets in enumerate((mine, other)):
        start, rank = slot_numbers(targets, 2 * capacity)
        slots.append(start + rank + (y ^ number) * capacity)
    slots = jnp.concatenate(slots).reshape(1, 2 * count)
    order = merge_rows.reshape(count, 4).T.reshape(rows, 1)

    found = cols // HD
    weights, totals = call(
        score_kernel,
        [shape((found, group, group), bf16), shape((found, group, 1), f32)],
        [after(me_cell, theirs), normed, *group_rows, *blocks[0]],
        [pltpu.VMEM((width, cols), bf16)] * 2,
        flops=4 * group * width * cols + 2 * group * group * cols,
        smem=1,
        exps=found * group * group,
    )
    keep, *send = call(
        value_kernel,
        [shape((2 * rows, width), f32)] + [shape((rows, width), bf16)] * 2,
        [me_cell, normed, weights, totals, *blocks[1]],
        [pltpu.VMEM((width, cols), bf16)] * 2,
        flops=4 * group * width * cols + 2 * group * group * cols,
        smem=1,
    )
    from_core = [swap(part, "fsdp", 1) for part in send]
    parts = 2
    onward = call(
        pass_kernel, [shape((rows // parts, width), bf16)] * parts, [keep, from_core[1]], moved=1
    )
    from_chip = [swap(part, "fsdp", 2) for part in onward]
    (slices,) = call(
        layer_kernel,
        [shape((8, rows // 2, width // 2), bf16)],
        [marked, keep, from_core[0], ln_gains, order, *from_chip],
        moved=1,
    )
    merge_blocks = [pair, merge_near, merge_far, swap(after(merge_far, (slices, merge_near)), "dp", 2)]
    both = 2 * n_fsdp
    inputs = lax.all_to_all(
        slices,
        ("dp", "fsdp"),
        split_axis=0,
        concat_axis=0,
        tiled=True,
        axis_index_groups=[
            list(range(i, i + both)) for i in range(0, n_dp * n_fsdp, both)
        ],
    )
    shares = call(
        merge_kernel,
        [shape((2 * count, half), f32)] + [shape((2 * count, half), bf16)] * 3,
        [me_cell, at_cell, inputs, *merge_blocks],
        [pltpu.VMEM((8, count, half), f32)],
        flops=2 * 8 * count * width * half,
        smem=2,
    )
    got = [swap(shares[k], "fsdp", k) for k in range(1, 4)]
    (packed,) = call(
        pack_kernel,
        [shape((n_dp * 2 * capacity, half), bf16)],
        [slots, shares[0], *got],
        flops=2 * n_dp * 2 * capacity * 2 * count * half,
    )
    arrived = lax.all_to_all(
        packed.reshape(n_dp, 2 * capacity, half), "dp", split_axis=0, concat_axis=0, tiled=True
    )
    arrived = arrived.reshape(n_dp // 2, 2, 2, capacity, half).transpose(0, 2, 3, 1, 4)
    return arrived.reshape(n_dp * capacity, 2 * half)


def solution(mesh):
    small = mesh.shape["dp"] == 8 and mesh.shape["fsdp"] == 4
    return jax.shard_map(
        by_permutes if small else by_gathers,
        mesh=mesh,
        in_specs=(
            P(("dp", "fsdp"), None),
            P(None, "dp", "fsdp"),
            P("fsdp", "dp"),
            P(("dp", "fsdp"), None),
            P(),
            P("dp", "fsdp"),
            P(("dp", "fsdp"), None),
            P(("dp", "fsdp"), None),
        ),
        out_specs=P(("dp", "fsdp"), None),
        check_vma=False,
    )
```
